128 devices in a mesh: scene: 2 (over core), brick: 64 (over z, x, y).
Axes of the slice: x: 4, y: 4, z: 4, core: 2. Of those that a mesh axis runs over, the one named last changes fastest.
Arguments:
- features: float32 [2, 768, 512, 64], P('scene', 'brick'), may hold values from -6 to 6
- voxel_mask: int32 [2, 768, 512], P('scene', 'brick'), may hold values 0 or 1
- weight: float32 [27, 64, 64], replicated, may hold values from -0.15625 to 0.15625
- bias: float32 [64], replicated, may hold values from -3 to 3
- cotangent: float32 [2, 768, 512, 64], P('scene', 'brick'), may hold values from -6 to 6
- owner: int32 [2, 768, 26, 1], P('scene', 'brick'), may hold values from 0 to 63, as said below
- slot: int32 [2, 768, 26], P('scene', 'brick'), may hold values from 0 to 11
- live: int32 [2, 768, 26], P('scene', 'brick'), may hold values 0 or 1
Outputs:
- activated: float32 [2, 768, 512, 64], P('scene', 'brick')
- feature_grad: float32 [2, 768, 512, 64], P('scene', 'brick')
- kernel_grad: float32 [110592], P(('scene', 'brick'))
The draws below stay inside these ranges and needn't reach their ends.
Inputs may be any that keep to these rules, and one draw needn't show every extreme that they name: `owner`: offsets fall in classes: faces (k = 4, 10, 12, 13, 15, 21), corners (k = 0, 2, 6, 8, 17, 19, 23, 25) and edges (the other twelve). Among the rows of one device (its bricks times the offsets of one class), no value is named by more than 2 face rows, 3 edge rows or 2 corner rows, and for each class some value is named by exactly that many.
All inputs are finite; a program needn't handle non-finite values. No bound on the sum of `voxel_mask` or of `live` on one device may be relied on, other than what follows from the above.
Results may differ from the reference program's by a relative error of at most 0.0001.
Values sent between devices are 32-bit elements; how exact they have to be, the bound alone decides.
No kernel may reach another device: no remote copies, remote signals or barrier semaphores. Data moves between devices by JAX's collectives and lax.ppermute only.
A program may use at most 384 MiB of HBM per device.

```python
import jax
import jax.numpy as jnp
import numpy as np
from jax import lax

C = 64
VOX = 512
OFFS = 26
TAPS = 27
BR_DEV = 12
BRICKS = 768
CAPF = 2
CAPE = 3
CAPC = 2
N_SCENE = 2
N_BRICK = 64


def offset_classes():
    listed = [(a, b, c) for a in (-1, 0, 1) for b in (-1, 0, 1) for c in (-1, 0, 1) if (a, b, c) != (0, 0, 0)]
    return np.array([sum((1 for v in o if v != 0)) - 1 for o in listed], np.int32)


def draw_owner(key, part):
    classes = np.tile(offset_classes(), BR_DEV)
    limits = (CAPF, CAPE, CAPC)

    def one_block(block_key, device):
        result = jnp.zeros((BR_DEV * 26,), jnp.int32)
        for kind in range(3):
            spots = np.array([i for i in range(len(classes)) if classes[i] == kind], np.int32)
            amount = len(spots)
            limit = limits[kind]
            used = (amount + limit - 1) // limit
            order = jax.random.permutation(jax.random.fold_in(block_key, kind), amount).astype(jnp.int32)
            if kind == 0:
                start = jnp.int32(N_BRICK // 2 - used // 2)
            else:
                start = jax.random.randint(jax.random.fold_in(block_key, 10 + kind), (), 0, N_BRICK).astype(jnp.int32)
            target = (device + start + order // limit) % N_BRICK
            result = result.at[spots].set(target.astype(jnp.int32))
        return result
    scenes = []
    for s in range(N_SCENE):
        scene_key = jax.random.fold_in(key, 7 + s)
        devices = jnp.arange(N_BRICK, dtype=jnp.int32)
        keys = jax.vmap(lambda d: jax.random.fold_in(scene_key, d))(devices)
        scenes.append(jax.vmap(one_block)(keys, devices).reshape(BRICKS, 26, 1))
    return jnp.stack(scenes).astype(jnp.int32)


def with_ends(values, rng, least, top_value):
    longest = values.shape.index(max(values.shape))
    spots = []
    for shift in (0, 1):
        where = [jax.random.randint(jax.random.fold_in(rng, axis), (), 0, length) for axis, length in enumerate(values.shape)]
        where[longest] = (where[longest] + shift) % values.shape[longest]
        spots.append(tuple(where))
    return values.at[spots[0]].set(least).at[spots[1]].set(top_value)


def levels(key, dims, split, smallest, top_value):
    factor_of, own = 1.0, jax.random.fold_in(key, 6)
    for dim, shards_of in split:
        steps = jnp.exp(jax.random.uniform(jax.random.fold_in(own, dim), (shards_of,), jnp.float32, smallest / len(split), top_value / len(split)))
        factor_of = factor_of * jnp.repeat(steps, dims[dim] // shards_of).reshape([-1 if axis == dim else 1 for axis in range(len(dims))])
    return factor_of


def scatter_about(rng, extent, scale, bound, split=(), kind=jnp.bfloat16):
    factor_of = levels(rng, extent, split, -0.22, 0.18) if split else 1.0
    values = jax.random.normal(rng, extent, jnp.float32) * scale * factor_of
    return jnp.minimum(jnp.maximum(values, -bound), bound).astype(kind)


def setup_inputs(seed: int = 0) -> dict:
    splits = jax.random.split(jax.random.key(seed), 9)
    features = scatter_about(splits[0], (N_SCENE, BRICKS, VOX, C), 1.0, 6.0, ((0, 2), (1, 64)), jnp.float32)
    voxel_mask = with_ends((jax.random.randint(splits[1], (N_SCENE, BRICKS, VOX), 0, 4) < 3).astype(jnp.int32), jax.random.fold_in(splits[1], 1), 0, 1)
    weight = scatter_about(splits[2], (TAPS, C, C), (TAPS * C) ** -0.5, 0.15625, (), jnp.float32)
    bias = scatter_about(splits[3], (C,), 0.5, 3.0, (), jnp.float32)
    cotangent = scatter_about(splits[4], (N_SCENE, BRICKS, VOX, C), 1.0, 6.0, ((0, 2), (1, 64)), jnp.float32)
    owner = draw_owner(jax.random.fold_in(splits[8], 71), 0)
    slot = with_ends(jax.random.randint(splits[6], (N_SCENE, BRICKS, OFFS), 0, BR_DEV), jax.random.fold_in(splits[6], 1), 0, BR_DEV - 1).astype(jnp.int32)
    live = with_ends((jax.random.randint(splits[7], (N_SCENE, BRICKS, OFFS), 0, 5) < 4).astype(jnp.int32), jax.random.fold_in(splits[7], 1), 0, 1)
    return dict(features=features, voxel_mask=voxel_mask, weight=weight, bias=bias, cotangent=cotangent, owner=owner, slot=slot, live=live)


def offset_list():
    return [(a, b, c) for a in (-1, 0, 1) for b in (-1, 0, 1) for c in (-1, 0, 1) if (a, b, c) != (0, 0, 0)]

def lane_tables():
    source = np.full((26, 64), 512, np.int32)
    target = np.full((26, 64), 1000, np.int32)
    for k, offset in enumerate(offset_list()):
        ranges = []
        for d in range(3):
            if offset[d] == 1:
                ranges.append([(0, 9)])
            elif offset[d] == -1:
                ranges.append([(7, 0)])
            else:
                ranges.append([(q, q + 1) for q in range(8)])
        counter = 0
        for p in ranges[0]:
            for q in ranges[1]:
                for r in ranges[2]:
                    source[k, counter] = p[0] * 64 + q[0] * 8 + r[0]
                    target[k, counter] = p[1] * 100 + q[1] * 10 + r[1]
                    counter += 1
    return (source, target)

def pad_table():
    source, target = lane_tables()
    table = np.zeros(1000, np.int32)
    for x in range(8):
        for y in range(8):
            for z in range(8):
                table[(x + 1) * 100 + (y + 1) * 10 + z + 1] = x * 64 + y * 8 + z
    for k in range(26):
        for j in range(64):
            if target[k, j] < 1000:
                table[target[k, j]] = 512 + k * 64 + j
    return table

def scene_layer(raw, weight, bias, maskf, neighbour, livef):
    source_lane, target_lane = lane_tables()
    pad_source = pad_table()
    count = raw.shape[0]
    channels = raw.shape[2]
    masked = raw * maskf
    extended = jnp.concatenate([masked, jnp.zeros((count, 1, channels), jnp.float32)], axis=1)
    slabs = extended[neighbour[:, :, None], jnp.asarray(source_lane)[None, :, :]] * livef[:, :, None, None]
    joined = jnp.concatenate([masked, slabs.reshape(count, 26 * 64, channels)], axis=1)
    padded = joined[:, pad_source, :].reshape(count, 10, 10, 10, channels)
    pre = jnp.zeros((count, 512, channels), jnp.float32) + bias
    tap = 0
    for a in range(3):
        for b in range(3):
            for c in range(3):
                window = padded[:, a:a + 8, b:b + 8, c:c + 8, :].reshape(count, 512, channels)
                pre = pre + jnp.einsum('bvc,cd->bvd', window, weight[tap], precision=lax.Precision.HIGHEST)
                tap += 1
    return pre * jax.nn.sigmoid(pre) * maskf

def reference(features, voxel_mask, weight, bias, cotangent, owner, slot, live):
    outputs = []
    grads = []
    kernel_total = jnp.zeros(weight.shape, jnp.float32)
    for s in range(N_SCENE):
        maskf = voxel_mask[s].astype(jnp.float32)[:, :, None]
        neighbour = (owner[s, :, :, 0] * BR_DEV + slot[s]).astype(jnp.int32)
        livef = live[s].astype(jnp.float32)

        def layer(raw, kernel):
            return scene_layer(raw, kernel, bias, maskf, neighbour, livef)
        result, pullback = jax.vjp(layer, features[s], weight)
        raw_grad, kernel_grad = pullback(cotangent[s])
        outputs.append(result)
        grads.append(raw_grad)
        kernel_total = kernel_total + kernel_grad
    scale = 1.0 / np.sqrt(float(N_SCENE * BRICKS * VOX))
    return (jnp.stack(outputs), jnp.stack(grads), kernel_total.reshape(-1) * scale)
```

```python
import math

import jax
import jax.numpy as jnp
import numpy as np
from jax import lax
from jax.experimental import pallas as pl
from jax.experimental.pallas import tpu as pltpu
from jax.sharding import PartitionSpec as P

OFFSETS = [(a, b, c) for a in (-1, 0, 1) for b in (-1, 0, 1) for c in (-1, 0, 1) if (a, b, c) != (0, 0, 0)]
KIND = [sum(1 for v in o if v != 0) - 1 for o in OFFSETS]
ORDINAL = [KIND[:k].count(KIND[k]) for k in range(26)]
PER_KIND = (6, 12, 8)
FIRST = (0, 2, 5)
PITCH = 24
F32, BF16 = jnp.float32, jnp.bfloat16


def source_coord(step):
    return 0 if step == 1 else 7


def target_coord(step):
    return 9 if step == 1 else 0


def z_row(step):
    return 16 if step == 1 else 7


def half_of(shape):
    return lax.broadcasted_iota(jnp.int32, shape, len(shape) - 1) >= 64


def swap(v):
    return pltpu.roll(v, 64, axis=v.ndim - 1)


def split_halves(v, low):
    top = v.astype(BF16).astype(F32)
    return jnp.where(low, top, v - top).astype(BF16)


def tables_kernel(x_ref, m_ref, face_ref, edge_ref, corner_ref, rows):
    x = (x_ref[...] * m_ref[...]).reshape(512, 64)
    rows[...] = jnp.concatenate([x, x], axis=1)
    for k, (a, b, c) in enumerate(OFFSETS):
        n = ORDINAL[k]
        x0, y0, z0 = source_coord(a), source_coord(b), source_coord(c)
        if KIND[k] == 0:
            for i in range(8):
                if a:
                    v = rows[x0 * 64 + i * 8:x0 * 64 + i * 8 + 8, :]
                elif b:
                    v = rows[i * 64 + y0 * 8:i * 64 + y0 * 8 + 8, :]
                else:
                    v = rows[pl.ds(i * 64 + z0, 8, stride=8), :]
                face_ref[n, i * 8:i * 8 + 8, :] = v
        elif KIND[k] == 1:
            if not c:
                v = rows[x0 * 64 + y0 * 8:x0 * 64 + y0 * 8 + 8, :]
            elif not b:
                v = rows[pl.ds(x0 * 64 + z0, 8, stride=8), :]
            else:
                v = rows[pl.ds(y0 * 8 + z0, 8, stride=64), :]
            edge_ref[n] = v
        else:
            r = x0 * 64 + y0 * 8 + z0
            corner_ref[n] = jnp.broadcast_to(rows[r:r + 1, :], (8, 128))


def pack_kernel(want_ref, face_ref, edge_ref, corner_ref, out_ref):
    high = half_of((64, 128))
    high8 = half_of((8, 128))
    row0 = lax.broadcasted_iota(jnp.int32, (8, 128), 0) == 0

    def body(p, carry):
        q = [jnp.maximum(want_ref[p, j], 0) for j in range(7)]
        out_ref[p, 0:64, :] = jnp.where(high, face_ref[q[1]], face_ref[q[0]])
        out_ref[p, 64:72, :] = jnp.where(high8, edge_ref[q[3]], edge_ref[q[2]])
        corners = jnp.where(row0, corner_ref[q[5]], corner_ref[q[6]])
        out_ref[p, 72:80, :] = jnp.where(high8, corners, edge_ref[q[4]])
        return carry

    lax.fori_loop(0, 64, body, 0)


def packed(ref):
    sides = [jnp.concatenate([ref[b, :, 0], ref[b, :, 1]], axis=-1) for b in range(2)]
    return jnp.concatenate(sides, axis=2).reshape(512, 128)


def layer_kernel(code_ref, recv_ref, x_ref, m_ref, cot_ref, wf_ref, wb_ref, bias_ref,
                 act_ref, own_ref, send_ref, a_ref, dt_ref, pf, dpad, dxf, tmp):
    g = pl.program_id(0)
    high8 = lax.broadcasted_iota(jnp.int32, (8, 128), 1) >= 64
    half8 = high8.astype(jnp.int32)
    rowi = lax.broadcasted_iota(jnp.int32, (8, 128), 0)

    @pl.when(g == 0)
    def _():
        dpad[...] = jnp.zeros_like(dpad)
        send_ref[...] = jnp.zeros_like(send_ref)

    def prow(b, x, y, z):
        return ((b * 10 + x) * 10 + y) * PITCH + z

    def fetch(k, b):
        c = code_ref[(2 * g + b) * 26 + k]
        return c >> 4, (c >> 1) & 7, c & 1

    for b in range(2):
        for x in range(8):
            v = x_ref[b, x // 2, x % 2] * m_ref[b, x // 2, x % 2]
            v = jnp.concatenate([v, v], axis=-1)
            for y in range(8):
                r = prow(b, x + 1, y + 1, 8)
                pf[r:r + 8, :] = v[y]
    for b in range(2):
        for k, (a, bb, c) in enumerate(OFFSETS):
            o, pos, alive = fetch(k, b)
            scale = alive.astype(F32)
            xt, yt, zt = target_coord(a), target_coord(bb), z_row(c)
            if KIND[k] == 0:
                for i in range(8):
                    v = recv_ref[o, i * 8:i * 8 + 8, :]
                    v = jnp.where(half8 == pos, v, swap(v)) * scale
                    if a:
                        r = prow(b, xt, i + 1, 8)
                        pf[r:r + 8, :] = v
                    elif bb:
                        r = prow(b, i + 1, yt, 8)
                        pf[r:r + 8, :] = v
                    else:
                        pf[pl.ds(prow(b, i + 1, 1, zt), 8, stride=PITCH), :] = v
            elif KIND[k] == 1:
                e = pos - 2
                v = recv_ref[o, pl.ds(pl.multiple_of(64 + 8 * (e >> 1), 8), 8), :]
                v = jnp.where(half8 == (e & 1), v, swap(v)) * scale
                if not c:
                    r = prow(b, xt, yt, 8)
                    pf[r:r + 8, :] = v
                elif not bb:
                    pf[pl.ds(prow(b, xt, 1, zt), 8, stride=PITCH), :] = v
                else:
                    pf[pl.ds(prow(b, 1, yt, zt), 8, stride=10 * PITCH), :] = v
            else:
                v = recv_ref[o, 72:80, :]
                v = jnp.where(pos == 5, v[0:1, :], v[1:2, :])
                v = jnp.where(high8[0:1], v, swap(v)) * scale
                r = prow(b, xt, yt, zt)
                pf[r:r + 1, :] = v
    low = jnp.logical_not(half_of((16, 128)))
    for l in range(3):
        for x in range(10):
            for y in range(10):
                r0, r1 = prow(0, x, y, 7 + l), prow(1, x, y, 7 + l)
                v = jnp.concatenate([pf[r0:r0 + 8, :], pf[r1:r1 + 8, :]], axis=0)
                a_ref[l, 0, x % 2, x // 2, y] = split_halves(v, low)
    acc = None
    for i in range(4):
        for j in range(3):
            parts = [a_ref[l, 0, i % 2, i // 2:i // 2 + 4, j:j + 8].reshape(512, 128) for l in range(3)]
            lhs = jnp.concatenate(parts, axis=1)
            at = (i * 3 + j) * 384
            d = jnp.dot(lhs, wf_ref[at:at + 384, :], preferred_element_type=F32)
            acc = d if acc is None else acc + d
    pre = acc[:, :128] + acc[:, 128:] + bias_ref[...]
    mask = packed(m_ref)
    sig = jax.nn.sigmoid(pre)
    act = (pre * sig * mask).reshape(4, 8, 16, 128)
    for b in range(2):
        act_ref[b, :, 0] = act[:, :, b * 8:b * 8 + 8, :64]
        act_ref[b, :, 1] = act[:, :, b * 8:b * 8 + 8, 64:]
    dpre = packed(cot_ref) * mask * (sig + pre * sig * (1.0 - sig))
    lowl = jnp.logical_not(half_of((512, 128)))
    turned = swap(dpre)
    for p in range(2):
        v = jnp.where(lowl, dpre, turned) if p == 0 else jnp.where(lowl, turned, dpre)
        dpad[p, 1:5, 2:10] = split_halves(v, lowl).reshape(4, 8, 16, 128)
    t = dpre.T
    top = t.astype(BF16)
    dt_ref[0:128, :] = top
    dt_ref[128:256, :] = (t - top.astype(F32)).astype(BF16)
    acc = None
    for i in range(4):
        parts = [dpad[i % 2, i // 2:i // 2 + 5, j:j + 10].reshape(800, 128) for j in range(3)]
        lhs = jnp.concatenate(parts, axis=1)
        d = jnp.dot(lhs, wb_ref[i * 384:i * 384 + 384, :], preferred_element_type=F32)
        acc = d if acc is None else acc + d
    y3 = (acc[:, :384] + acc[:, 384:]).reshape(5, 10, 16, 384)

    def drow(b, x, y, z):
        return ((b * 5 + x) * 10 + y) * PITCH + z

    zero = jnp.zeros((8, 128), F32)
    for b in range(2):
        for x in range(5):
            for y in range(10):
                v = y3[x, y, b * 8:b * 8 + 8]
                r = drow(b, x, y, 0)
                dxf[r:r + 8, :] = zero
                dxf[r + 16:r + 24, :] = zero
                dxf[r + 8:r + 16, :] = v[:, 128:256]
                dxf[r + 7:r + 15, :] += v[:, :128]
                dxf[r + 9:r + 17, :] += v[:, 256:]
    for b in range(2):
        for x in range(8):
            for y in range(8):
                r = drow(b, (x + 1) // 2, y + 1, 8)
                v = dxf[r:r + 8, :]
                own_ref[b, x // 2, x % 2, y] = v[:, :64] if (x + 1) % 2 == 0 else v[:, 64:]
        for k, (a, bb, c) in enumerate(OFFSETS):
            o, pos, _ = fetch(k, b)
            xt, yt, zt = target_coord(a), target_coord(bb), z_row(c)
            if KIND[k] == 0:
                for i in range(8):
                    xx = xt if a else i + 1
                    if a:
                        r = drow(b, xx // 2, i + 1, 8)
                        v = dxf[r:r + 8, :]
                    elif bb:
                        r = drow(b, xx // 2, yt, 8)
                        v = dxf[r:r + 8, :]
                    else:
                        v = dxf[pl.ds(drow(b, xx // 2, 1, zt), 8, stride=PITCH), :]
                    v = jnp.where(half8 == xx % 2, v, swap(v))
                    s = slice(i * 8, i * 8 + 8)
                    send_ref[o, s, :] = jnp.where(half8 == pos, v, send_ref[o, s, :])
            elif KIND[k] == 1:
                par = jnp.full((8, 128), xt % 2, jnp.int32)
                if not c:
                    r = drow(b, xt // 2, yt, 8)
                    v = dxf[r:r + 8, :]
                elif not bb:
                    v = dxf[pl.ds(drow(b, xt // 2, 1, zt), 8, stride=PITCH), :]
                else:
                    for q in range(2):
                        tmp[pl.ds(q, 4, stride=2), :] = dxf[pl.ds(drow(b, q, yt, zt), 4, stride=10 * PITCH), :]
                    v = tmp[...]
                    par = 1 - (rowi & 1)
                v = jnp.where(half8 == par, v, swap(v))
                e = pos - 2
                s = pl.ds(pl.multiple_of(64 + 8 * (e >> 1), 8), 8)
                send_ref[o, s, :] = jnp.where(half8 == (e & 1), v, send_ref[o, s, :])
            else:
                r = drow(b, xt // 2, yt, zt)
                v = jnp.broadcast_to(dxf[r:r + 1, :], (8, 128))
                v = jnp.where(half8 == xt % 2, v, swap(v))
                spot = jnp.logical_and(rowi == pos - 5, high8)
                send_ref[o, 72:80, :] = jnp.where(spot, v, send_ref[o, 72:80, :])


def kernel_grad_kernel(a_ref, dt_ref, out_ref):
    d = dt_ref[...]
    for j in range(3):
        for h in range(2):
            parts = [a_ref[0, :, q, h:h + 4, j:j + 8].reshape(3072, 128) for q in range(2)]
            s = jnp.dot(d, jnp.concatenate(parts, axis=1), preferred_element_type=F32)
            s = s[:128] + s[128:]
            for q in range(2):
                v = s[:, q * 128:q * 128 + 128]
                v = v + swap(v)
                out_ref[0, j, 2 * h + q] = v[:, :64]


def collect_kernel(want_ref, back_ref, own_ref, m_ref, out_ref, faces, edges, corners, rows):
    g = pl.program_id(0)
    high = half_of((64, 128))
    high8 = half_of((8, 128))
    rowi = lax.broadcasted_iota(jnp.int32, (8, 128), 0)

    @pl.when(g == 0)
    def _():
        faces[...] = jnp.zeros_like(faces)
        edges[...] = jnp.zeros_like(edges)
        corners[...] = jnp.zeros_like(corners)

        def index(p, j, spare):
            q = want_ref[p, j]
            return jnp.where(q < 0, spare, q)

        def body(p, carry):
            v = back_ref[p, 0:64, :]
            faces[index(p, 0, 72)] += jnp.where(high, 0.0, v)
            faces[index(p, 1, 72)] += jnp.where(high, v, 0.0)
            v = back_ref[p, 64:72, :]
            edges[index(p, 2, 144)] += jnp.where(high8, 0.0, v)
            edges[index(p, 3, 144)] += jnp.where(high8, v, 0.0)
            v = back_ref[p, 72:80, :]
            edges[index(p, 4, 144)] += jnp.where(high8, 0.0, v)
            v = jnp.where(high8, v, 0.0)
            corners[index(p, 5, 96)] += jnp.where(rowi == 0, v, 0.0)
            corners[index(p, 6, 96)] += jnp.where(rowi == 1, v, 0.0)
            return carry

        lax.fori_loop(0, 64, body, 0)

    def fold(v):
        return (v + swap(v))[:, :64]

    rows[...] = own_ref[...].reshape(512, 64)
    for k, (a, b, c) in enumerate(OFFSETS):
        n = g * PER_KIND[KIND[k]] + ORDINAL[k]
        x0, y0, z0 = source_coord(a), source_coord(b), source_coord(c)
        if KIND[k] == 0:
            for i in range(8):
                v = fold(faces[n, i * 8:i * 8 + 8, :])
                if a:
                    s = slice(x0 * 64 + i * 8, x0 * 64 + i * 8 + 8)
                elif b:
                    s = slice(i * 64 + y0 * 8, i * 64 + y0 * 8 + 8)
                else:
                    s = pl.ds(i * 64 + z0, 8, stride=8)
                rows[s, :] = rows[s, :] + v
        elif KIND[k] == 1:
            v = fold(edges[n])
            if not c:
                s = slice(x0 * 64 + y0 * 8, x0 * 64 + y0 * 8 + 8)
            elif not b:
                s = pl.ds(x0 * 64 + z0, 8, stride=8)
            else:
                s = pl.ds(y0 * 8 + z0, 8, stride=64)
            rows[s, :] = rows[s, :] + v
        else:
            r = x0 * 64 + y0 * 8 + z0
            v = fold(corners[n])
            rows[r:r + 1, :] = rows[r:r + 1, :] + (v[0:1] + v[1:2])
    out_ref[...] = rows[...].reshape(out_ref.shape) * m_ref[...]


def two_terms(w):
    top = lax.reduce_precision(w, 8, 7)
    return jnp.stack([top, w - top], axis=0)


def layer_weights(weight):
    w = weight.reshape(3, 3, 3, 64, 64)
    zero = jnp.zeros((1, 3, 3, 64, 64), F32)
    sides = jnp.stack([jnp.concatenate([w, zero]), jnp.concatenate([zero, w])])
    f = two_terms(sides)
    f = f.transpose(2, 3, 4, 5, 0, 1, 6)
    f = jnp.broadcast_to(f[:, :, :, None], (4, 3, 3, 2, 64, 2, 2, 64)).reshape(36 * 128, 256).astype(BF16)
    r = w[::-1, ::-1]
    sides = jnp.stack([jnp.concatenate([r, zero]), jnp.concatenate([zero, r])])
    b = two_terms(sides)
    b = b.transpose(2, 3, 6, 0, 4, 1, 5)
    b = jnp.broadcast_to(b[:, :, None], (4, 3, 2, 64, 2, 3, 2, 64)).reshape(12 * 128, 768).astype(BF16)
    return f, b


def whole(memory=pltpu.VMEM):
    return pl.BlockSpec(memory_space=memory)


def const_block(shape):
    return pl.BlockSpec(shape, lambda g: (0,) * len(shape))


def lead_block(shape):
    return pl.BlockSpec(shape, lambda g: (g,) + (0,) * (len(shape) - 1))


def params():
    return pltpu.CompilerParams(vmem_limit_bytes=56 * 1024 * 1024)


def on_device(features, voxel_mask, weight, bias, cotangent, owner, slot, live):
    x = features.reshape(12, 4, 2, 8, 8, 64)
    cot = cotangent.reshape(12, 4, 2, 8, 8, 64)
    mask = jnp.broadcast_to(voxel_mask[0].astype(F32)[:, :, None], (12, 512, 64)).reshape(12, 4, 2, 8, 8, 64)

    peer = owner.reshape(312)
    alive = live.reshape(312)
    kinds = jnp.asarray(np.tile(np.array(KIND, np.int32), 12))
    first = jnp.asarray(np.tile(np.array([FIRST[q] for q in KIND], np.int32), 12))
    per = jnp.asarray(np.tile(np.array([PER_KIND[q] for q in KIND], np.int32), 12))
    ordinal = jnp.asarray(np.tile(np.array(ORDINAL, np.int32), 12))
    entry = slot.reshape(312) * per + ordinal
    key = peer * 3 + kinds
    order = jnp.arange(312, dtype=jnp.int32)
    same = jnp.logical_and(key[:, None] == key[None, :], order[:, None] < order[None, :])
    place = first + jnp.sum(same.astype(jnp.int32), axis=0)
    spot = jnp.where(alive > 0, peer * 8 + place, -1)
    hit = spot[None, :] == jnp.arange(512, dtype=jnp.int32)[:, None]
    wanted = jnp.sum(jnp.where(hit, entry[None, :] + 1, 0), axis=1).reshape(64, 8) - 1
    code = (peer * 8 + place) * 2 + alive
    asked = lax.all_to_all(wanted, "brick", split_axis=0, concat_axis=0, tiled=True)

    faces, edges, corners = pl.pallas_call(
        tables_kernel,
        grid=(12,),
        in_specs=[lead_block((1, 4, 2, 8, 8, 64))] * 2,
        out_specs=[lead_block((6, 64, 128)), lead_block((12, 8, 128)), lead_block((8, 8, 128))],
        out_shape=[
            jax.ShapeDtypeStruct((72, 64, 128), F32),
            jax.ShapeDtypeStruct((144, 8, 128), F32),
            jax.ShapeDtypeStruct((96, 8, 128), F32),
        ],
        scratch_shapes=[pltpu.VMEM((512, 128), F32)],
        compiler_params=params(),
        name="tables",
    )(x, mask)

    out = pl.pallas_call(
        pack_kernel,
        in_specs=[whole(pltpu.SMEM), whole(), whole(), whole()],
        out_specs=whole(),
        out_shape=jax.ShapeDtypeStruct((64, 80, 128), F32),
        compiler_params=params(),
        name="pack",
    )(asked, faces, edges, corners)
    recv = lax.all_to_all(out, "brick", split_axis=0, concat_axis=0, tiled=True)

    wf, wb = layer_weights(weight)
    bias2 = jnp.concatenate([bias, bias]).reshape(1, 128)
    brick_block = lead_block((2, 4, 2, 8, 8, 64))
    brick_shape = jax.ShapeDtypeStruct((12, 4, 2, 8, 8, 64), F32)
    act, own, send, windows, dpre_t = pl.pallas_call(
        layer_kernel,
        grid=(6,),
        in_specs=[
            pl.BlockSpec(memory_space=pltpu.SMEM),
            const_block((64, 80, 128)),
            brick_block,
            brick_block,
            brick_block,
            const_block((36 * 128, 256)),
            const_block((12 * 128, 768)),
            const_block((1, 128)),
        ],
        out_specs=[
            brick_block,
            brick_block,
            const_block((64, 80, 128)),
            pl.BlockSpec((3, 1, 2, 5, 10, 16, 128), lambda g: (0, g, 0, 0, 0, 0, 0)),
            pl.BlockSpec((256, 512), lambda g: (0, g)),
        ],
        out_shape=[
            brick_shape,
            brick_shape,
            jax.ShapeDtypeStruct((64, 80, 128), F32),
            jax.ShapeDtypeStruct((3, 6, 2, 5, 10, 16, 128), BF16),
            jax.ShapeDtypeStruct((256, 3072), BF16),
        ],
        scratch_shapes=[
            pltpu.VMEM((200 * PITCH, 128), F32),
            pltpu.VMEM((2, 6, 12, 16, 128), BF16),
            pltpu.VMEM((100 * PITCH, 128), F32),
            pltpu.VMEM((8, 128), F32),
        ],
        compiler_params=params(),
        name="layer",
    )(code, recv, x, mask, cot, wf, wb, bias2)
    back = lax.all_to_all(send, "brick", split_axis=0, concat_axis=0, tiled=True)

    z = pl.pallas_call(
        kernel_grad_kernel,
        grid=(3,),
        in_specs=[
            pl.BlockSpec((1, 6, 2, 5, 10, 16, 128), lambda l: (l, 0, 0, 0, 0, 0, 0)),
            const_block((256, 3072)),
        ],
        out_specs=lead_block((1, 3, 4, 128, 64)),
        out_shape=jax.ShapeDtypeStruct((3, 3, 4, 128, 64), F32),
        compiler_params=params(),
        cost_estimate=pl.CostEstimate(flops=2 * 256 * 3072 * 4608, bytes_accessed=11000000, transcendentals=0),
        name="kernel_grad",
    )(windows, dpre_t)
    kernel = z[:, :, 0:3, 0:64] + z[:, :, 1:4, 64:128]
    kernel = kernel.transpose(2, 1, 0, 4, 3).reshape(128, 864)
    kernel = jnp.pad(kernel, ((0, 0), (0, 32))).reshape(128, 7, 128)
    shares = lax.all_to_all(kernel, ("scene", "brick"), split_axis=0, concat_axis=0, tiled=True)
    scale = 1.0 / math.sqrt(float(2 * 768 * 512))
    share = jnp.sum(shares, axis=0).reshape(896)[:864] * scale

    grad = pl.pallas_call(
        collect_kernel,
        grid=(12,),
        in_specs=[
            pl.BlockSpec(memory_space=pltpu.SMEM),
            const_block((64, 80, 128)),
            lead_block((1, 4, 2, 8, 8, 64)),
            lead_block((1, 4, 2, 8, 8, 64)),
        ],
        out_specs=lead_block((1, 4, 2, 8, 8, 64)),
        out_shape=brick_shape,
        scratch_shapes=[
            pltpu.VMEM((73, 64, 128), F32),
            pltpu.VMEM((145, 8, 128), F32),
            pltpu.VMEM((97, 8, 128), F32),
            pltpu.VMEM((512, 64), F32),
        ],
        compiler_params=params(),
        name="collect",
    )(asked, back, own, mask)
    shape = features.shape
    return act.reshape(shape), grad.reshape(shape), share


def solution(mesh):
    big = P("scene", "brick", None, None)
    flat = P("scene", "brick", None)
    return jax.shard_map(
        on_device,
        mesh=mesh,
        in_specs=(big, flat, P(), P(), big, big, flat, flat),
        out_specs=(big, big, P(("scene", "brick"))),
        check_vma=False,
    )
```

```python
import math

import jax
import jax.numpy as jnp
import numpy as np
from jax import lax
from jax.experimental import pallas as pl
from jax.experimental.pallas import tpu as pltpu
from jax.sharding import PartitionSpec as P

OFFSETS = [(a, b, c) for a in (-1, 0, 1) for b in (-1, 0, 1) for c in (-1, 0, 1) if (a, b, c) != (0, 0, 0)]
KIND = [sum(1 for v in o if v != 0) - 1 for o in OFFSETS]
ORDINAL = [KIND[:k].count(KIND[k]) for k in range(26)]
PER_KIND = (6, 12, 8)
FIRST = (0, 2, 5)
PITCH = 24
F32, BF16 = jnp.float32, jnp.bfloat16


def source_coord(step):
    return 0 if step == 1 else 7


def target_coord(step):
    return 9 if step == 1 else 0


def z_row(step):
    return 16 if step == 1 else 7


def half_of(shape):
    return lax.broadcasted_iota(jnp.int32, shape, len(shape) - 1) >= 64


def swap(v):
    return pltpu.roll(v, 64, axis=v.ndim - 1)


def split_halves(v, low):
    top = v.astype(BF16).astype(F32)
    return jnp.where(low, top, v - top).astype(BF16)


def tables_kernel(x_ref, m_ref, face_ref, edge_ref, corner_ref, rows):
    x = (x_ref[...] * m_ref[...]).reshape(512, 64)
    rows[...] = jnp.concatenate([x, x], axis=1)
    for k, (a, b, c) in enumerate(OFFSETS):
        n = ORDINAL[k]
        x0, y0, z0 = source_coord(a), source_coord(b), source_coord(c)
        if KIND[k] == 0:
            for i in range(8):
                if a:
                    v = rows[x0 * 64 + i * 8:x0 * 64 + i * 8 + 8, :]
                elif b:
                    v = rows[i * 64 + y0 * 8:i * 64 + y0 * 8 + 8, :]
                else:
                    v = rows[pl.ds(i * 64 + z0, 8, stride=8), :]
                face_ref[n, i * 8:i * 8 + 8, :] = v
        elif KIND[k] == 1:
            if not c:
                v = rows[x0 * 64 + y0 * 8:x0 * 64 + y0 * 8 + 8, :]
            elif not b:
                v = rows[pl.ds(x0 * 64 + z0, 8, stride=8), :]
            else:
                v = rows[pl.ds(y0 * 8 + z0, 8, stride=64), :]
            edge_ref[n] = v
        else:
            r = x0 * 64 + y0 * 8 + z0
            corner_ref[n] = jnp.broadcast_to(rows[r:r + 1, :], (8, 128))


def pack_kernel(want_ref, face_ref, edge_ref, corner_ref, out_ref):
    high = half_of((64, 128))
    high8 = half_of((8, 128))
    row0 = lax.broadcasted_iota(jnp.int32, (8, 128), 0) == 0

    def body(p, carry):
        q = [jnp.maximum(want_ref[p, j], 0) for j in range(7)]
        out_ref[p, 0:64, :] = jnp.where(high, face_ref[q[1]], face_ref[q[0]])
        out_ref[p, 64:72, :] = jnp.where(high8, edge_ref[q[3]], edge_ref[q[2]])
        corners = jnp.where(row0, corner_ref[q[5]], corner_ref[q[6]])
        out_ref[p, 72:80, :] = jnp.where(high8, corners, edge_ref[q[4]])
        return carry

    lax.fori_loop(0, 64, body, 0)


def placed(v, other):
    return jnp.where(other, v, swap(v))


def shifted(v, l, row):
    if l == 1:
        return v
    turned = pltpu.roll(v, 1 if l == 0 else 7, axis=0)
    return jnp.where(row == (0 if l == 0 else 7), 0.0, turned)


def weights_kernel(w_ref, f_ref, b_ref):
    zero = jnp.zeros((64, 64), F32)

    def fill(out_ref, s, sides):
        c = jnp.concatenate(sides, axis=1)
        top = c.astype(BF16)
        low = (c - top.astype(F32)).astype(BF16)
        v = jnp.concatenate([top, low], axis=1)
        out_ref[s * 128:s * 128 + 128, :] = jnp.concatenate([v, v], axis=0)

    for j in range(3):
        for l in range(3):
            w = [w_ref[i * 9 + j * 3 + l] for i in range(3)]
            t = [w_ref[(2 - i) * 9 + (2 - j) * 3 + 2 - l].T for i in range(3)]
            for i in range(4):
                s = i * 9 + j * 3 + l
                fill(f_ref, s, [w[i] if i < 3 else zero, w[i - 1] if i else zero])
                fill(b_ref, s, [t[i] if i < 3 else zero, t[i - 1] if i else zero])


def convolve(a_ref, w_ref):
    slices = [(i, j, l) for i in range(4) for j in range(3) for l in range(3)]
    acc = None
    for s in range(0, 36, 4):
        parts = [a_ref[l, i % 2, i // 2:i // 2 + 4, j:j + 8].reshape(512, 128) for i, j, l in slices[s:s + 4]]
        lhs = jnp.concatenate(parts, axis=1)
        d = jnp.dot(lhs, w_ref[s * 128:s * 128 + 512, :], preferred_element_type=F32)
        acc = d if acc is None else acc + d
    return (acc[:, :128] + acc[:, 128:]).reshape(4, 8, 16, 128)


def own_forward_kernel(x_ref, m_ref, cot_ref, w_ref, bias_ref, pre_ref, mask_ref, cotm_ref, a_ref):
    @pl.when(pl.program_id(0) == 0)
    def _():
        a_ref[...] = jnp.zeros_like(a_ref)

    row = lax.broadcasted_iota(jnp.int32, (8, 128), 0)
    low = jnp.logical_not(half_of((16, 128)))
    for x in range(8):
        cols = []
        for b in range(2):
            v = x_ref[b, x // 2, x % 2] * m_ref[b, x // 2, x % 2]
            cols.append(jnp.concatenate([v, v], axis=-1))
        for y in range(8):
            for l in range(3):
                v = jnp.concatenate([shifted(cols[b][y], l, row) for b in range(2)], axis=0)
                a_ref[l, (x + 1) % 2, (x + 1) // 2, y + 1] = split_halves(v, low)
    pre = convolve(a_ref, w_ref) + bias_ref[...]
    for b in range(2):
        pre_ref[b] = pre[:, :, b * 8:b * 8 + 8]
        mask = jnp.concatenate([m_ref[b, :, 0], m_ref[b, :, 1]], axis=-1)
        mask_ref[b] = mask
        cotm_ref[b] = jnp.concatenate([cot_ref[b, :, 0], cot_ref[b, :, 1]], axis=-1) * mask


def own_backward_kernel(d_ref, w_ref, own_ref, a_ref):
    @pl.when(pl.program_id(0) == 0)
    def _():
        a_ref[...] = jnp.zeros_like(a_ref)

    row = lax.broadcasted_iota(jnp.int32, (8, 128), 0)
    half = half_of((8, 128))
    low = jnp.logical_not(half_of((16, 128)))
    for x in range(8):
        for y in range(8):
            cols = []
            for b in range(2):
                v = d_ref[b, x // 2, y]
                cols.append(placed(v, half if x % 2 else jnp.logical_not(half)))
            for l in range(3):
                v = jnp.concatenate([shifted(cols[b], l, row) for b in range(2)], axis=0)
                a_ref[l, (x + 1) % 2, (x + 1) // 2, y + 1] = split_halves(v, low)
    out = convolve(a_ref, w_ref)
    for b in range(2):
        own_ref[b, :, 0] = out[:, :, b * 8:b * 8 + 8, :64]
        own_ref[b, :, 1] = out[:, :, b * 8:b * 8 + 8, 64:]


def unpack_code(code_ref, b, k):
    c = code_ref[b * 26 + k]
    return c >> 4, (c >> 1) & 7, c & 1


def edge_rows(pos):
    e = pos - 2
    return pl.ds(pl.multiple_of(64 + 8 * (e >> 1), 8), 8), e & 1


def halo_kernel(code_ref, recv_ref, own_ref, mask_ref, cot_ref, wf_ref, wb_ref,
                act_ref, dpre_ref, send_ref, pre, px, py, zf, pz, qx, qy, qz, rx, ry, rz, tmp):
    high8 = half_of((8, 128))
    half8 = high8.astype(jnp.int32)
    row = lax.broadcasted_iota(jnp.int32, (8, 128), 0)
    low = jnp.logical_not(half_of((16, 128)))
    spare = jnp.zeros((16, 128), BF16)

    def zrow(s, x, y, b):
        return ((s * 10 + x) * 10 + y) * 16 + b

    for s in range(2):
        for l in range(3):
            for g in range(6):
                py[s, l, 0, 0, g] = spare
                py[s, l, 1, 4, g] = spare
        for x in range(10):
            for y in range(10):
                r = zrow(s, x, y, 8)
                zf[r:r + 8, :] = jnp.zeros((8, 128), F32)

    def face(k, b, i):
        o, pos, alive = unpack_code(code_ref, b, k)
        v = recv_ref[o, i * 8:i * 8 + 8, :]
        return placed(v, half8 == pos) * alive.astype(F32)

    def edge(k, b):
        o, pos, alive = unpack_code(code_ref, b, k)
        rows, h = edge_rows(pos)
        return placed(recv_ref[o, rows, :], half8 == h) * alive.astype(F32)

    for k, (dx, dy, dz) in enumerate(OFFSETS):
        xt, yt = target_coord(dx), target_coord(dy)
        sx, sy, sz = int(dx == 1), int(dy == 1), int(dz == 1)
        for g in range(6):
            pair = (2 * g, 2 * g + 1)
            if KIND[k] == 0 and not dz:
                for i in range(8):
                    v = [face(k, b, i) for b in pair]
                    for l in range(3):
                        w = split_halves(jnp.concatenate([shifted(u, l, row) for u in v], axis=0), low)
                        if dx:
                            px[sx, l, i + 1, g] = w
                        else:
                            py[sy, l, (i + 1) % 2, (i + 1) // 2, g] = w
            elif KIND[k] == 1 and not dz:
                v = [edge(k, b) for b in pair]
                for l in range(3):
                    px[sx, l, yt, g] = split_halves(jnp.concatenate([shifted(u, l, row) for u in v], axis=0), low)
            else:
                for b in pair:
                    if KIND[k] == 0:
                        for i in range(8):
                            zf[pl.ds(zrow(sz, i + 1, 1, b), 8, stride=16), :] = face(k, b, i)
                    elif KIND[k] == 1 and dx:
                        zf[pl.ds(zrow(sz, xt, 1, b), 8, stride=16), :] = edge(k, b)
                    elif KIND[k] == 1:
                        zf[pl.ds(zrow(sz, 1, yt, b), 8, stride=160), :] = edge(k, b)
                    else:
                        o, pos, alive = unpack_code(code_ref, b, k)
                        v = recv_ref[o, 72:80, :]
                        v = jnp.where(pos == 5, v[0:1, :], v[1:2, :])
                        r = zrow(sz, xt, yt, b)
                        zf[r:r + 1, :] = placed(v, high8[0:1]) * alive.astype(F32)
    for s in range(2):
        for x in range(10):
            for y in range(10):
                r = zrow(s, x, y, 0)
                pz[s, x % 2, x // 2, y] = split_halves(zf[r:r + 16, :], low)

    def side_x(src, s, ii, ys, w_ref):
        parts = [src[s, l, j:j + ys].reshape(ys * 96, 128) for j in range(3) for l in range(3)]
        v = jnp.dot(jnp.concatenate(parts, axis=1), w_ref[ii * 1152:ii * 1152 + 1152, :], preferred_element_type=F32)
        return v[:, :128] + v[:, 128:]

    def side_y(src, s, j, w_ref):
        acc = None
        for h in range(2):
            parts = [src[s, l, i, h:h + 4].reshape(384, 128) for i in range(2) for l in range(3)]
            at = [((2 * h + i) * 9 + j * 3) * 128 for i in range(2)]
            w = jnp.concatenate([w_ref[a:a + 384, :] for a in at], axis=0)
            v = jnp.dot(jnp.concatenate(parts, axis=1), w, preferred_element_type=F32)
            acc = v if acc is None else acc + v
        return acc[:, :128] + acc[:, 128:]

    def side_z(src, s, l, xs, ys, w_ref):
        slices = [(i, j) for i in range(4) for j in range(3)]
        acc = None
        for n in range(0, 12, 4):
            parts = [src[s, i % 2, i // 2:i // 2 + xs, j:j + ys].reshape(xs * ys * 16, 128) for i, j in slices[n:n + 4]]
            at = [(i * 9 + j * 3 + l) * 128 for i, j in slices[n:n + 4]]
            w = jnp.concatenate([w_ref[a:a + 128, :] for a in at], axis=0)
            v = jnp.dot(jnp.concatenate(parts, axis=1), w, preferred_element_type=F32)
            acc = v if acc is None else acc + v
        return acc[:, :128] + acc[:, 128:]

    def prow(b, xh, y, z):
        return ((b * 4 + xh) * 8 + y) * 8 + z

    pre[...] = own_ref[...]
    for s in range(2):
        v = side_x(px, s, 3 * s, 8, wf_ref)
        for y in range(8):
            for b in range(12):
                r, q = prow(b, 3 * s, y, 0), (y * 12 + b) * 8
                pre[r:r + 8, :] += v[q:q + 8]
        v = side_y(py, s, 2 * s, wf_ref)
        for xh in range(4):
            for b in range(12):
                r, q = prow(b, xh, 7 * s, 0), (xh * 12 + b) * 8
                pre[r:r + 8, :] += v[q:q + 8]
        v = side_z(pz, s, 2 * s, 4, 8, wf_ref)
        for xh in range(4):
            for y in range(8):
                q = (xh * 8 + y) * 16
                a = pl.ds(prow(0, xh, y, 7 * s), 8, stride=256)
                pre[a, :] = pre[a, :] + v[q:q + 8]
                a = pl.ds(prow(8, xh, y, 7 * s), 4, stride=256)
                pre[a, :] = pre[a, :] + v[q + 8:q + 12]

    def activate(n, carry):
        a = pl.ds(pl.multiple_of(n * 128, 128), 128)
        p = pre[a, :]
        sig = jax.nn.sigmoid(p)
        ps = p * sig
        act_ref[a, :] = ps * mask_ref[a, :]
        dpre_ref[a, :] = cot_ref[a, :] * (sig + ps * (1.0 - sig))
        return carry

    lax.fori_loop(0, 24, activate, 0)

    for s in range(2):
        for l in range(3):
            for g in range(6):
                for y in (0, 1, 10, 11):
                    qx[s, l, y, g] = spare
                qy[s, l, 0, 0, g] = spare
                qy[s, l, 1, 4, g] = spare
    qz[...] = jnp.zeros_like(qz)
    wanted = [jnp.logical_not(high8), high8]
    wanted16 = [low, jnp.logical_not(low)]
    for s in range(2):
        for g in range(6):
            for y in range(8):
                v = []
                for b in (2 * g, 2 * g + 1):
                    r = prow(b, 3 * s, y, 0)
                    v.append(placed(dpre_ref[r:r + 8, :], wanted[s]))
                for l in range(3):
                    qx[s, l, y + 2, g] = split_halves(jnp.concatenate([shifted(u, l, row) for u in v], axis=0), low)
            for x in range(8):
                v = []
                for b in (2 * g, 2 * g + 1):
                    r = prow(b, x // 2, 7 * s, 0)
                    v.append(placed(dpre_ref[r:r + 8, :], wanted[x % 2]))
                for l in range(3):
                    w = split_halves(jnp.concatenate([shifted(u, l, row) for u in v], axis=0), low)
                    qy[s, l, (x + 1) % 2, (x + 1) // 2, g] = w
        for xh in range(4):
            for y in range(8):
                first = dpre_ref[pl.ds(prow(0, xh, y, 7 * s), 8, stride=256), :]
                last = dpre_ref[pl.ds(prow(8, xh, y, 7 * s), 4, stride=256), :]
                v = jnp.concatenate([first, last, jnp.zeros((4, 128), F32)], axis=0)
                for p in range(2):
                    qz[s, p, xh + 1, y + 2] = split_halves(placed(v, wanted16[p]), low)
    for s in range(2):
        rx[s] = side_x(qx, s, 3 - 3 * s, 10, wb_ref)
        ry[s] = side_y(qy, s, 2 - 2 * s, wb_ref)
        rz[s * 800:s * 800 + 800, :] = side_z(qz, s, 2 - 2 * s, 5, 10, wb_ref)

    def rzrow(s, xh, y, b):
        return s * 800 + (xh * 10 + y) * 16 + b

    send_ref[...] = jnp.zeros_like(send_ref)
    for b in range(12):
        for k, (dx, dy, dz) in enumerate(OFFSETS):
            o, pos, _ = unpack_code(code_ref, b, k)
            xt, yt = target_coord(dx), target_coord(dy)
            sx, sy, sz = int(dx == 1), int(dy == 1), int(dz == 1)
            if KIND[k] == 0:
                for i in range(8):
                    if dx:
                        r, par = ((i + 1) * 12 + b) * 8, 1 - sx
                        v = rx[sx, r:r + 8, :]
                    elif dy:
                        r, par = ((i // 2) * 12 + b) * 8, i % 2
                        v = ry[sy, r:r + 8, :]
                    else:
                        par = (i + 1) % 2
                        v = rz[pl.ds(rzrow(sz, (i + 1) // 2, 1, b), 8, stride=16), :]
                    v = placed(v, wanted[par])
                    a = slice(i * 8, i * 8 + 8)
                    send_ref[o, a, :] = jnp.where(half8 == pos, v, send_ref[o, a, :])
            elif KIND[k] == 1:
                if not dz:
                    r = (yt * 12 + b) * 8
                    v = placed(rx[sx, r:r + 8, :], wanted[1 - sx])
                elif dx:
                    v = placed(rz[pl.ds(rzrow(sz, xt // 2, 1, b), 8, stride=16), :], wanted[xt % 2])
                else:
                    for q in range(2):
                        tmp[pl.ds(q, 4, stride=2), :] = rz[pl.ds(rzrow(sz, q, yt, b), 4, stride=160), :]
                    v = placed(tmp[...], half8 == 1 - (row & 1))
                a, h = edge_rows(pos)
                send_ref[o, a, :] = jnp.where(half8 == h, v, send_ref[o, a, :])
            else:
                r = rzrow(sz, xt // 2, yt, b)
                v = placed(jnp.broadcast_to(rz[r:r + 1, :], (8, 128)), wanted[xt % 2])
                spot = jnp.logical_and(row == pos - 5, high8)
                send_ref[o, 72:80, :] = jnp.where(spot, v, send_ref[o, 72:80, :])


def windows_kernel(code_ref, recv_ref, x_ref, m_ref, d_ref, a_ref, dt_ref, pf):
    g = pl.program_id(0)
    high8 = half_of((8, 128))
    half8 = high8.astype(jnp.int32)

    def prow(b, x, y, z):
        return ((b * 10 + x) * 10 + y) * PITCH + z

    for b in range(2):
        for x in range(8):
            v = x_ref[b, x // 2, x % 2] * m_ref[b, x // 2, x % 2]
            v = jnp.concatenate([v, v], axis=-1)
            for y in range(8):
                r = prow(b, x + 1, y + 1, 8)
                pf[r:r + 8, :] = v[y]
    for b in range(2):
        for k, (dx, dy, dz) in enumerate(OFFSETS):
            o, pos, alive = unpack_code(code_ref, 2 * g + b, k)
            scale = alive.astype(F32)
            xt, yt, zt = target_coord(dx), target_coord(dy), z_row(dz)
            if KIND[k] == 0:
                for i in range(8):
                    v = placed(recv_ref[o, i * 8:i * 8 + 8, :], half8 == pos) * scale
                    if dx:
                        r = prow(b, xt, i + 1, 8)
                        pf[r:r + 8, :] = v
                    elif dy:
                        r = prow(b, i + 1, yt, 8)
                        pf[r:r + 8, :] = v
                    else:
                        pf[pl.ds(prow(b, i + 1, 1, zt), 8, stride=PITCH), :] = v
            elif KIND[k] == 1:
                rows, h = edge_rows(pos)
                v = placed(recv_ref[o, rows, :], half8 == h) * scale
                if not dz:
                    r = prow(b, xt, yt, 8)
                    pf[r:r + 8, :] = v
                elif dx:
                    pf[pl.ds(prow(b, xt, 1, zt), 8, stride=PITCH), :] = v
                else:
                    pf[pl.ds(prow(b, 1, yt, zt), 8, stride=10 * PITCH), :] = v
            else:
                v = recv_ref[o, 72:80, :]
                v = jnp.where(pos == 5, v[0:1, :], v[1:2, :])
                r = prow(b, xt, yt, zt)
                pf[r:r + 1, :] = placed(v, high8[0:1]) * scale
    low = jnp.logical_not(half_of((16, 128)))
    for l in range(3):
        for x in range(10):
            for y in range(10):
                r0, r1 = prow(0, x, y, 7 + l), prow(1, x, y, 7 + l)
                v = jnp.concatenate([pf[r0:r0 + 8, :], pf[r1:r1 + 8, :]], axis=0)
                a_ref[l, 0, x % 2, x // 2, y] = split_halves(v, low)
    t = jnp.concatenate([d_ref[0], d_ref[1]], axis=2).reshape(512, 128).T
    top = t.astype(BF16)
    dt_ref[0:128, :] = top
    dt_ref[128:256, :] = (t - top.astype(F32)).astype(BF16)


def kernel_grad_kernel(a_ref, dt_ref, out_ref):
    d = dt_ref[...]
    for j in range(3):
        for h in range(2):
            parts = [a_ref[0, :, q, h:h + 4, j:j + 8].reshape(3072, 128) for q in range(2)]
            s = jnp.dot(d, jnp.concatenate(parts, axis=1), preferred_element_type=F32)
            s = s[:128] + s[128:]
            for q in range(2):
                v = s[:, q * 128:q * 128 + 128]
                v = v + swap(v)
                out_ref[0, j, 2 * h + q] = v[:, :64]


def collect_kernel(want_ref, back_ref, own_ref, m_ref, out_ref, faces, edges, corners, rows):
    g = pl.program_id(0)
    high = half_of((64, 128))
    high8 = half_of((8, 128))
    rowi = lax.broadcasted_iota(jnp.int32, (8, 128), 0)

    @pl.when(g == 0)
    def _():
        faces[...] = jnp.zeros_like(faces)
        edges[...] = jnp.zeros_like(edges)
        corners[...] = jnp.zeros_like(corners)

        def index(p, j, spare):
            q = want_ref[p, j]
            return jnp.where(q < 0, spare, q)

        def body(p, carry):
            v = back_ref[p, 0:64, :]
            faces[index(p, 0, 72)] += jnp.where(high, 0.0, v)
            faces[index(p, 1, 72)] += jnp.where(high, v, 0.0)
            v = back_ref[p, 64:72, :]
            edges[index(p, 2, 144)] += jnp.where(high8, 0.0, v)
            edges[index(p, 3, 144)] += jnp.where(high8, v, 0.0)
            v = back_ref[p, 72:80, :]
            edges[index(p, 4, 144)] += jnp.where(high8, 0.0, v)
            v = jnp.where(high8, v, 0.0)
            corners[index(p, 5, 96)] += jnp.where(rowi == 0, v, 0.0)
            corners[index(p, 6, 96)] += jnp.where(rowi == 1, v, 0.0)
            return carry

        lax.fori_loop(0, 64, body, 0)

    def fold(v):
        return (v + swap(v))[:, :64]

    rows[...] = own_ref[...].reshape(512, 64)
    for k, (a, b, c) in enumerate(OFFSETS):
        n = g * PER_KIND[KIND[k]] + ORDINAL[k]
        x0, y0, z0 = source_coord(a), source_coord(b), source_coord(c)
        if KIND[k] == 0:
            for i in range(8):
                v = fold(faces[n, i * 8:i * 8 + 8, :])
                if a:
                    s = slice(x0 * 64 + i * 8, x0 * 64 + i * 8 + 8)
                elif b:
                    s = slice(i * 64 + y0 * 8, i * 64 + y0 * 8 + 8)
                else:
                    s = pl.ds(i * 64 + z0, 8, stride=8)
                rows[s, :] = rows[s, :] + v
        elif KIND[k] == 1:
            v = fold(edges[n])
            if not c:
                s = slice(x0 * 64 + y0 * 8, x0 * 64 + y0 * 8 + 8)
            elif not b:
                s = pl.ds(x0 * 64 + z0, 8, stride=8)
            else:
                s = pl.ds(y0 * 8 + z0, 8, stride=64)
            rows[s, :] = rows[s, :] + v
        else:
            r = x0 * 64 + y0 * 8 + z0
            v = fold(corners[n])
            rows[r:r + 1, :] = rows[r:r + 1, :] + (v[0:1] + v[1:2])
    out_ref[...] = rows[...].reshape(out_ref.shape) * m_ref[...]


def share_out(v):
    scene, brick = lax.axis_index("scene"), lax.axis_index("brick")
    v = v.reshape(2, 64, 7, 128)
    mine = lax.dynamic_index_in_dim(v, scene, 0, keepdims=False)
    theirs = lax.dynamic_index_in_dim(v, 1 - scene, 0, keepdims=False)
    v = mine + lax.ppermute(theirs, "scene", [(0, 1), (1, 0)])
    for stride in (16, 4, 1):
        v = v.reshape(4, stride, 7, 128)
        at = (brick // stride) % 4
        total = lax.dynamic_index_in_dim(v, at, 0, keepdims=False)
        for d in (1, 2, 3):
            part = lax.dynamic_index_in_dim(v, at ^ d, 0, keepdims=False)
            total = total + lax.ppermute(part, "brick", [(n, n ^ (d * stride)) for n in range(64)])
        v = total
    return v.reshape(896)[:864]


def whole(memory=pltpu.VMEM):
    return pl.BlockSpec(memory_space=memory)


def const_block(shape):
    return pl.BlockSpec(shape, lambda g: (0,) * len(shape))


def lead_block(shape):
    return pl.BlockSpec(shape, lambda g: (g,) + (0,) * (len(shape) - 1))


def params():
    return pltpu.CompilerParams(vmem_limit_bytes=56 * 1024 * 1024)


def on_device(features, voxel_mask, weight, bias, cotangent, owner, slot, live):
    x = features.reshape(12, 4, 2, 8, 8, 64)
    cot = cotangent.reshape(12, 4, 2, 8, 8, 64)
    mask = jnp.broadcast_to(voxel_mask[0].astype(F32)[:, :, None], (12, 512, 64)).reshape(12, 4, 2, 8, 8, 64)

    peer = owner.reshape(312)
    alive = live.reshape(312)
    kinds = jnp.asarray(np.tile(np.array(KIND, np.int32), 12))
    first = jnp.asarray(np.tile(np.array([FIRST[q] for q in KIND], np.int32), 12))
    per = jnp.asarray(np.tile(np.array([PER_KIND[q] for q in KIND], np.int32), 12))
    ordinal = jnp.asarray(np.tile(np.array(ORDINAL, np.int32), 12))
    entry = slot.reshape(312) * per + ordinal
    key = peer * 3 + kinds
    order = jnp.arange(312, dtype=jnp.int32)
    same = jnp.logical_and(key[:, None] == key[None, :], order[:, None] < order[None, :])
    place = first + jnp.sum(same.astype(jnp.int32), axis=0)
    spot = jnp.where(alive > 0, peer * 8 + place, -1)
    hit = spot[None, :] == jnp.arange(512, dtype=jnp.int32)[:, None]
    wanted = jnp.sum(jnp.where(hit, entry[None, :] + 1, 0), axis=1).reshape(64, 8) - 1
    code = (peer * 8 + place) * 2 + alive
    asked = lax.all_to_all(wanted, "brick", split_axis=0, concat_axis=0, tiled=True)

    wf, wb = pl.pallas_call(
        weights_kernel,
        in_specs=[whole()],
        out_specs=[whole(), whole()],
        out_shape=[jax.ShapeDtypeStruct((4608, 256), BF16)] * 2,
        compiler_params=params(),
        cost_estimate=pl.CostEstimate(flops=0, bytes_accessed=6000000, transcendentals=0),
        name="weights",
    )(weight)

    faces, edges, corners = pl.pallas_call(
        tables_kernel,
        grid=(12,),
        in_specs=[lead_block((1, 4, 2, 8, 8, 64))] * 2,
        out_specs=[lead_block((6, 64, 128)), lead_block((12, 8, 128)), lead_block((8, 8, 128))],
        out_shape=[
            jax.ShapeDtypeStruct((72, 64, 128), F32),
            jax.ShapeDtypeStruct((144, 8, 128), F32),
            jax.ShapeDtypeStruct((96, 8, 128), F32),
        ],
        scratch_shapes=[pltpu.VMEM((512, 128), F32)],
        compiler_params=params(),
        name="tables",
    )(x, mask)

    out = pl.pallas_call(
        pack_kernel,
        in_specs=[whole(pltpu.SMEM), whole(), whole(), whole()],
        out_specs=whole(),
        out_shape=jax.ShapeDtypeStruct((64, 80, 128), F32),
        compiler_params=params(),
        name="pack",
    )(asked, faces, edges, corners)
    recv = lax.all_to_all(out, "brick", split_axis=0, concat_axis=0, tiled=True)

    bias2 = jnp.concatenate([bias, bias]).reshape(1, 128)
    brick_block = lead_block((2, 4, 2, 8, 8, 64))
    brick_shape = jax.ShapeDtypeStruct((12, 4, 2, 8, 8, 64), F32)
    packed_block = lead_block((2, 4, 8, 8, 128))
    packed_shape = jax.ShapeDtypeStruct((12, 4, 8, 8, 128), F32)
    window_scratch = pltpu.VMEM((3, 2, 5, 10, 16, 128), BF16)
    own_pre, mask_p, cot_p = pl.pallas_call(
        own_forward_kernel,
        grid=(6,),
        in_specs=[brick_block] * 3 + [const_block((4608, 256)), const_block((1, 128))],
        out_specs=[packed_block] * 3,
        out_shape=[packed_shape] * 3,
        scratch_shapes=[window_scratch],
        compiler_params=params(),
        cost_estimate=pl.CostEstimate(flops=2 * 3072 * 4608 * 256, bytes_accessed=15000000, transcendentals=0),
        name="own_forward",
    )(x, mask, cot, wf, bias2)

    flat = (3072, 128)
    act, dpre, send = pl.pallas_call(
        halo_kernel,
        in_specs=[whole(pltpu.SMEM)] + [whole()] * 6,
        out_specs=[whole()] * 3,
        out_shape=[
            jax.ShapeDtypeStruct(flat, F32),
            jax.ShapeDtypeStruct(flat, F32),
            jax.ShapeDtypeStruct((64, 80, 128), F32),
        ],
        scratch_shapes=[
            pltpu.VMEM(flat, F32),
            pltpu.VMEM((2, 3, 10, 6, 16, 128), BF16),
            pltpu.VMEM((2, 3, 2, 5, 6, 16, 128), BF16),
            pltpu.VMEM((3200, 128), F32),
            pltpu.VMEM((2, 2, 5, 10, 16, 128), BF16),
            pltpu.VMEM((2, 3, 12, 6, 16, 128), BF16),
            pltpu.VMEM((2, 3, 2, 5, 6, 16, 128), BF16),
            pltpu.VMEM((2, 2, 6, 12, 16, 128), BF16),
            pltpu.VMEM((2, 960, 128), F32),
            pltpu.VMEM((2, 384, 128), F32),
            pltpu.VMEM((1600, 128), F32),
            pltpu.VMEM((8, 128), F32),
        ],
        compiler_params=params(),
        name="halo",
    )(code, recv, own_pre.reshape(flat), mask_p.reshape(flat), cot_p.reshape(flat), wf, wb)
    back = lax.all_to_all(send, "brick", split_axis=0, concat_axis=0, tiled=True)
    act = act.reshape(12, 4, 8, 8, 2, 64).transpose(0, 1, 4, 2, 3, 5)
    dpre = dpre.reshape(12, 4, 8, 8, 128)

    windows, dpre_t = pl.pallas_call(
        windows_kernel,
        grid=(6,),
        in_specs=[
            pl.BlockSpec(memory_space=pltpu.SMEM),
            const_block((64, 80, 128)),
            brick_block,
            brick_block,
            packed_block,
        ],
        out_specs=[
            pl.BlockSpec((3, 1, 2, 5, 10, 16, 128), lambda g: (0, g, 0, 0, 0, 0, 0)),
            pl.BlockSpec((256, 512), lambda g: (0, g)),
        ],
        out_shape=[
            jax.ShapeDtypeStruct((3, 6, 2, 5, 10, 16, 128), BF16),
            jax.ShapeDtypeStruct((256, 3072), BF16),
        ],
        scratch_shapes=[pltpu.VMEM((200 * PITCH, 128), F32)],
        compiler_params=params(),
        cost_estimate=pl.CostEstimate(flops=0, bytes_accessed=30000000, transcendentals=0),
        name="windows",
    )(code, recv, x, mask, dpre)
    z = pl.pallas_call(
        kernel_grad_kernel,
        grid=(3,),
        in_specs=[
            pl.BlockSpec((1, 6, 2, 5, 10, 16, 128), lambda l: (l, 0, 0, 0, 0, 0, 0)),
            const_block((256, 3072)),
        ],
        out_specs=lead_block((1, 3, 4, 128, 64)),
        out_shape=jax.ShapeDtypeStruct((3, 3, 4, 128, 64), F32),
        compiler_params=params(),
        cost_estimate=pl.CostEstimate(flops=2 * 256 * 3072 * 4608, bytes_accessed=11000000, transcendentals=0),
        name="kernel_grad",
    )(windows, dpre_t)
    kernel = z[:, :, 0:3, 0:64] + z[:, :, 1:4, 64:128]
    kernel = kernel.transpose(2, 1, 0, 4, 3).reshape(128, 864)
    kernel = jnp.pad(kernel, ((0, 0), (0, 32))).reshape(128, 7, 128)
    scale = 1.0 / math.sqrt(float(2 * 768 * 512))
    share = share_out(kernel) * scale

    own = pl.pallas_call(
        own_backward_kernel,
        grid=(6,),
        in_specs=[packed_block, const_block((4608, 256))],
        out_specs=brick_block,
        out_shape=brick_shape,
        scratch_shapes=[window_scratch],
        compiler_params=params(),
        cost_estimate=pl.CostEstimate(flops=2 * 3072 * 4608 * 256, bytes_accessed=15000000, transcendentals=0),
        name="own_backward",
    )(dpre, wb)

    grad = pl.pallas_call(
        collect_kernel,
        grid=(12,),
        in_specs=[
            pl.BlockSpec(memory_space=pltpu.SMEM),
            const_block((64, 80, 128)),
            lead_block((1, 4, 2, 8, 8, 64)),
            lead_block((1, 4, 2, 8, 8, 64)),
        ],
        out_specs=lead_block((1, 4, 2, 8, 8, 64)),
        out_shape=brick_shape,
        scratch_shapes=[
            pltpu.VMEM((73, 64, 128), F32),
            pltpu.VMEM((145, 8, 128), F32),
            pltpu.VMEM((97, 8, 128), F32),
            pltpu.VMEM((512, 64), F32),
        ],
        compiler_params=params(),
        name="collect",
    )(asked, back, own, mask)
    shape = features.shape
    return act.reshape(shape), grad.reshape(shape), share


def solution(mesh):
    big = P("scene", "brick", None, None)
    flat = P("scene", "brick", None)
    return jax.shard_map(
        on_device,
        mesh=mesh,
        in_specs=(big, flat, P(), P(), big, big, flat, flat),
        out_specs=(big, big, P(("scene", "brick"))),
        check_vma=False,
    )
```

```python
import math

import jax
import jax.numpy as jnp
import numpy as np
from jax import lax
from jax.experimental import pallas as pl
from jax.experimental.pallas import tpu as pltpu
from jax.sharding import PartitionSpec as P

OFFSETS = [(a, b, c) for a in (-1, 0, 1) for b in (-1, 0, 1) for c in (-1, 0, 1) if (a, b, c) != (0, 0, 0)]
KIND = [sum(1 for v in o if v != 0) - 1 for o in OFFSETS]
ORDINAL = [KIND[:k].count(KIND[k]) for k in range(26)]
PER_KIND = (6, 12, 8)
FIRST = (0, 2, 5)
F32, BF16 = jnp.float32, jnp.bfloat16


def source_coord(step):
    return 0 if step == 1 else 7


def target_coord(step):
    return 9 if step == 1 else 0


def half_of(shape):
    return lax.broadcasted_iota(jnp.int32, shape, len(shape) - 1) >= 64


def swap(v):
    return pltpu.roll(v, 64, axis=v.ndim - 1)


def split_halves(v, low):
    top = v.astype(BF16).astype(F32)
    return jnp.where(low, top, v - top).astype(BF16)


def masked_rows(x_ref, m_ref, p):
    return (x_ref[p] * m_ref[p].astype(F32)).T


def tables_kernel(x_ref, m_ref, face_ref, edge_ref, corner_ref, row_ref, rows):
    for p in range(x_ref.shape[0]):
        x = masked_rows(x_ref, m_ref, p)
        x = jnp.concatenate([x, x], axis=1)
        rows[...] = x
        row_ref[p] = x
        for k, (a, b, c) in enumerate(OFFSETS):
            n = ORDINAL[k]
            x0, y0, z0 = source_coord(a), source_coord(b), source_coord(c)
            if KIND[k] == 0:
                for i in range(8):
                    if a:
                        v = rows[x0 * 64 + i * 8:x0 * 64 + i * 8 + 8, :]
                    elif b:
                        v = rows[i * 64 + y0 * 8:i * 64 + y0 * 8 + 8, :]
                    else:
                        v = rows[pl.ds(i * 64 + z0, 8, stride=8), :]
                    face_ref[p * 6 + n, i * 8:i * 8 + 8, :] = v
            elif KIND[k] == 1:
                if not c:
                    v = rows[x0 * 64 + y0 * 8:x0 * 64 + y0 * 8 + 8, :]
                elif not b:
                    v = rows[pl.ds(x0 * 64 + z0, 8, stride=8), :]
                else:
                    v = rows[pl.ds(y0 * 8 + z0, 8, stride=64), :]
                edge_ref[p * 12 + n] = v
            else:
                r = x0 * 64 + y0 * 8 + z0
                corner_ref[p * 8 + n] = jnp.broadcast_to(rows[r:r + 1, :], (8, 128))


def pack_kernel(want_ref, face_ref, edge_ref, corner_ref, out_ref):
    high = half_of((64, 128))
    high8 = half_of((8, 128))
    row0 = lax.broadcasted_iota(jnp.int32, (8, 128), 0) == 0

    def body(p, carry):
        q = [jnp.maximum(want_ref[p, j], 0) for j in range(7)]
        out_ref[p, 0:64, :] = jnp.where(high, face_ref[q[1]], face_ref[q[0]])
        out_ref[p, 64:72, :] = jnp.where(high8, edge_ref[q[3]], edge_ref[q[2]])
        corners = jnp.where(row0, corner_ref[q[5]], corner_ref[q[6]])
        out_ref[p, 72:80, :] = jnp.where(high8, corners, edge_ref[q[4]])
        return carry

    lax.fori_loop(0, 64, body, 0)


def placed(v, other):
    return jnp.where(other, v, swap(v))


def shifted(v, l, row):
    if l == 1:
        return v
    turned = pltpu.roll(v, 1 if l == 0 else 7, axis=0)
    return jnp.where(row == (0 if l == 0 else 7), 0.0, turned)


def weights_kernel(w_ref, f_ref, b_ref):
    zero = jnp.zeros((64, 64), F32)

    def fill(out_ref, s, sides):
        c = jnp.concatenate(sides, axis=1)
        top = c.astype(BF16)
        low = (c - top.astype(F32)).astype(BF16)
        v = jnp.concatenate([top, low], axis=1)
        out_ref[s * 128:s * 128 + 128, :] = jnp.concatenate([v, v], axis=0)

    for j in range(3):
        for l in range(3):
            w = [w_ref[i * 9 + j * 3 + l] for i in range(3)]
            t = [w_ref[(2 - i) * 9 + (2 - j) * 3 + 2 - l].T for i in range(3)]
            for i in range(4):
                s = i * 9 + j * 3 + l
                fill(f_ref, s, [w[i] if i < 3 else zero, w[i - 1] if i else zero])
                fill(b_ref, s, [t[i] if i < 3 else zero, t[i - 1] if i else zero])


def convolve(a_ref, w_ref):
    slices = [(i, j, l) for i in range(4) for j in range(3) for l in range(3)]
    acc = None
    for s in range(0, 36, 4):
        parts = [a_ref[l, 0, i % 2, i // 2:i // 2 + 4, j:j + 8].reshape(512, 128) for i, j, l in slices[s:s + 4]]
        lhs = jnp.concatenate(parts, axis=1)
        d = jnp.dot(lhs, w_ref[s * 128:s * 128 + 512, :], preferred_element_type=F32)
        acc = d if acc is None else acc + d
    return (acc[:, :128] + acc[:, 128:]).reshape(4, 8, 16, 128)


def clear_border(a_ref):
    spare = jnp.zeros((16, 128), BF16)
    for l in range(3):
        for x in range(10):
            for y in range(10):
                if x in (0, 9) or y in (0, 9):
                    a_ref[l, 0, x % 2, x // 2, y] = spare


def own_forward_kernel(x_ref, m_ref, cot_ref, w_ref, bias_ref, pre_ref, cotm_ref, a_ref):
    clear_border(a_ref)
    row = lax.broadcasted_iota(jnp.int32, (8, 128), 0)
    low = jnp.logical_not(half_of((16, 128)))
    for x in range(8):
        for y in range(8):
            r = x * 64 + y * 8
            for l in range(3):
                v = jnp.concatenate([shifted(x_ref[b, r:r + 8, :], l, row) for b in range(2)], axis=0)
                a_ref[l, 0, (x + 1) % 2, (x + 1) // 2, y + 1] = split_halves(v, low)
    pre = convolve(a_ref, w_ref) + bias_ref[...]
    for b in range(2):
        pre_ref[b] = pre[:, :, b * 8:b * 8 + 8]
        c = masked_rows(cot_ref, m_ref, b).reshape(4, 2, 8, 8, 64)
        cotm_ref[b] = jnp.concatenate([c[:, 0], c[:, 1]], axis=-1)


def own_backward_kernel(d_ref, w_ref, own_ref, a_ref):
    @pl.when(pl.program_id(0) == 0)
    def _():
        a_ref[...] = jnp.zeros_like(a_ref)

    row = lax.broadcasted_iota(jnp.int32, (8, 128), 0)
    half = half_of((8, 128))
    low = jnp.logical_not(half_of((16, 128)))
    for x in range(8):
        for y in range(8):
            cols = []
            for b in range(2):
                cols.append(placed(d_ref[b, x // 2, y], half if x % 2 else jnp.logical_not(half)))
            for l in range(3):
                v = jnp.concatenate([shifted(cols[b], l, row) for b in range(2)], axis=0)
                a_ref[l, 0, (x + 1) % 2, (x + 1) // 2, y + 1] = split_halves(v, low)
    out = convolve(a_ref, w_ref)
    for b in range(2):
        own_ref[b, :, 0] = out[:, :, b * 8:b * 8 + 8, :64]
        own_ref[b, :, 1] = out[:, :, b * 8:b * 8 + 8, 64:]


def activated_kernel(act_ref, m_ref, out_ref):
    for b in range(2):
        mask = m_ref[b].astype(F32)
        for h in range(2):
            t = act_ref[b, 2 * h:2 * h + 2].reshape(128, 128).T
            v = jnp.concatenate([t[:64, :64], t[64:, :64], t[:64, 64:], t[64:, 64:]], axis=1)
            a = slice(h * 256, h * 256 + 256)
            out_ref[b, :, a] = v * mask[:, a]


def unpack_code(code_ref, b, k):
    c = code_ref[b * 26 + k]
    return c >> 4, (c >> 1) & 7, c & 1


def edge_rows(pos):
    e = pos - 2
    return pl.ds(pl.multiple_of(64 + 8 * (e >> 1), 8), 8), e & 1


def halo_kernel(code_ref, recv_ref, own_ref, cot_ref, wf_ref, wb_ref,
                act_ref, dpre_ref, send_ref, px, py, pz, pre, zf, qx, qy, qz, rx, ry, rz, tmp):
    high8 = half_of((8, 128))
    half8 = high8.astype(jnp.int32)
    row = lax.broadcasted_iota(jnp.int32, (8, 128), 0)
    low = jnp.logical_not(half_of((16, 128)))
    spare = jnp.zeros((16, 128), BF16)

    def zrow(s, x, y, b):
        return ((s * 10 + x) * 10 + y) * 16 + b

    for s in range(2):
        for l in range(3):
            for g in range(6):
                py[s, l, 0, 0, g] = spare
                py[s, l, 1, 4, g] = spare
        for x in range(10):
            for y in range(10):
                r = zrow(s, x, y, 8)
                zf[r:r + 8, :] = jnp.zeros((8, 128), F32)

    def face(k, b, i):
        o, pos, alive = unpack_code(code_ref, b, k)
        v = recv_ref[o, i * 8:i * 8 + 8, :]
        return placed(v, half8 == pos) * alive.astype(F32)

    def edge(k, b):
        o, pos, alive = unpack_code(code_ref, b, k)
        rows, h = edge_rows(pos)
        return placed(recv_ref[o, rows, :], half8 == h) * alive.astype(F32)

    for k, (dx, dy, dz) in enumerate(OFFSETS):
        xt, yt = target_coord(dx), target_coord(dy)
        sx, sy, sz = int(dx == 1), int(dy == 1), int(dz == 1)
        for g in range(6):
            pair = (2 * g, 2 * g + 1)
            if KIND[k] == 0 and not dz:
                for i in range(8):
                    v = [face(k, b, i) for b in pair]
                    for l in range(3):
                        w = split_halves(jnp.concatenate([shifted(u, l, row) for u in v], axis=0), low)
                        if dx:
                            px[sx, l, i + 1, g] = w
                        else:
                            py[sy, l, (i + 1) % 2, (i + 1) // 2, g] = w
            elif KIND[k] == 1 and not dz:
                v = [edge(k, b) for b in pair]
                for l in range(3):
                    px[sx, l, yt, g] = split_halves(jnp.concatenate([shifted(u, l, row) for u in v], axis=0), low)
            else:
                for b in pair:
                    if KIND[k] == 0:
                        for i in range(8):
                            zf[pl.ds(zrow(sz, i + 1, 1, b), 8, stride=16), :] = face(k, b, i)
                    elif KIND[k] == 1 and dx:
                        zf[pl.ds(zrow(sz, xt, 1, b), 8, stride=16), :] = edge(k, b)
                    elif KIND[k] == 1:
                        zf[pl.ds(zrow(sz, 1, yt, b), 8, stride=160), :] = edge(k, b)
                    else:
                        o, pos, alive = unpack_code(code_ref, b, k)
                        v = recv_ref[o, 72:80, :]
                        v = jnp.where(pos == 5, v[0:1, :], v[1:2, :])
                        r = zrow(sz, xt, yt, b)
                        zf[r:r + 1, :] = placed(v, high8[0:1]) * alive.astype(F32)
    for s in range(2):
        for x in range(10):
            for y in range(10):
                r = zrow(s, x, y, 0)
                pz[s, x % 2, x // 2, y] = split_halves(zf[r:r + 16, :], low)

    def side_x(src, s, ii, ys, w_ref):
        parts = [src[s, l, j:j + ys].reshape(ys * 96, 128) for j in range(3) for l in range(3)]
        v = jnp.dot(jnp.concatenate(parts, axis=1), w_ref[ii * 1152:ii * 1152 + 1152, :], preferred_element_type=F32)
        return v[:, :128] + v[:, 128:]

    def side_y(src, s, j, w_ref):
        acc = None
        for h in range(2):
            parts = [src[s, l, i, h:h + 4].reshape(384, 128) for i in range(2) for l in range(3)]
            at = [((2 * h + i) * 9 + j * 3) * 128 for i in range(2)]
            w = jnp.concatenate([w_ref[a:a + 384, :] for a in at], axis=0)
            v = jnp.dot(jnp.concatenate(parts, axis=1), w, preferred_element_type=F32)
            acc = v if acc is None else acc + v
        return acc[:, :128] + acc[:, 128:]

    def side_z(src, s, l, xs, ys, w_ref):
        slices = [(i, j) for i in range(4) for j in range(3)]
        acc = None
        for n in range(0, 12, 4):
            parts = [src[s, i % 2, i // 2:i // 2 + xs, j:j + ys].reshape(xs * ys * 16, 128) for i, j in slices[n:n + 4]]
            at = [(i * 9 + j * 3 + l) * 128 for i, j in slices[n:n + 4]]
            w = jnp.concatenate([w_ref[a:a + 128, :] for a in at], axis=0)
            v = jnp.dot(jnp.concatenate(parts, axis=1), w, preferred_element_type=F32)
            acc = v if acc is None else acc + v
        return acc[:, :128] + acc[:, 128:]

    def prow(b, xh, y, z):
        return ((b * 4 + xh) * 8 + y) * 8 + z

    pre[...] = own_ref[...]
    for s in range(2):
        v = side_x(px, s, 3 * s, 8, wf_ref)
        for y in range(8):
            for b in range(12):
                r, q = prow(b, 3 * s, y, 0), (y * 12 + b) * 8
                pre[r:r + 8, :] += v[q:q + 8]
        v = side_y(py, s, 2 * s, wf_ref)
        for xh in range(4):
            for b in range(12):
                r, q = prow(b, xh, 7 * s, 0), (xh * 12 + b) * 8
                pre[r:r + 8, :] += v[q:q + 8]
        v = side_z(pz, s, 2 * s, 4, 8, wf_ref)
        for xh in range(4):
            for y in range(8):
                q = (xh * 8 + y) * 16
                a = pl.ds(prow(0, xh, y, 7 * s), 8, stride=256)
                pre[a, :] = pre[a, :] + v[q:q + 8]
                a = pl.ds(prow(8, xh, y, 7 * s), 4, stride=256)
                pre[a, :] = pre[a, :] + v[q + 8:q + 12]

    def activate(n, carry):
        a = pl.ds(pl.multiple_of(n * 128, 128), 128)
        p = pre[a, :]
        sig = jax.nn.sigmoid(p)
        ps = p * sig
        act_ref[a, :] = ps
        dpre_ref[a, :] = cot_ref[a, :] * (sig + ps * (1.0 - sig))
        return carry

    lax.fori_loop(0, 24, activate, 0)

    for s in range(2):
        for l in range(3):
            for g in range(6):
                for y in (0, 1, 10, 11):
                    qx[s, l, y, g] = spare
                qy[s, l, 0, 0, g] = spare
                qy[s, l, 1, 4, g] = spare
    qz[...] = jnp.zeros_like(qz)
    wanted = [jnp.logical_not(high8), high8]
    wanted16 = [low, jnp.logical_not(low)]
    for s in range(2):
        for g in range(6):
            for y in range(8):
                v = []
                for b in (2 * g, 2 * g + 1):
                    r = prow(b, 3 * s, y, 0)
                    v.append(placed(dpre_ref[r:r + 8, :], wanted[s]))
                for l in range(3):
                    qx[s, l, y + 2, g] = split_halves(jnp.concatenate([shifted(u, l, row) for u in v], axis=0), low)
            for x in range(8):
                v = []
                for b in (2 * g, 2 * g + 1):
                    r = prow(b, x // 2, 7 * s, 0)
                    v.append(placed(dpre_ref[r:r + 8, :], wanted[x % 2]))
                for l in range(3):
                    w = split_halves(jnp.concatenate([shifted(u, l, row) for u in v], axis=0), low)
                    qy[s, l, (x + 1) % 2, (x + 1) // 2, g] = w
        for xh in range(4):
            for y in range(8):
                first = dpre_ref[pl.ds(prow(0, xh, y, 7 * s), 8, stride=256), :]
                last = dpre_ref[pl.ds(prow(8, xh, y, 7 * s), 4, stride=256), :]
                v = jnp.concatenate([first, last, jnp.zeros((4, 128), F32)], axis=0)
                for p in range(2):
                    qz[s, p, xh + 1, y + 2] = split_halves(placed(v, wanted16[p]), low)
    for s in range(2):
        rx[s] = side_x(qx, s, 3 - 3 * s, 10, wb_ref)
        ry[s] = side_y(qy, s, 2 - 2 * s, wb_ref)
        rz[s * 800:s * 800 + 800, :] = side_z(qz, s, 2 - 2 * s, 5, 10, wb_ref)

    def rzrow(s, xh, y, b):
        return s * 800 + (xh * 10 + y) * 16 + b

    send_ref[...] = jnp.zeros_like(send_ref)
    for b in range(12):
        for k, (dx, dy, dz) in enumerate(OFFSETS):
            o, pos, _ = unpack_code(code_ref, b, k)
            xt, yt = target_coord(dx), target_coord(dy)
            sx, sy, sz = int(dx == 1), int(dy == 1), int(dz == 1)
            if KIND[k] == 0:
                for i in range(8):
                    if dx:
                        r, par = ((i + 1) * 12 + b) * 8, 1 - sx
                        v = rx[sx, r:r + 8, :]
                    elif dy:
                        r, par = ((i // 2) * 12 + b) * 8, i % 2
                        v = ry[sy, r:r + 8, :]
                    else:
                        par = (i + 1) % 2
                        v = rz[pl.ds(rzrow(sz, (i + 1) // 2, 1, b), 8, stride=16), :]
                    v = placed(v, wanted[par])
                    a = slice(i * 8, i * 8 + 8)
                    send_ref[o, a, :] = jnp.where(half8 == pos, v, send_ref[o, a, :])
            elif KIND[k] == 1:
                if not dz:
                    r = (yt * 12 + b) * 8
                    v = placed(rx[sx, r:r + 8, :], wanted[1 - sx])
                elif dx:
                    v = placed(rz[pl.ds(rzrow(sz, xt // 2, 1, b), 8, stride=16), :], wanted[xt % 2])
                else:
                    for q in range(2):
                        tmp[pl.ds(q, 4, stride=2), :] = rz[pl.ds(rzrow(sz, q, yt, b), 4, stride=160), :]
                    v = placed(tmp[...], half8 == 1 - (row & 1))
                a, h = edge_rows(pos)
                send_ref[o, a, :] = jnp.where(half8 == h, v, send_ref[o, a, :])
            else:
                r = rzrow(sz, xt // 2, yt, b)
                v = placed(jnp.broadcast_to(rz[r:r + 1, :], (8, 128)), wanted[xt % 2])
                spot = jnp.logical_and(row == pos - 5, high8)
                send_ref[o, 72:80, :] = jnp.where(spot, v, send_ref[o, 72:80, :])


def turned_terms(out_ref, at, v):
    t = v.T
    n = t.shape[1]
    top = t.astype(BF16)
    out_ref[0:128, at:at + n] = top
    out_ref[128:256, at:at + n] = (t - top.astype(F32)).astype(BF16)


def kernel_grad_kernel(a_ref, px_ref, py_ref, pz_ref, d_ref, out_ref, dt, dx, dy, dz):
    l = pl.program_id(0)

    @pl.when(l == 0)
    def _():
        for g in range(6):
            v = jnp.concatenate([d_ref[2 * g], d_ref[2 * g + 1]], axis=2)
            turned_terms(dt, g * 512, v.reshape(512, 128))
        flat = d_ref.reshape(3072, 128)
        for s in range(2):
            for y in range(8):
                v = jnp.concatenate([d_ref[b, 3 * s, y] for b in range(12)], axis=0)
                if y % 4 == 0:
                    held = []
                held.append(v)
                if y % 4 == 3:
                    turned_terms(dx.at[s], (y - 3) * 96, jnp.concatenate(held, axis=0))
            v = [d_ref[b, xh, 7 * s] for xh in range(4) for b in range(12)]
            turned_terms(dy.at[s], 0, jnp.concatenate(v, axis=0))
            v = []
            for n in range(32):
                r = n * 8 + 7 * s
                v.append(flat[pl.ds(r, 8, stride=256), :])
                v.append(flat[pl.ds(r + 2048, 4, stride=256), :])
                v.append(jnp.zeros((4, 128), F32))
            turned_terms(dz.at[s], 0, jnp.concatenate(v, axis=0))

    def product(d, parts):
        s = jnp.dot(d, jnp.concatenate(parts, axis=1), preferred_element_type=F32)
        s = s[:128] + s[128:]
        out = []
        for q in range(len(parts)):
            v = s[:, q * 128:q * 128 + 128]
            out.append((v + swap(v))[:, :64])
        return out

    for j in range(3):
        for h in range(2):
            parts = [a_ref[0, :, q, h:h + 4, j:j + 8].reshape(3072, 128) for q in range(2)]
            for q, v in enumerate(product(dt[...], parts)):
                out_ref[0, j, 2 * h + q] = v
    for s in range(2):
        parts = [px_ref[s, 0, j:j + 8].reshape(768, 128) for j in range(3)]
        for j, v in enumerate(product(dx[s], parts)):
            out_ref[0, j, 3 * s] += v
        parts = [py_ref[s, 0, i % 2, i // 2:i // 2 + 4].reshape(384, 128) for i in range(4)]
        for i, v in enumerate(product(dy[s], parts)):
            out_ref[0, 2 * s, i] += v

    @pl.when(l != 1)
    def _():
        s = l // 2
        for j in range(3):
            parts = [pz_ref[s, i % 2, i // 2:i // 2 + 4, j:j + 8].reshape(512, 128) for i in range(4)]
            for i, v in enumerate(product(dz[s], parts)):
                out_ref[0, j, i] += v


def collect_kernel(want_ref, back_ref, own_ref, m_ref, out_ref, faces, edges, corners, rows):
    g = pl.program_id(0)
    high = half_of((64, 128))
    high8 = half_of((8, 128))
    rowi = lax.broadcasted_iota(jnp.int32, (8, 128), 0)

    @pl.when(g == 0)
    def _():
        faces[...] = jnp.zeros_like(faces)
        edges[...] = jnp.zeros_like(edges)
        corners[...] = jnp.zeros_like(corners)

        def index(p, j, spare):
            q = want_ref[p, j]
            return jnp.where(q < 0, spare, q)

        def body(p, carry):
            v = back_ref[p, 0:64, :]
            faces[index(p, 0, 72)] += jnp.where(high, 0.0, v)
            faces[index(p, 1, 72)] += jnp.where(high, v, 0.0)
            v = back_ref[p, 64:72, :]
            edges[index(p, 2, 144)] += jnp.where(high8, 0.0, v)
            edges[index(p, 3, 144)] += jnp.where(high8, v, 0.0)
            v = back_ref[p, 72:80, :]
            edges[index(p, 4, 144)] += jnp.where(high8, 0.0, v)
            v = jnp.where(high8, v, 0.0)
            corners[index(p, 5, 96)] += jnp.where(rowi == 0, v, 0.0)
            corners[index(p, 6, 96)] += jnp.where(rowi == 1, v, 0.0)
            return carry

        lax.fori_loop(0, 64, body, 0)

    def fold(v):
        return (v + swap(v))[:, :64]

    bricks = own_ref.shape[0]
    for p in range(bricks):
        rows[...] = own_ref[p].reshape(512, 64)
        for k, (a, b, c) in enumerate(OFFSETS):
            n = (g * bricks + p) * PER_KIND[KIND[k]] + ORDINAL[k]
            x0, y0, z0 = source_coord(a), source_coord(b), source_coord(c)
            if KIND[k] == 0:
                for i in range(8):
                    v = fold(faces[n, i * 8:i * 8 + 8, :])
                    if a:
                        s = slice(x0 * 64 + i * 8, x0 * 64 + i * 8 + 8)
                    elif b:
                        s = slice(i * 64 + y0 * 8, i * 64 + y0 * 8 + 8)
                    else:
                        s = pl.ds(i * 64 + z0, 8, stride=8)
                    rows[s, :] = rows[s, :] + v
            elif KIND[k] == 1:
                v = fold(edges[n])
                if not c:
                    s = slice(x0 * 64 + y0 * 8, x0 * 64 + y0 * 8 + 8)
                elif not b:
                    s = pl.ds(x0 * 64 + z0, 8, stride=8)
                else:
                    s = pl.ds(y0 * 8 + z0, 8, stride=64)
                rows[s, :] = rows[s, :] + v
            else:
                r = x0 * 64 + y0 * 8 + z0
                v = fold(corners[n])
                rows[r:r + 1, :] = rows[r:r + 1, :] + (v[0:1] + v[1:2])
        out_ref[p] = rows[...].T * m_ref[p].astype(F32)


def swap_scenes(v):
    scene = lax.axis_index("scene")
    v = v.reshape(2, 64, 7, 128)
    mine = lax.dynamic_index_in_dim(v, scene, 0, keepdims=False)
    theirs = lax.dynamic_index_in_dim(v, 1 - scene, 0, keepdims=False)
    return mine + lax.ppermute(theirs, "scene", [(0, 1), (1, 0)])


def sum_stage(v, stride):
    at = (lax.axis_index("brick") // stride) % 4
    v = v.reshape(4, stride, 7, 128)
    sent = [lax.ppermute(lax.dynamic_index_in_dim(v, at ^ d, 0, keepdims=False), "brick",
                         [(n, n ^ (d * stride)) for n in range(64)]) for d in (1, 2, 3)]
    return lax.dynamic_index_in_dim(v, at, 0, keepdims=False), sent


def whole(memory=pltpu.VMEM):
    return pl.BlockSpec(memory_space=memory)


def const_block(shape):
    return pl.BlockSpec(shape, lambda g: (0,) * len(shape))


def lead_block(shape):
    return pl.BlockSpec(shape, lambda g: (g,) + (0,) * (len(shape) - 1))


def params(mib):
    return pltpu.CompilerParams(vmem_limit_bytes=mib * 1024 * 1024)


def on_device(features, voxel_mask, weight, bias, cotangent, owner, slot, live):
    x = features[0].transpose(0, 2, 1)
    cot = cotangent[0].transpose(0, 2, 1)
    mask = voxel_mask.reshape(12, 1, 512)

    peer = owner.reshape(312)
    alive = live.reshape(312)
    kinds = jnp.asarray(np.tile(np.array(KIND, np.int32), 12))
    first = jnp.asarray(np.tile(np.array([FIRST[q] for q in KIND], np.int32), 12))
    per = jnp.asarray(np.tile(np.array([PER_KIND[q] for q in KIND], np.int32), 12))
    ordinal = jnp.asarray(np.tile(np.array(ORDINAL, np.int32), 12))
    entry = slot.reshape(312) * per + ordinal
    key = peer * 3 + kinds
    order = jnp.arange(312, dtype=jnp.int32)
    same = jnp.logical_and(key[:, None] == key[None, :], order[:, None] < order[None, :])
    place = first + jnp.sum(same.astype(jnp.int32), axis=0)
    spot = jnp.where(alive > 0, peer * 8 + place, -1)
    hit = spot[None, :] == jnp.arange(512, dtype=jnp.int32)[:, None]
    wanted = jnp.sum(jnp.where(hit, entry[None, :] + 1, 0), axis=1).reshape(64, 8) - 1
    code = (peer * 8 + place) * 2 + alive
    asked = lax.all_to_all(wanted, "brick", split_axis=0, concat_axis=0, tiled=True)

    wf, wb = pl.pallas_call(
        weights_kernel,
        in_specs=[whole()],
        out_specs=[whole(), whole()],
        out_shape=[jax.ShapeDtypeStruct((4608, 256), BF16)] * 2,
        compiler_params=params(16),
        cost_estimate=pl.CostEstimate(flops=0, bytes_accessed=6000000, transcendentals=0),
        name="weights",
    )(weight)

    faces, edges, corners, rows = pl.pallas_call(
        tables_kernel,
        grid=(3,),
        in_specs=[lead_block((4, 64, 512)), lead_block((4, 1, 512))],
        out_specs=[
            lead_block((24, 64, 128)),
            lead_block((48, 8, 128)),
            lead_block((32, 8, 128)),
            lead_block((4, 512, 128)),
        ],
        out_shape=[
            jax.ShapeDtypeStruct((72, 64, 128), F32),
            jax.ShapeDtypeStruct((144, 8, 128), F32),
            jax.ShapeDtypeStruct((96, 8, 128), F32),
            jax.ShapeDtypeStruct((12, 512, 128), F32),
        ],
        scratch_shapes=[pltpu.VMEM((512, 128), F32)],
        compiler_params=params(16),
        name="tables",
    )(x, mask)

    out = pl.pallas_call(
        pack_kernel,
        in_specs=[whole(pltpu.SMEM), whole(), whole(), whole()],
        out_specs=whole(),
        out_shape=jax.ShapeDtypeStruct((64, 80, 128), F32),
        compiler_params=params(16),
        name="pack",
    )(asked, faces, edges, corners)
    recv = lax.all_to_all(out, "brick", split_axis=0, concat_axis=0, tiled=True)

    bias2 = jnp.concatenate([bias, bias]).reshape(1, 128)
    turned_block = lead_block((2, 64, 512))
    turned_shape = jax.ShapeDtypeStruct((12, 64, 512), F32)
    mask_block = lead_block((2, 1, 512))
    brick_block = lead_block((2, 4, 2, 8, 8, 64))
    brick_shape = jax.ShapeDtypeStruct((12, 4, 2, 8, 8, 64), F32)
    packed_block = lead_block((2, 4, 8, 8, 128))
    packed_shape = jax.ShapeDtypeStruct((12, 4, 8, 8, 128), F32)
    own_pre, cot_p, windows = pl.pallas_call(
        own_forward_kernel,
        grid=(6,),
        in_specs=[lead_block((2, 512, 128)), mask_block, turned_block, const_block((4608, 256)), const_block((1, 128))],
        out_specs=[
            packed_block,
            packed_block,
            pl.BlockSpec((3, 1, 2, 5, 10, 16, 128), lambda g: (0, g, 0, 0, 0, 0, 0)),
        ],
        out_shape=[packed_shape, packed_shape, jax.ShapeDtypeStruct((3, 6, 2, 5, 10, 16, 128), BF16)],
        compiler_params=params(24),
        cost_estimate=pl.CostEstimate(flops=2 * 3072 * 4608 * 256, bytes_accessed=15000000, transcendentals=0),
        name="own_forward",
    )(rows, mask, cot, wf, bias2)

    flat = (3072, 128)
    side_x, side_y, side_z = (2, 3, 10, 6, 16, 128), (2, 3, 2, 5, 6, 16, 128), (2, 2, 5, 10, 16, 128)
    act, dpre, send, px, py, pz = pl.pallas_call(
        halo_kernel,
        in_specs=[whole(pltpu.SMEM)] + [whole()] * 5,
        out_specs=[whole()] * 6,
        out_shape=[
            jax.ShapeDtypeStruct(flat, F32),
            jax.ShapeDtypeStruct(flat, F32),
            jax.ShapeDtypeStruct((64, 80, 128), F32),
            jax.ShapeDtypeStruct(side_x, BF16),
            jax.ShapeDtypeStruct(side_y, BF16),
            jax.ShapeDtypeStruct(side_z, BF16),
        ],
        scratch_shapes=[
            pltpu.VMEM(flat, F32),
            pltpu.VMEM((3200, 128), F32),
            pltpu.VMEM((2, 3, 12, 6, 16, 128), BF16),
            pltpu.VMEM((2, 3, 2, 5, 6, 16, 128), BF16),
            pltpu.VMEM((2, 2, 6, 12, 16, 128), BF16),
            pltpu.VMEM((2, 960, 128), F32),
            pltpu.VMEM((2, 384, 128), F32),
            pltpu.VMEM((1600, 128), F32),
            pltpu.VMEM((8, 128), F32),
        ],
        compiler_params=params(40),
        name="halo",
    )(code, recv, own_pre.reshape(flat), cot_p.reshape(flat), wf, wb)
    back = lax.all_to_all(send, "brick", split_axis=0, concat_axis=0, tiled=True)
    act = act.reshape(packed_shape.shape)
    dpre = dpre.reshape(packed_shape.shape)

    z = pl.pallas_call(
        kernel_grad_kernel,
        grid=(3,),
        in_specs=[
            pl.BlockSpec((1, 6, 2, 5, 10, 16, 128), lambda l: (l, 0, 0, 0, 0, 0, 0)),
            pl.BlockSpec((2, 1, 10, 6, 16, 128), lambda l: (0, l, 0, 0, 0, 0)),
            pl.BlockSpec((2, 1, 2, 5, 6, 16, 128), lambda l: (0, l, 0, 0, 0, 0, 0)),
            const_block(side_z),
            const_block(packed_shape.shape),
        ],
        out_specs=lead_block((1, 3, 4, 128, 64)),
        out_shape=jax.ShapeDtypeStruct((3, 3, 4, 128, 64), F32),
        scratch_shapes=[
            pltpu.VMEM((256, 3072), BF16),
            pltpu.VMEM((2, 256, 768), BF16),
            pltpu.VMEM((2, 256, 384), BF16),
            pltpu.VMEM((2, 256, 512), BF16),
        ],
        compiler_params=params(40),
        cost_estimate=pl.CostEstimate(flops=0, bytes_accessed=1000, transcendentals=0),
        name="kernel_grad",
    )(windows, px, py, pz, dpre)
    kernel = z[:, :, 0:3, 0:64] + z[:, :, 1:4, 64:128]
    kernel = kernel.transpose(2, 1, 0, 4, 3).reshape(128, 864)
    kernel = jnp.pad(kernel, ((0, 0), (0, 32))).reshape(128, 7, 128)
    scale = 1.0 / math.sqrt(float(2 * 768 * 512))
    act, kernel = lax.optimization_barrier((act, kernel))
    total = swap_scenes(kernel)
    dpre, total = lax.optimization_barrier((dpre, total))
    kept, sent = sum_stage(total, 16)

    own = pl.pallas_call(
        own_backward_kernel,
        grid=(6,),
        in_specs=[packed_block, const_block((4608, 256))],
        out_specs=brick_block,
        out_shape=brick_shape,
        scratch_shapes=[pltpu.VMEM((3, 1, 2, 5, 10, 16, 128), BF16)],
        compiler_params=params(24),
        cost_estimate=pl.CostEstimate(flops=0, bytes_accessed=1000, transcendentals=0),
        name="own_backward",
    )(dpre, wb)
    activated = pl.pallas_call(
        activated_kernel,
        grid=(6,),
        in_specs=[packed_block, mask_block],
        out_specs=turned_block,
        out_shape=turned_shape,
        compiler_params=params(8),
        cost_estimate=pl.CostEstimate(flops=0, bytes_accessed=1000, transcendentals=0),
        name="activated",
    )(act, mask)

    total = kept + sent[0] + sent[1] + sent[2]
    own, total, activated = lax.optimization_barrier((own, total, activated))
    kept, sent = sum_stage(total, 4)
    total = kept + sent[0] + sent[1] + sent[2]
    back, total = lax.optimization_barrier((back, total))
    kept, sent = sum_stage(total, 1)

    grad = pl.pallas_call(
        collect_kernel,
        grid=(4,),
        in_specs=[
            pl.BlockSpec(memory_space=pltpu.SMEM),
            const_block((64, 80, 128)),
            lead_block((3, 4, 2, 8, 8, 64)),
            lead_block((3, 1, 512)),
        ],
        out_specs=lead_block((3, 64, 512)),
        out_shape=turned_shape,
        scratch_shapes=[
            pltpu.VMEM((73, 64, 128), F32),
            pltpu.VMEM((145, 8, 128), F32),
            pltpu.VMEM((97, 8, 128), F32),
            pltpu.VMEM((512, 64), F32),
        ],
        compiler_params=params(24),
        name="collect",
    )(asked, back, own, mask)
    grad, kept = lax.optimization_barrier((grad, kept))
    share = (kept + sent[0] + sent[1] + sent[2]).reshape(896)[:864] * scale
    return activated.transpose(0, 2, 1)[None], grad.transpose(0, 2, 1)[None], share


def solution(mesh):
    big = P("scene", "brick", None, None)
    flat = P("scene", "brick", None)
    return jax.shard_map(
        on_device,
        mesh=mesh,
        in_specs=(big, flat, P(), P(), big, big, flat, flat),
        out_specs=(big, big, P(("scene", "brick"))),
        check_vma=False,
    )
```

```python
import math

import jax
import jax.numpy as jnp
import numpy as np
from jax import lax
from jax.experimental import pallas as pl
from jax.experimental.pallas import tpu as pltpu
from jax.sharding import PartitionSpec as P

OFFSETS = [(a, b, c) for a in (-1, 0, 1) for b in (-1, 0, 1) for c in (-1, 0, 1) if (a, b, c) != (0, 0, 0)]
KIND = [sum(1 for v in o if v != 0) - 1 for o in OFFSETS]
ORDINAL = [KIND[:k].count(KIND[k]) for k in range(26)]
PER_KIND = (6, 12, 8)
FIRST = (0, 2, 5)
F32, BF16 = jnp.float32, jnp.bfloat16


def source_coord(step):
    return 0 if step == 1 else 7


def target_coord(step):
    return 9 if step == 1 else 0


def half_of(shape):
    return lax.broadcasted_iota(jnp.int32, shape, len(shape) - 1) >= 64


def swap(v):
    return pltpu.roll(v, 64, axis=v.ndim - 1)


def split_halves(v, low):
    top = v.astype(BF16).astype(F32)
    return jnp.where(low, top, v - top).astype(BF16)


def masked_rows(x_ref, m_ref, p):
    return (x_ref[p] * m_ref[p].astype(F32)).T


def tables_kernel(x_ref, m_ref, face_ref, edge_ref, corner_ref, row_ref, rows):
    for p in range(x_ref.shape[0]):
        x = masked_rows(x_ref, m_ref, p)
        x = jnp.concatenate([x, x], axis=1)
        rows[...] = x
        row_ref[p] = x
        for k, (a, b, c) in enumerate(OFFSETS):
            n = ORDINAL[k]
            x0, y0, z0 = source_coord(a), source_coord(b), source_coord(c)
            if KIND[k] == 0:
                for i in range(8):
                    if a:
                        v = rows[x0 * 64 + i * 8:x0 * 64 + i * 8 + 8, :]
                    elif b:
                        v = rows[i * 64 + y0 * 8:i * 64 + y0 * 8 + 8, :]
                    else:
                        v = rows[pl.ds(i * 64 + z0, 8, stride=8), :]
                    face_ref[p * 6 + n, i * 8:i * 8 + 8, :] = v
            elif KIND[k] == 1:
                if not c:
                    v = rows[x0 * 64 + y0 * 8:x0 * 64 + y0 * 8 + 8, :]
                elif not b:
                    v = rows[pl.ds(x0 * 64 + z0, 8, stride=8), :]
                else:
                    v = rows[pl.ds(y0 * 8 + z0, 8, stride=64), :]
                edge_ref[p * 12 + n] = v
            else:
                r = x0 * 64 + y0 * 8 + z0
                corner_ref[p * 8 + n] = jnp.broadcast_to(rows[r:r + 1, :], (8, 128))


def pack_kernel(want_ref, face_ref, edge_ref, corner_ref, out_ref):
    high = half_of((64, 128))
    high8 = half_of((8, 128))
    row0 = lax.broadcasted_iota(jnp.int32, (8, 128), 0) == 0

    def body(p, carry):
        q = [jnp.maximum(want_ref[p, j], 0) for j in range(7)]
        out_ref[p, 0:64, :] = jnp.where(high, face_ref[q[1]], face_ref[q[0]])
        out_ref[p, 64:72, :] = jnp.where(high8, edge_ref[q[3]], edge_ref[q[2]])
        corners = jnp.where(row0, corner_ref[q[5]], corner_ref[q[6]])
        out_ref[p, 72:80, :] = jnp.where(high8, corners, edge_ref[q[4]])
        return carry

    lax.fori_loop(0, 64, body, 0)


def placed(v, other):
    return jnp.where(other, v, swap(v))


def shifted(v, l, row):
    if l == 1:
        return v
    turned = pltpu.roll(v, 1 if l == 0 else 7, axis=0)
    return jnp.where(row == (0 if l == 0 else 7), 0.0, turned)


def weights_kernel(w_ref, f_ref, b_ref):
    zero = jnp.zeros((64, 64), F32)

    def fill(out_ref, s, sides):
        c = jnp.concatenate(sides, axis=1)
        top = c.astype(BF16)
        low = (c - top.astype(F32)).astype(BF16)
        v = jnp.concatenate([top, low], axis=1)
        out_ref[s * 128:s * 128 + 128, :] = jnp.concatenate([v, v], axis=0)

    for j in range(3):
        for l in range(3):
            w = [w_ref[i * 9 + j * 3 + l] for i in range(3)]
            t = [w_ref[(2 - i) * 9 + (2 - j) * 3 + 2 - l].T for i in range(3)]
            for i in range(4):
                s = i * 9 + j * 3 + l
                fill(f_ref, s, [w[i] if i < 3 else zero, w[i - 1] if i else zero])
                fill(b_ref, s, [t[i] if i < 3 else zero, t[i - 1] if i else zero])


def convolve(a_ref, w_ref):
    slices = [(i, j, l) for i in range(4) for j in range(3) for l in range(3)]
    acc = None
    for s in range(0, 36, 4):
        parts = [a_ref[l, 0, i % 2, i // 2:i // 2 + 4, j:j + 8].reshape(512, 128) for i, j, l in slices[s:s + 4]]
        lhs = jnp.concatenate(parts, axis=1)
        d = jnp.dot(lhs, w_ref[s * 128:s * 128 + 512, :], preferred_element_type=F32)
        acc = d if acc is None else acc + d
    return (acc[:, :128] + acc[:, 128:]).reshape(4, 8, 16, 128)


def clear_border(a_ref):
    spare = jnp.zeros((16, 128), BF16)
    for l in range(3):
        for x in range(10):
            for y in range(10):
                if x in (0, 9) or y in (0, 9):
                    a_ref[l, 0, x % 2, x // 2, y] = spare


def own_forward_kernel(x_ref, m_ref, cot_ref, w_ref, bias_ref, pre_ref, cotm_ref, a_ref):
    clear_border(a_ref)
    row = lax.broadcasted_iota(jnp.int32, (8, 128), 0)
    low = jnp.logical_not(half_of((16, 128)))
    for x in range(8):
        for y in range(8):
            r = x * 64 + y * 8
            for l in range(3):
                v = jnp.concatenate([shifted(x_ref[b, r:r + 8, :], l, row) for b in range(2)], axis=0)
                a_ref[l, 0, (x + 1) % 2, (x + 1) // 2, y + 1] = split_halves(v, low)
    pre = convolve(a_ref, w_ref) + bias_ref[...]
    for b in range(2):
        pre_ref[b] = pre[:, :, b * 8:b * 8 + 8]
        c = masked_rows(cot_ref, m_ref, b).reshape(4, 2, 8, 8, 64)
        cotm_ref[b] = jnp.concatenate([c[:, 0], c[:, 1]], axis=-1)


def own_backward_kernel(d_ref, w_ref, own_ref, a_ref):
    @pl.when(pl.program_id(0) == 0)
    def _():
        a_ref[...] = jnp.zeros_like(a_ref)

    row = lax.broadcasted_iota(jnp.int32, (8, 128), 0)
    half = half_of((8, 128))
    low = jnp.logical_not(half_of((16, 128)))
    for x in range(8):
        for y in range(8):
            cols = []
            for b in range(2):
                cols.append(placed(d_ref[b, x // 2, y], half if x % 2 else jnp.logical_not(half)))
            for l in range(3):
                v = jnp.concatenate([shifted(cols[b], l, row) for b in range(2)], axis=0)
                a_ref[l, 0, (x + 1) % 2, (x + 1) // 2, y + 1] = split_halves(v, low)
    out = convolve(a_ref, w_ref)
    for b in range(2):
        own_ref[b, :, 0] = out[:, :, b * 8:b * 8 + 8, :64]
        own_ref[b, :, 1] = out[:, :, b * 8:b * 8 + 8, 64:]


def activated_kernel(act_ref, m_ref, out_ref):
    for b in range(2):
        mask = m_ref[b].astype(F32)
        for h in range(2):
            t = act_ref[b, 2 * h:2 * h + 2].reshape(128, 128).T
            v = jnp.concatenate([t[:64, :64], t[64:, :64], t[:64, 64:], t[64:, 64:]], axis=1)
            a = slice(h * 256, h * 256 + 256)
            out_ref[b, :, a] = v * mask[:, a]


def unpack_code(code_ref, b, k):
    c = code_ref[b * 26 + k]
    return c >> 4, (c >> 1) & 7, c & 1


def edge_rows(pos):
    e = pos - 2
    return pl.ds(pl.multiple_of(64 + 8 * (e >> 1), 8), 8), e & 1


def halo_kernel(code_ref, recv_ref, own_hbm, cot_hbm, wf_hbm, wb_hbm,
                act_hbm, dpre_hbm, send_ref, px_hbm, py_hbm, pz_hbm,
                pre, cot_ref, wf_ref, wb_ref, act_ref, dpre_ref, px, py, pz,
                zf, qx, qy, qz, rx, ry, rz, tmp, sems):
    arriving = [pltpu.make_async_copy(a, b, sems.at[n]) for n, (a, b) in enumerate(
        [(own_hbm, pre), (wf_hbm, wf_ref), (cot_hbm, cot_ref), (wb_hbm, wb_ref)])]
    leaving = [pltpu.make_async_copy(a, b, sems.at[4 + n]) for n, (a, b) in enumerate(
        [(px, px_hbm), (py, py_hbm), (pz, pz_hbm), (act_ref, act_hbm), (dpre_ref, dpre_hbm)])]
    for c in arriving:
        c.start()
    high8 = half_of((8, 128))
    half8 = high8.astype(jnp.int32)
    row = lax.broadcasted_iota(jnp.int32, (8, 128), 0)
    low = jnp.logical_not(half_of((16, 128)))
    spare = jnp.zeros((16, 128), BF16)

    def zrow(s, x, y, b):
        return ((s * 10 + x) * 10 + y) * 16 + b

    for s in range(2):
        for l in range(3):
            for g in range(6):
                py[s, l, 0, 0, g] = spare
                py[s, l, 1, 4, g] = spare
        for x in range(10):
            for y in range(10):
                r = zrow(s, x, y, 8)
                zf[r:r + 8, :] = jnp.zeros((8, 128), F32)

    def face(k, b, i):
        o, pos, alive = unpack_code(code_ref, b, k)
        v = recv_ref[o, i * 8:i * 8 + 8, :]
        return placed(v, half8 == pos) * alive.astype(F32)

    def edge(k, b):
        o, pos, alive = unpack_code(code_ref, b, k)
        rows, h = edge_rows(pos)
        return placed(recv_ref[o, rows, :], half8 == h) * alive.astype(F32)

    for k, (dx, dy, dz) in enumerate(OFFSETS):
        xt, yt = target_coord(dx), target_coord(dy)
        sx, sy, sz = int(dx == 1), int(dy == 1), int(dz == 1)
        for g in range(6):
            pair = (2 * g, 2 * g + 1)
            if KIND[k] == 0 and not dz:
                for i in range(8):
                    v = [face(k, b, i) for b in pair]
                    for l in range(3):
                        w = split_halves(jnp.concatenate([shifted(u, l, row) for u in v], axis=0), low)
                        if dx:
                            px[sx, l, i + 1, g] = w
                        else:
                            py[sy, l, (i + 1) % 2, (i + 1) // 2, g] = w
            elif KIND[k] == 1 and not dz:
                v = [edge(k, b) for b in pair]
                for l in range(3):
                    px[sx, l, yt, g] = split_halves(jnp.concatenate([shifted(u, l, row) for u in v], axis=0), low)
            else:
                for b in pair:
                    if KIND[k] == 0:
                        for i in range(8):
                            zf[pl.ds(zrow(sz, i + 1, 1, b), 8, stride=16), :] = face(k, b, i)
                    elif KIND[k] == 1 and dx:
                        zf[pl.ds(zrow(sz, xt, 1, b), 8, stride=16), :] = edge(k, b)
                    elif KIND[k] == 1:
                        zf[pl.ds(zrow(sz, 1, yt, b), 8, stride=160), :] = edge(k, b)
                    else:
                        o, pos, alive = unpack_code(code_ref, b, k)
                        v = recv_ref[o, 72:80, :]
                        v = jnp.where(pos == 5, v[0:1, :], v[1:2, :])
                        r = zrow(sz, xt, yt, b)
                        zf[r:r + 1, :] = placed(v, high8[0:1]) * alive.astype(F32)
    for s in range(2):
        for x in range(10):
            for y in range(10):
                r = zrow(s, x, y, 0)
                pz[s, x % 2, x // 2, y] = split_halves(zf[r:r + 16, :], low)

    def side_x(src, s, ii, ys, w_ref):
        parts = [src[s, l, j:j + ys].reshape(ys * 96, 128) for j in range(3) for l in range(3)]
        v = jnp.dot(jnp.concatenate(parts, axis=1), w_ref[ii * 1152:ii * 1152 + 1152, :], preferred_element_type=F32)
        return v[:, :128] + v[:, 128:]

    def side_y(src, s, j, w_ref):
        acc = None
        for h in range(2):
            parts = [src[s, l, i, h:h + 4].reshape(384, 128) for i in range(2) for l in range(3)]
            at = [((2 * h + i) * 9 + j * 3) * 128 for i in range(2)]
            w = jnp.concatenate([w_ref[a:a + 384, :] for a in at], axis=0)
            v = jnp.dot(jnp.concatenate(parts, axis=1), w, preferred_element_type=F32)
            acc = v if acc is None else acc + v
        return acc[:, :128] + acc[:, 128:]

    def side_z(src, s, l, xs, ys, w_ref):
        slices = [(i, j) for i in range(4) for j in range(3)]
        acc = None
        for n in range(0, 12, 4):
            parts = [src[s, i % 2, i // 2:i // 2 + xs, j:j + ys].reshape(xs * ys * 16, 128) for i, j in slices[n:n + 4]]
            at = [(i * 9 + j * 3 + l) * 128 for i, j in slices[n:n + 4]]
            w = jnp.concatenate([w_ref[a:a + 128, :] for a in at], axis=0)
            v = jnp.dot(jnp.concatenate(parts, axis=1), w, preferred_element_type=F32)
            acc = v if acc is None else acc + v
        return acc[:, :128] + acc[:, 128:]

    def prow(b, xh, y, z):
        return ((b * 4 + xh) * 8 + y) * 8 + z

    for c in leaving[:3]:
        c.start()
    arriving[0].wait()
    arriving[1].wait()
    for s in range(2):
        v = side_x(px, s, 3 * s, 8, wf_ref)
        for y in range(8):
            for b in range(12):
                r, q = prow(b, 3 * s, y, 0), (y * 12 + b) * 8
                pre[r:r + 8, :] += v[q:q + 8]
        v = side_y(py, s, 2 * s, wf_ref)
        for xh in range(4):
            for b in range(12):
                r, q = prow(b, xh, 7 * s, 0), (xh * 12 + b) * 8
                pre[r:r + 8, :] += v[q:q + 8]
        v = side_z(pz, s, 2 * s, 4, 8, wf_ref)
        for xh in range(4):
            for y in range(8):
                q = (xh * 8 + y) * 16
                a = pl.ds(prow(0, xh, y, 7 * s), 8, stride=256)
                pre[a, :] = pre[a, :] + v[q:q + 8]
                a = pl.ds(prow(8, xh, y, 7 * s), 4, stride=256)
                pre[a, :] = pre[a, :] + v[q + 8:q + 12]

    def activate(n, carry):
        a = pl.ds(pl.multiple_of(n * 128, 128), 128)
        p = pre[a, :]
        sig = jax.nn.sigmoid(p)
        ps = p * sig
        act_ref[a, :] = ps
        dpre_ref[a, :] = cot_ref[a, :] * (sig + ps * (1.0 - sig))
        return carry

    arriving[2].wait()
    lax.fori_loop(0, 24, activate, 0)
    leaving[3].start()
    leaving[4].start()

    for s in range(2):
        for l in range(3):
            for g in range(6):
                for y in (0, 1, 10, 11):
                    qx[s, l, y, g] = spare
                qy[s, l, 0, 0, g] = spare
                qy[s, l, 1, 4, g] = spare
    qz[...] = jnp.zeros_like(qz)
    wanted = [jnp.logical_not(high8), high8]
    wanted16 = [low, jnp.logical_not(low)]
    for s in range(2):
        for g in range(6):
            for y in range(8):
                v = []
                for b in (2 * g, 2 * g + 1):
                    r = prow(b, 3 * s, y, 0)
                    v.append(placed(dpre_ref[r:r + 8, :], wanted[s]))
                for l in range(3):
                    qx[s, l, y + 2, g] = split_halves(jnp.concatenate([shifted(u, l, row) for u in v], axis=0), low)
            for x in range(8):
                v = []
                for b in (2 * g, 2 * g + 1):
                    r = prow(b, x // 2, 7 * s, 0)
                    v.append(placed(dpre_ref[r:r + 8, :], wanted[x % 2]))
                for l in range(3):
                    w = split_halves(jnp.concatenate([shifted(u, l, row) for u in v], axis=0), low)
                    qy[s, l, (x + 1) % 2, (x + 1) // 2, g] = w
        for xh in range(4):
            for y in range(8):
                first = dpre_ref[pl.ds(prow(0, xh, y, 7 * s), 8, stride=256), :]
                last = dpre_ref[pl.ds(prow(8, xh, y, 7 * s), 4, stride=256), :]
                v = jnp.concatenate([first, last, jnp.zeros((4, 128), F32)], axis=0)
                for p in range(2):
                    qz[s, p, xh + 1, y + 2] = split_halves(placed(v, wanted16[p]), low)
    arriving[3].wait()
    for s in range(2):
        rx[s] = side_x(qx, s, 3 - 3 * s, 10, wb_ref)
        ry[s] = side_y(qy, s, 2 - 2 * s, wb_ref)
        rz[s * 800:s * 800 + 800, :] = side_z(qz, s, 2 - 2 * s, 5, 10, wb_ref)

    def rzrow(s, xh, y, b):
        return s * 800 + (xh * 10 + y) * 16 + b

    send_ref[...] = jnp.zeros_like(send_ref)
    for b in range(12):
        for k, (dx, dy, dz) in enumerate(OFFSETS):
            o, pos, _ = unpack_code(code_ref, b, k)
            xt, yt = target_coord(dx), target_coord(dy)
            sx, sy, sz = int(dx == 1), int(dy == 1), int(dz == 1)
            if KIND[k] == 0:
                for i in range(8):
                    if dx:
                        r, par = ((i + 1) * 12 + b) * 8, 1 - sx
                        v = rx[sx, r:r + 8, :]
                    elif dy:
                        r, par = ((i // 2) * 12 + b) * 8, i % 2
                        v = ry[sy, r:r + 8, :]
                    else:
                        par = (i + 1) % 2
                        v = rz[pl.ds(rzrow(sz, (i + 1) // 2, 1, b), 8, stride=16), :]
                    v = placed(v, wanted[par])
                    a = slice(i * 8, i * 8 + 8)
                    send_ref[o, a, :] = jnp.where(half8 == pos, v, send_ref[o, a, :])
            elif KIND[k] == 1:
                if not dz:
                    r = (yt * 12 + b) * 8
                    v = placed(rx[sx, r:r + 8, :], wanted[1 - sx])
                elif dx:
                    v = placed(rz[pl.ds(rzrow(sz, xt // 2, 1, b), 8, stride=16), :], wanted[xt % 2])
                else:
                    for q in range(2):
                        tmp[pl.ds(q, 4, stride=2), :] = rz[pl.ds(rzrow(sz, q, yt, b), 4, stride=160), :]
                    v = placed(tmp[...], half8 == 1 - (row & 1))
                a, h = edge_rows(pos)
                send_ref[o, a, :] = jnp.where(half8 == h, v, send_ref[o, a, :])
            else:
                r = rzrow(sz, xt // 2, yt, b)
                v = placed(jnp.broadcast_to(rz[r:r + 1, :], (8, 128)), wanted[xt % 2])
                spot = jnp.logical_and(row == pos - 5, high8)
                send_ref[o, 72:80, :] = jnp.where(spot, v, send_ref[o, 72:80, :])
    for c in leaving:
        c.wait()


def turned_terms(out_ref, at, v):
    t = v.T
    n = t.shape[1]
    top = t.astype(BF16)
    out_ref[0:128, at:at + n] = top
    out_ref[128:256, at:at + n] = (t - top.astype(F32)).astype(BF16)


def kernel_grad_kernel(a_ref, px_ref, py_ref, pz_ref, d_ref, out_ref, dt, dx, dy, dz, sums):
    l = pl.program_id(0)

    @pl.when(l == 0)
    def _():
        for g in range(6):
            v = jnp.concatenate([d_ref[2 * g], d_ref[2 * g + 1]], axis=2)
            turned_terms(dt, g * 512, v.reshape(512, 128))
        flat = d_ref.reshape(3072, 128)
        for s in range(2):
            for y in range(8):
                v = jnp.concatenate([d_ref[b, 3 * s, y] for b in range(12)], axis=0)
                if y % 4 == 0:
                    held = []
                held.append(v)
                if y % 4 == 3:
                    turned_terms(dx.at[s], (y - 3) * 96, jnp.concatenate(held, axis=0))
            v = [d_ref[b, xh, 7 * s] for xh in range(4) for b in range(12)]
            turned_terms(dy.at[s], 0, jnp.concatenate(v, axis=0))
            v = []
            for n in range(32):
                r = n * 8 + 7 * s
                v.append(flat[pl.ds(r, 8, stride=256), :])
                v.append(flat[pl.ds(r + 2048, 4, stride=256), :])
                v.append(jnp.zeros((4, 128), F32))
            turned_terms(dz.at[s], 0, jnp.concatenate(v, axis=0))

    def product(d, parts):
        s = jnp.dot(d, jnp.concatenate(parts, axis=1), preferred_element_type=F32)
        s = s[:128] + s[128:]
        out = []
        for q in range(len(parts)):
            v = s[:, q * 128:q * 128 + 128]
            out.append((v + swap(v))[:, :64])
        return out

    for j in range(3):
        for h in range(2):
            parts = [a_ref[0, :, q, h:h + 4, j:j + 8].reshape(3072, 128) for q in range(2)]
            for q, v in enumerate(product(dt[...], parts)):
                sums[j, 2 * h + q] = v
    for s in range(2):
        parts = [px_ref[s, 0, j:j + 8].reshape(768, 128) for j in range(3)]
        for j, v in enumerate(product(dx[s], parts)):
            sums[j, 3 * s] += v
        parts = [py_ref[s, 0, i % 2, i // 2:i // 2 + 4].reshape(384, 128) for i in range(4)]
        for i, v in enumerate(product(dy[s], parts)):
            sums[2 * s, i] += v

    @pl.when(l != 1)
    def _():
        s = l // 2
        for j in range(3):
            parts = [pz_ref[s, i % 2, i // 2:i // 2 + 4, j:j + 8].reshape(512, 128) for i in range(4)]
            for i, v in enumerate(product(dz[s], parts)):
                sums[j, i] += v

    for i in range(3):
        for j in range(3):
            out_ref[i, j, 0] = (sums[j, i, 0:64] + sums[j, i + 1, 64:128]).T


def collect_kernel(want_ref, back_ref, own_ref, m_ref, out_ref, faces, edges, corners, rows):
    g = pl.program_id(0)
    high = half_of((64, 128))
    high8 = half_of((8, 128))
    rowi = lax.broadcasted_iota(jnp.int32, (8, 128), 0)

    @pl.when(g == 0)
    def _():
        faces[...] = jnp.zeros_like(faces)
        edges[...] = jnp.zeros_like(edges)
        corners[...] = jnp.zeros_like(corners)

        def index(p, j, spare):
            q = want_ref[p, j]
            return jnp.where(q < 0, spare, q)

        def body(p, carry):
            v = back_ref[p, 0:64, :]
            faces[index(p, 0, 72)] += jnp.where(high, 0.0, v)
            faces[index(p, 1, 72)] += jnp.where(high, v, 0.0)
            v = back_ref[p, 64:72, :]
            edges[index(p, 2, 144)] += jnp.where(high8, 0.0, v)
            edges[index(p, 3, 144)] += jnp.where(high8, v, 0.0)
            v = back_ref[p, 72:80, :]
            edges[index(p, 4, 144)] += jnp.where(high8, 0.0, v)
            v = jnp.where(high8, v, 0.0)
            corners[index(p, 5, 96)] += jnp.where(rowi == 0, v, 0.0)
            corners[index(p, 6, 96)] += jnp.where(rowi == 1, v, 0.0)
            return carry

        lax.fori_loop(0, 64, body, 0)

    def fold(v):
        return (v + swap(v))[:, :64]

    bricks = own_ref.shape[0]
    for p in range(bricks):
        rows[...] = own_ref[p].reshape(512, 64)
        for k, (a, b, c) in enumerate(OFFSETS):
            n = (g * bricks + p) * PER_KIND[KIND[k]] + ORDINAL[k]
            x0, y0, z0 = source_coord(a), source_coord(b), source_coord(c)
            if KIND[k] == 0:
                for i in range(8):
                    v = fold(faces[n, i * 8:i * 8 + 8, :])
                    if a:
                        s = slice(x0 * 64 + i * 8, x0 * 64 + i * 8 + 8)
                    elif b:
                        s = slice(i * 64 + y0 * 8, i * 64 + y0 * 8 + 8)
                    else:
                        s = pl.ds(i * 64 + z0, 8, stride=8)
                    rows[s, :] = rows[s, :] + v
            elif KIND[k] == 1:
                v = fold(edges[n])
                if not c:
                    s = slice(x0 * 64 + y0 * 8, x0 * 64 + y0 * 8 + 8)
                elif not b:
                    s = pl.ds(x0 * 64 + z0, 8, stride=8)
                else:
                    s = pl.ds(y0 * 8 + z0, 8, stride=64)
                rows[s, :] = rows[s, :] + v
            else:
                r = x0 * 64 + y0 * 8 + z0
                v = fold(corners[n])
                rows[r:r + 1, :] = rows[r:r + 1, :] + (v[0:1] + v[1:2])
        out_ref[p] = rows[...].T * m_ref[p].astype(F32)


def swap_scenes(v):
    scene = lax.axis_index("scene")
    mine = lax.dynamic_slice_in_dim(v, scene * 864, 864, 0)
    theirs = lax.dynamic_slice_in_dim(v, (1 - scene) * 864, 864, 0)
    return mine + lax.ppermute(theirs, "scene", [(0, 1), (1, 0)])


def sum_stage(v, stride):
    at = (lax.axis_index("brick") // stride) % 4
    n = v.shape[0] // 4

    def quarter(k):
        return lax.dynamic_slice_in_dim(v, k * n, n, 0)

    sent = [lax.ppermute(quarter(at ^ d), "brick", [(m, m ^ (d * stride)) for m in range(64)]) for d in (1, 2, 3)]
    return quarter(at), sent


def whole(memory=pltpu.VMEM):
    return pl.BlockSpec(memory_space=memory)


def const_block(shape):
    return pl.BlockSpec(shape, lambda g: (0,) * len(shape))


def lead_block(shape):
    return pl.BlockSpec(shape, lambda g: (g,) + (0,) * (len(shape) - 1))


def in_hbm(x):
    return pltpu.with_memory_space_constraint(x, pltpu.HBM)


def hbm_out(shape, kind):
    return pltpu.HBM(shape, kind)


def params(mib):
    return pltpu.CompilerParams(vmem_limit_bytes=mib * 1024 * 1024)


def on_device(features, voxel_mask, weight, bias, cotangent, owner, slot, live):
    x = features[0].transpose(0, 2, 1)
    cot = cotangent[0].transpose(0, 2, 1)
    mask = voxel_mask.reshape(12, 1, 512)

    peer = owner.reshape(312)
    alive = live.reshape(312)
    kinds = jnp.asarray(np.tile(np.array(KIND, np.int32), 12))
    first = jnp.asarray(np.tile(np.array([FIRST[q] for q in KIND], np.int32), 12))
    per = jnp.asarray(np.tile(np.array([PER_KIND[q] for q in KIND], np.int32), 12))
    ordinal = jnp.asarray(np.tile(np.array(ORDINAL, np.int32), 12))
    entry = slot.reshape(312) * per + ordinal
    key = peer * 3 + kinds
    order = jnp.arange(312, dtype=jnp.int32)
    same = jnp.logical_and(key[:, None] == key[None, :], order[:, None] < order[None, :])
    place = first + jnp.sum(same.astype(jnp.int32), axis=0)
    spot = jnp.where(alive > 0, peer * 8 + place, -1)
    hit = spot[None, :] == jnp.arange(512, dtype=jnp.int32)[:, None]
    wanted = jnp.sum(jnp.where(hit, entry[None, :] + 1, 0), axis=1).reshape(64, 8) - 1
    code = (peer * 8 + place) * 2 + alive
    asked = lax.all_to_all(wanted, "brick", split_axis=0, concat_axis=0, tiled=True)

    wf, wb = pl.pallas_call(
        weights_kernel,
        in_specs=[whole()],
        out_specs=[whole(), whole()],
        out_shape=[hbm_out((4608, 256), BF16)] * 2,
        compiler_params=params(16),
        cost_estimate=pl.CostEstimate(flops=0, bytes_accessed=6000000, transcendentals=0),
        name="weights",
    )(weight)

    faces, edges, corners, rows = pl.pallas_call(
        tables_kernel,
        grid=(3,),
        in_specs=[lead_block((4, 64, 512)), lead_block((4, 1, 512))],
        out_specs=[
            lead_block((24, 64, 128)),
            lead_block((48, 8, 128)),
            lead_block((32, 8, 128)),
            lead_block((4, 512, 128)),
        ],
        out_shape=[
            jax.ShapeDtypeStruct((72, 64, 128), F32),
            jax.ShapeDtypeStruct((144, 8, 128), F32),
            jax.ShapeDtypeStruct((96, 8, 128), F32),
            hbm_out((12, 512, 128), F32),
        ],
        scratch_shapes=[pltpu.VMEM((512, 128), F32)],
        compiler_params=params(16),
        name="tables",
    )(x, mask)

    out = pl.pallas_call(
        pack_kernel,
        in_specs=[whole(pltpu.SMEM), whole(), whole(), whole()],
        out_specs=whole(),
        out_shape=jax.ShapeDtypeStruct((64, 80, 128), F32),
        compiler_params=params(16),
        name="pack",
    )(asked, faces, edges, corners)
    recv = lax.all_to_all(out, "brick", split_axis=0, concat_axis=0, tiled=True)

    bias2 = jnp.concatenate([bias, bias]).reshape(1, 128)
    turned_block = lead_block((2, 64, 512))
    turned_shape = jax.ShapeDtypeStruct((12, 64, 512), F32)
    mask_block = lead_block((2, 1, 512))
    brick_block = lead_block((2, 4, 2, 8, 8, 64))
    brick_shape = jax.ShapeDtypeStruct((12, 4, 2, 8, 8, 64), F32)
    packed_block = lead_block((2, 4, 8, 8, 128))
    packed_shape = jax.ShapeDtypeStruct((12, 4, 8, 8, 128), F32)
    own_pre, cot_p, windows = pl.pallas_call(
        own_forward_kernel,
        grid=(6,),
        in_specs=[lead_block((2, 512, 128)), mask_block, turned_block, const_block((4608, 256)), const_block((1, 128))],
        out_specs=[
            packed_block,
            packed_block,
            pl.BlockSpec((3, 1, 2, 5, 10, 16, 128), lambda g: (0, g, 0, 0, 0, 0, 0)),
        ],
        out_shape=[
            hbm_out(packed_shape.shape, F32),
            hbm_out(packed_shape.shape, F32),
            hbm_out((3, 6, 2, 5, 10, 16, 128), BF16),
        ],
        compiler_params=params(24),
        cost_estimate=pl.CostEstimate(flops=2 * 3072 * 4608 * 256, bytes_accessed=15000000, transcendentals=0),
        name="own_forward",
    )(in_hbm(rows), mask, in_hbm(cot), in_hbm(wf), bias2)

    flat = (3072, 128)
    side_x, side_y, side_z = (2, 3, 10, 6, 16, 128), (2, 3, 2, 5, 6, 16, 128), (2, 2, 5, 10, 16, 128)
    held = pl.BlockSpec(memory_space=pl.ANY)
    act, dpre, send, px, py, pz = pl.pallas_call(
        halo_kernel,
        in_specs=[whole(pltpu.SMEM), whole()] + [held] * 4,
        out_specs=[held, held, whole(), held, held, held],
        out_shape=[
            hbm_out(flat, F32),
            hbm_out(flat, F32),
            jax.ShapeDtypeStruct((64, 80, 128), F32),
            hbm_out(side_x, BF16),
            hbm_out(side_y, BF16),
            hbm_out(side_z, BF16),
        ],
        scratch_shapes=[
            pltpu.VMEM(flat, F32),
            pltpu.VMEM(flat, F32),
            pltpu.VMEM((4608, 256), BF16),
            pltpu.VMEM((4608, 256), BF16),
            pltpu.VMEM(flat, F32),
            pltpu.VMEM(flat, F32),
            pltpu.VMEM(side_x, BF16),
            pltpu.VMEM(side_y, BF16),
            pltpu.VMEM(side_z, BF16),
            pltpu.VMEM((3200, 128), F32),
            pltpu.VMEM((2, 3, 12, 6, 16, 128), BF16),
            pltpu.VMEM((2, 3, 2, 5, 6, 16, 128), BF16),
            pltpu.VMEM((2, 2, 6, 12, 16, 128), BF16),
            pltpu.VMEM((2, 960, 128), F32),
            pltpu.VMEM((2, 384, 128), F32),
            pltpu.VMEM((1600, 128), F32),
            pltpu.VMEM((8, 128), F32),
            pltpu.SemaphoreType.DMA((9,)),
        ],
        compiler_params=params(44),
        name="halo",
    )(code, recv, in_hbm(own_pre.reshape(flat)), in_hbm(cot_p.reshape(flat)), in_hbm(wf), in_hbm(wb))
    back = lax.all_to_all(send, "brick", split_axis=0, concat_axis=0, tiled=True)
    act = act.reshape(packed_shape.shape)
    dpre = dpre.reshape(packed_shape.shape)

    z = pl.pallas_call(
        kernel_grad_kernel,
        grid=(3,),
        in_specs=[
            pl.BlockSpec((1, 6, 2, 5, 10, 16, 128), lambda l: (l, 0, 0, 0, 0, 0, 0)),
            pl.BlockSpec((2, 1, 10, 6, 16, 128), lambda l: (0, l, 0, 0, 0, 0)),
            pl.BlockSpec((2, 1, 2, 5, 6, 16, 128), lambda l: (0, l, 0, 0, 0, 0, 0)),
            const_block(side_z),
            const_block(packed_shape.shape),
        ],
        out_specs=pl.BlockSpec((3, 3, 1, 64, 64), lambda l: (0, 0, l, 0, 0)),
        out_shape=jax.ShapeDtypeStruct((3, 3, 3, 64, 64), F32),
        scratch_shapes=[
            pltpu.VMEM((256, 3072), BF16),
            pltpu.VMEM((2, 256, 768), BF16),
            pltpu.VMEM((2, 256, 384), BF16),
            pltpu.VMEM((2, 256, 512), BF16),
            pltpu.VMEM((3, 4, 128, 64), F32),
        ],
        compiler_params=params(40),
        cost_estimate=pl.CostEstimate(flops=0, bytes_accessed=1000, transcendentals=0),
        name="kernel_grad",
    )(in_hbm(windows), in_hbm(px), in_hbm(py), in_hbm(pz), in_hbm(dpre))
    kernel = z.reshape(1728, 64)
    scale = 1.0 / math.sqrt(float(2 * 768 * 512))
    act, kernel = lax.optimization_barrier((act, kernel))
    total = swap_scenes(kernel)
    dpre, total = lax.optimization_barrier((dpre, total))
    kept, sent = sum_stage(total, 16)

    own = pl.pallas_call(
        own_backward_kernel,
        grid=(6,),
        in_specs=[packed_block, const_block((4608, 256))],
        out_specs=brick_block,
        out_shape=brick_shape,
        scratch_shapes=[pltpu.VMEM((3, 1, 2, 5, 10, 16, 128), BF16)],
        compiler_params=params(24),
        cost_estimate=pl.CostEstimate(flops=0, bytes_accessed=1000, transcendentals=0),
        name="own_backward",
    )(in_hbm(dpre), in_hbm(wb))
    activated = pl.pallas_call(
        activated_kernel,
        grid=(6,),
        in_specs=[packed_block, mask_block],
        out_specs=turned_block,
        out_shape=turned_shape,
        compiler_params=params(8),
        cost_estimate=pl.CostEstimate(flops=0, bytes_accessed=1000, transcendentals=0),
        name="activated",
    )(in_hbm(act), mask)

    total = kept + sent[0] + sent[1] + sent[2]
    own, total, activated = lax.optimization_barrier((own, total, activated))
    total = jnp.pad(total.reshape(16, 864), ((0, 0), (0, 32))).reshape(16, 7, 128)
    kept, sent = sum_stage(total, 4)
    total = kept + sent[0] + sent[1] + sent[2]
    back, total = lax.optimization_barrier((back, total))
    kept, sent = sum_stage(total, 1)

    grad = pl.pallas_call(
        collect_kernel,
        grid=(4,),
        in_specs=[
            pl.BlockSpec(memory_space=pltpu.SMEM),
            const_block((64, 80, 128)),
            lead_block((3, 4, 2, 8, 8, 64)),
            lead_block((3, 1, 512)),
        ],
        out_specs=lead_block((3, 64, 512)),
        out_shape=turned_shape,
        scratch_shapes=[
            pltpu.VMEM((73, 64, 128), F32),
            pltpu.VMEM((145, 8, 128), F32),
            pltpu.VMEM((97, 8, 128), F32),
            pltpu.VMEM((512, 64), F32),
        ],
        compiler_params=params(24),
        name="collect",
    )(asked, back, own, mask)
    grad, kept = lax.optimization_barrier((grad, kept))
    share = (kept + sent[0] + sent[1] + sent[2]).reshape(896)[:864] * scale
    return activated.transpose(0, 2, 1)[None], grad.transpose(0, 2, 1)[None], share


def solution(mesh):
    big = P("scene", "brick", None, None)
    flat = P("scene", "brick", None)
    return jax.shard_map(
        on_device,
        mesh=mesh,
        in_specs=(big, flat, P(), P(), big, big, flat, flat),
        out_specs=(big, big, P(("scene", "brick"))),
        check_vma=False,
    )
```

```python
import math

import jax
import jax.numpy as jnp
import numpy as np
from jax import lax
from jax.experimental import pallas as pl
from jax.experimental.pallas import tpu as pltpu
from jax.sharding import PartitionSpec as P

OFFSETS = [(a, b, c) for a in (-1, 0, 1) for b in (-1, 0, 1) for c in (-1, 0, 1) if (a, b, c) != (0, 0, 0)]
KIND = [sum(1 for v in o if v != 0) - 1 for o in OFFSETS]
ORDINAL = [KIND[:k].count(KIND[k]) for k in range(26)]
PER_KIND = (6, 12, 8)
FIRST = (0, 2, 5)
F32, BF16 = jnp.float32, jnp.bfloat16


def source_coord(step):
    return 0 if step == 1 else 7


def target_coord(step):
    return 9 if step == 1 else 0


def half_of(shape):
    return lax.broadcasted_iota(jnp.int32, shape, len(shape) - 1) >= 64


def swap(v):
    return pltpu.roll(v, 64, axis=v.ndim - 1)


def split_halves(v, low):
    top = v.astype(BF16).astype(F32)
    return jnp.where(low, top, v - top).astype(BF16)


def masked_rows(x_ref, m_ref, p):
    return (x_ref[p] * m_ref[p].astype(F32)).T


def tables_kernel(x_ref, m_ref, face_ref, edge_ref, corner_ref, row_ref, rows):
    for p in range(x_ref.shape[0]):
        x = masked_rows(x_ref, m_ref, p)
        x = jnp.concatenate([x, x], axis=1)
        rows[...] = x
        row_ref[p] = x
        for k, (a, b, c) in enumerate(OFFSETS):
            n = ORDINAL[k]
            x0, y0, z0 = source_coord(a), source_coord(b), source_coord(c)
            if KIND[k] == 0:
                for i in range(8):
                    if a:
                        v = rows[x0 * 64 + i * 8:x0 * 64 + i * 8 + 8, :]
                    elif b:
                        v = rows[i * 64 + y0 * 8:i * 64 + y0 * 8 + 8, :]
                    else:
                        v = rows[pl.ds(i * 64 + z0, 8, stride=8), :]
                    face_ref[p * 6 + n, i * 8:i * 8 + 8, :] = v
            elif KIND[k] == 1:
                if not c:
                    v = rows[x0 * 64 + y0 * 8:x0 * 64 + y0 * 8 + 8, :]
                elif not b:
                    v = rows[pl.ds(x0 * 64 + z0, 8, stride=8), :]
                else:
                    v = rows[pl.ds(y0 * 8 + z0, 8, stride=64), :]
                edge_ref[p * 12 + n] = v
            else:
                r = x0 * 64 + y0 * 8 + z0
                corner_ref[p * 8 + n] = jnp.broadcast_to(rows[r:r + 1, :], (8, 128))


def pack_kernel(want_ref, face_ref, edge_ref, corner_ref, out_ref):
    high = half_of((64, 128))
    high8 = half_of((8, 128))
    row0 = lax.broadcasted_iota(jnp.int32, (8, 128), 0) == 0

    def body(p, carry):
        q = [jnp.maximum(want_ref[p, j], 0) for j in range(7)]
        out_ref[p, 0:64, :] = jnp.where(high, face_ref[q[1]], face_ref[q[0]])
        out_ref[p, 64:72, :] = jnp.where(high8, edge_ref[q[3]], edge_ref[q[2]])
        corners = jnp.where(row0, corner_ref[q[5]], corner_ref[q[6]])
        out_ref[p, 72:80, :] = jnp.where(high8, corners, edge_ref[q[4]])
        return carry

    lax.fori_loop(0, 64, body, 0)


def placed(v, other):
    return jnp.where(other, v, swap(v))


def shifted(v, l, row):
    if l == 1:
        return v
    turned = pltpu.roll(v, 1 if l == 0 else 7, axis=0)
    return jnp.where(row == (0 if l == 0 else 7), 0.0, turned)


def weights_kernel(w_ref, f_ref, b_ref):
    zero = jnp.zeros((64, 64), F32)

    def fill(out_ref, s, sides):
        c = jnp.concatenate(sides, axis=1)
        top = c.astype(BF16)
        low = (c - top.astype(F32)).astype(BF16)
        v = jnp.concatenate([top, low], axis=1)
        out_ref[s * 128:s * 128 + 128, :] = jnp.concatenate([v, v], axis=0)

    for j in range(3):
        for l in range(3):
            w = [w_ref[i * 9 + j * 3 + l] for i in range(3)]
            t = [w_ref[(2 - i) * 9 + (2 - j) * 3 + 2 - l].T for i in range(3)]
            for i in range(4):
                s = i * 9 + j * 3 + l
                fill(f_ref, s, [w[i] if i < 3 else zero, w[i - 1] if i else zero])
                fill(b_ref, s, [t[i] if i < 3 else zero, t[i - 1] if i else zero])


def convolve(a_ref, w_ref):
    slices = [(i, j, l) for i in range(4) for j in range(3) for l in range(3)]
    acc = None
    for s in range(0, 36, 4):
        parts = [a_ref[l, 0, i % 2, i // 2:i // 2 + 4, j:j + 8].reshape(512, 128) for i, j, l in slices[s:s + 4]]
        lhs = jnp.concatenate(parts, axis=1)
        d = jnp.dot(lhs, w_ref[s * 128:s * 128 + 512, :], preferred_element_type=F32)
        acc = d if acc is None else acc + d
    return (acc[:, :128] + acc[:, 128:]).reshape(4, 8, 16, 128)


def clear_border(a_ref):
    spare = jnp.zeros((16, 128), BF16)
    for l in range(3):
        for x in range(10):
            for y in range(10):
                if x in (0, 9) or y in (0, 9):
                    a_ref[l, 0, x % 2, x // 2, y] = spare


def own_forward_kernel(x_ref, m_ref, cot_ref, w_ref, bias_ref, pre_ref, cotm_ref, a_ref):
    clear_border(a_ref)
    row = lax.broadcasted_iota(jnp.int32, (8, 128), 0)
    low = jnp.logical_not(half_of((16, 128)))
    for x in range(8):
        for y in range(8):
            r = x * 64 + y * 8
            for l in range(3):
                v = jnp.concatenate([shifted(x_ref[b, r:r + 8, :], l, row) for b in range(2)], axis=0)
                a_ref[l, 0, (x + 1) % 2, (x + 1) // 2, y + 1] = split_halves(v, low)
    pre = convolve(a_ref, w_ref) + bias_ref[...]
    for b in range(2):
        pre_ref[b] = pre[:, :, b * 8:b * 8 + 8]
        c = masked_rows(cot_ref, m_ref, b).reshape(4, 2, 8, 8, 64)
        cotm_ref[b] = jnp.concatenate([c[:, 0], c[:, 1]], axis=-1)


def own_backward_kernel(d_ref, act_ref, m_ref, w_ref, own_ref, out_ref, a_ref):
    @pl.when(pl.program_id(0) == 0)
    def _():
        a_ref[...] = jnp.zeros_like(a_ref)

    row = lax.broadcasted_iota(jnp.int32, (8, 128), 0)
    half = half_of((8, 128))
    low = jnp.logical_not(half_of((16, 128)))
    for x in range(8):
        for y in range(8):
            cols = []
            for b in range(2):
                cols.append(placed(d_ref[b, x // 2, y], half if x % 2 else jnp.logical_not(half)))
            for l in range(3):
                v = jnp.concatenate([shifted(cols[b], l, row) for b in range(2)], axis=0)
                a_ref[l, 0, (x + 1) % 2, (x + 1) // 2, y + 1] = split_halves(v, low)
    out = convolve(a_ref, w_ref)
    for b in range(2):
        own_ref[b, :, 0] = out[:, :, b * 8:b * 8 + 8, :64]
        own_ref[b, :, 1] = out[:, :, b * 8:b * 8 + 8, 64:]
        mask = m_ref[b].astype(F32)
        for h in range(2):
            t = act_ref[b, 2 * h:2 * h + 2].reshape(128, 128).T
            v = jnp.concatenate([t[:64, :64], t[64:, :64], t[:64, 64:], t[64:, 64:]], axis=1)
            a = slice(h * 256, h * 256 + 256)
            out_ref[b, :, a] = v * mask[:, a]


def rest_kernel(d_ref, act_ref, m_ref, w_ref, own_held, out_held, own_ref, out_ref, a_ref):
    own_backward_kernel(d_ref, act_ref, m_ref, w_ref, own_ref, out_ref, a_ref)


def unpack_code(code_ref, b, k):
    c = code_ref[b * 26 + k]
    return c >> 4, (c >> 1) & 7, c & 1


def edge_rows(pos):
    e = pos - 2
    return pl.ds(pl.multiple_of(64 + 8 * (e >> 1), 8), 8), e & 1


def halo_kernel(code_ref, recv_ref, own_hbm, cot_hbm, wf_hbm, wb_hbm,
                act_hbm, dpre_hbm, send_ref, px_hbm, py_hbm, pz_hbm,
                pre, cot_ref, wf_ref, wb_ref, act_ref, dpre_ref, px, py, pz,
                zf, qx, qy, qz, rx, ry, rz, tmp, sems):
    arriving = [pltpu.make_async_copy(a, b, sems.at[n]) for n, (a, b) in enumerate(
        [(own_hbm, pre), (wf_hbm, wf_ref), (cot_hbm, cot_ref), (wb_hbm, wb_ref)])]
    leaving = [pltpu.make_async_copy(a, b, sems.at[4 + n]) for n, (a, b) in enumerate(
        [(px, px_hbm), (py, py_hbm), (pz, pz_hbm), (act_ref, act_hbm), (dpre_ref, dpre_hbm)])]
    for c in arriving:
        c.start()
    high8 = half_of((8, 128))
    half8 = high8.astype(jnp.int32)
    row = lax.broadcasted_iota(jnp.int32, (8, 128), 0)
    low = jnp.logical_not(half_of((16, 128)))
    spare = jnp.zeros((16, 128), BF16)

    def zrow(s, x, y, b):
        return ((s * 10 + x) * 10 + y) * 16 + b

    for s in range(2):
        for l in range(3):
            for g in range(6):
                py[s, l, 0, 0, g] = spare
                py[s, l, 1, 4, g] = spare
        for x in range(10):
            for y in range(10):
                r = zrow(s, x, y, 8)
                zf[r:r + 8, :] = jnp.zeros((8, 128), F32)

    def face(k, b, i):
        o, pos, alive = unpack_code(code_ref, b, k)
        v = recv_ref[o, i * 8:i * 8 + 8, :]
        return placed(v, half8 == pos) * alive.astype(F32)

    def edge(k, b):
        o, pos, alive = unpack_code(code_ref, b, k)
        rows, h = edge_rows(pos)
        return placed(recv_ref[o, rows, :], half8 == h) * alive.astype(F32)

    for k, (dx, dy, dz) in enumerate(OFFSETS):
        xt, yt = target_coord(dx), target_coord(dy)
        sx, sy, sz = int(dx == 1), int(dy == 1), int(dz == 1)
        for g in range(6):
            pair = (2 * g, 2 * g + 1)
            if KIND[k] == 0 and not dz:
                for i in range(8):
                    v = [face(k, b, i) for b in pair]
                    for l in range(3):
                        w = split_halves(jnp.concatenate([shifted(u, l, row) for u in v], axis=0), low)
                        if dx:
                            px[sx, l, i + 1, g] = w
                        else:
                            py[sy, l, (i + 1) % 2, (i + 1) // 2, g] = w
            elif KIND[k] == 1 and not dz:
                v = [edge(k, b) for b in pair]
                for l in range(3):
                    px[sx, l, yt, g] = split_halves(jnp.concatenate([shifted(u, l, row) for u in v], axis=0), low)
            else:
                for b in pair:
                    if KIND[k] == 0:
                        for i in range(8):
                            zf[pl.ds(zrow(sz, i + 1, 1, b), 8, stride=16), :] = face(k, b, i)
                    elif KIND[k] == 1 and dx:
                        zf[pl.ds(zrow(sz, xt, 1, b), 8, stride=16), :] = edge(k, b)
                    elif KIND[k] == 1:
                        zf[pl.ds(zrow(sz, 1, yt, b), 8, stride=160), :] = edge(k, b)
                    else:
                        o, pos, alive = unpack_code(code_ref, b, k)
                        v = recv_ref[o, 72:80, :]
                        v = jnp.where(pos == 5, v[0:1, :], v[1:2, :])
                        r = zrow(sz, xt, yt, b)
                        zf[r:r + 1, :] = placed(v, high8[0:1]) * alive.astype(F32)
    for s in range(2):
        for x in range(10):
            for y in range(10):
                r = zrow(s, x, y, 0)
                pz[s, x % 2, x // 2, y] = split_halves(zf[r:r + 16, :], low)

    def side_x(src, s, ii, ys, w_ref):
        parts = [src[s, l, j:j + ys].reshape(ys * 96, 128) for j in range(3) for l in range(3)]
        v = jnp.dot(jnp.concatenate(parts, axis=1), w_ref[ii * 1152:ii * 1152 + 1152, :], preferred_element_type=F32)
        return v[:, :128] + v[:, 128:]

    def side_y(src, s, j, w_ref):
        acc = None
        for h in range(2):
            parts = [src[s, l, i, h:h + 4].reshape(384, 128) for i in range(2) for l in range(3)]
            at = [((2 * h + i) * 9 + j * 3) * 128 for i in range(2)]
            w = jnp.concatenate([w_ref[a:a + 384, :] for a in at], axis=0)
            v = jnp.dot(jnp.concatenate(parts, axis=1), w, preferred_element_type=F32)
            acc = v if acc is None else acc + v
        return acc[:, :128] + acc[:, 128:]

    def side_z(src, s, l, xs, ys, w_ref):
        slices = [(i, j) for i in range(4) for j in range(3)]
        acc = None
        for n in range(0, 12, 4):
            parts = [src[s, i % 2, i // 2:i // 2 + xs, j:j + ys].reshape(xs * ys * 16, 128) for i, j in slices[n:n + 4]]
            at = [(i * 9 + j * 3 + l) * 128 for i, j in slices[n:n + 4]]
            w = jnp.concatenate([w_ref[a:a + 128, :] for a in at], axis=0)
            v = jnp.dot(jnp.concatenate(parts, axis=1), w, preferred_element_type=F32)
            acc = v if acc is None else acc + v
        return acc[:, :128] + acc[:, 128:]

    def prow(b, xh, y, z):
        return ((b * 4 + xh) * 8 + y) * 8 + z

    for c in leaving[:3]:
        c.start()
    arriving[0].wait()
    arriving[1].wait()
    for s in range(2):
        v = side_x(px, s, 3 * s, 8, wf_ref)
        for y in range(8):
            for b in range(12):
                r, q = prow(b, 3 * s, y, 0), (y * 12 + b) * 8
                pre[r:r + 8, :] += v[q:q + 8]
        v = side_y(py, s, 2 * s, wf_ref)
        for xh in range(4):
            for b in range(12):
                r, q = prow(b, xh, 7 * s, 0), (xh * 12 + b) * 8
                pre[r:r + 8, :] += v[q:q + 8]
        v = side_z(pz, s, 2 * s, 4, 8, wf_ref)
        for xh in range(4):
            for y in range(8):
                q = (xh * 8 + y) * 16
                a = pl.ds(prow(0, xh, y, 7 * s), 8, stride=256)
                pre[a, :] = pre[a, :] + v[q:q + 8]
                a = pl.ds(prow(8, xh, y, 7 * s), 4, stride=256)
                pre[a, :] = pre[a, :] + v[q + 8:q + 12]

    def activate(n, carry):
        a = pl.ds(pl.multiple_of(n * 128, 128), 128)
        p = pre[a, :]
        sig = jax.nn.sigmoid(p)
        ps = p * sig
        act_ref[a, :] = ps
        dpre_ref[a, :] = cot_ref[a, :] * (sig + ps * (1.0 - sig))
        return carry

    arriving[2].wait()
    lax.fori_loop(0, 24, activate, 0)
    leaving[3].start()
    leaving[4].start()

    for s in range(2):
        for l in range(3):
            for g in range(6):
                for y in (0, 1, 10, 11):
                    qx[s, l, y, g] = spare
                qy[s, l, 0, 0, g] = spare
                qy[s, l, 1, 4, g] = spare
    qz[...] = jnp.zeros_like(qz)
    wanted = [jnp.logical_not(high8), high8]
    wanted16 = [low, jnp.logical_not(low)]
    for s in range(2):
        for g in range(6):
            for y in range(8):
                v = []
                for b in (2 * g, 2 * g + 1):
                    r = prow(b, 3 * s, y, 0)
                    v.append(placed(dpre_ref[r:r + 8, :], wanted[s]))
                for l in range(3):
                    qx[s, l, y + 2, g] = split_halves(jnp.concatenate([shifted(u, l, row) for u in v], axis=0), low)
            for x in range(8):
                v = []
                for b in (2 * g, 2 * g + 1):
                    r = prow(b, x // 2, 7 * s, 0)
                    v.append(placed(dpre_ref[r:r + 8, :], wanted[x % 2]))
                for l in range(3):
                    w = split_halves(jnp.concatenate([shifted(u, l, row) for u in v], axis=0), low)
                    qy[s, l, (x + 1) % 2, (x + 1) // 2, g] = w
        for xh in range(4):
            for y in range(8):
                first = dpre_ref[pl.ds(prow(0, xh, y, 7 * s), 8, stride=256), :]
                last = dpre_ref[pl.ds(prow(8, xh, y, 7 * s), 4, stride=256), :]
                v = jnp.concatenate([first, last, jnp.zeros((4, 128), F32)], axis=0)
                for p in range(2):
                    qz[s, p, xh + 1, y + 2] = split_halves(placed(v, wanted16[p]), low)
    arriving[3].wait()
    for s in range(2):
        rx[s] = side_x(qx, s, 3 - 3 * s, 10, wb_ref)
        ry[s] = side_y(qy, s, 2 - 2 * s, wb_ref)
        rz[s * 800:s * 800 + 800, :] = side_z(qz, s, 2 - 2 * s, 5, 10, wb_ref)

    def rzrow(s, xh, y, b):
        return s * 800 + (xh * 10 + y) * 16 + b

    send_ref[...] = jnp.zeros_like(send_ref)
    for b in range(12):
        for k, (dx, dy, dz) in enumerate(OFFSETS):
            o, pos, _ = unpack_code(code_ref, b, k)
            xt, yt = target_coord(dx), target_coord(dy)
            sx, sy, sz = int(dx == 1), int(dy == 1), int(dz == 1)
            if KIND[k] == 0:
                for i in range(8):
                    if dx:
                        r, par = ((i + 1) * 12 + b) * 8, 1 - sx
                        v = rx[sx, r:r + 8, :]
                    elif dy:
                        r, par = ((i // 2) * 12 + b) * 8, i % 2
                        v = ry[sy, r:r + 8, :]
                    else:
                        par = (i + 1) % 2
                        v = rz[pl.ds(rzrow(sz, (i + 1) // 2, 1, b), 8, stride=16), :]
                    v = placed(v, wanted[par])
                    a = slice(i * 8, i * 8 + 8)
                    send_ref[o, a, :] = jnp.where(half8 == pos, v, send_ref[o, a, :])
            elif KIND[k] == 1:
                if not dz:
                    r = (yt * 12 + b) * 8
                    v = placed(rx[sx, r:r + 8, :], wanted[1 - sx])
                elif dx:
                    v = placed(rz[pl.ds(rzrow(sz, xt // 2, 1, b), 8, stride=16), :], wanted[xt % 2])
                else:
                    for q in range(2):
                        tmp[pl.ds(q, 4, stride=2), :] = rz[pl.ds(rzrow(sz, q, yt, b), 4, stride=160), :]
                    v = placed(tmp[...], half8 == 1 - (row & 1))
                a, h = edge_rows(pos)
                send_ref[o, a, :] = jnp.where(half8 == h, v, send_ref[o, a, :])
            else:
                r = rzrow(sz, xt // 2, yt, b)
                v = placed(jnp.broadcast_to(rz[r:r + 1, :], (8, 128)), wanted[xt % 2])
                spot = jnp.logical_and(row == pos - 5, high8)
                send_ref[o, 72:80, :] = jnp.where(spot, v, send_ref[o, 72:80, :])
    for c in leaving:
        c.wait()


def turned_terms(out_ref, at, v):
    t = v.T
    n = t.shape[1]
    top = t.astype(BF16)
    out_ref[0:128, at:at + n] = top
    out_ref[128:256, at:at + n] = (t - top.astype(F32)).astype(BF16)


def kernel_grad_kernel(a_ref, px_ref, py_ref, pz_ref, d_ref, out_ref, dt, dx, dy, dz, sums):
    l = pl.program_id(0)

    @pl.when(l == 0)
    def _():
        for g in range(6):
            v = jnp.concatenate([d_ref[2 * g], d_ref[2 * g + 1]], axis=2)
            turned_terms(dt, g * 512, v.reshape(512, 128))
        flat = d_ref.reshape(3072, 128)
        for s in range(2):
            for y in range(8):
                v = jnp.concatenate([d_ref[b, 3 * s, y] for b in range(12)], axis=0)
                if y % 4 == 0:
                    held = []
                held.append(v)
                if y % 4 == 3:
                    turned_terms(dx.at[s], (y - 3) * 96, jnp.concatenate(held, axis=0))
            v = [d_ref[b, xh, 7 * s] for xh in range(4) for b in range(12)]
            turned_terms(dy.at[s], 0, jnp.concatenate(v, axis=0))
            v = []
            for n in range(32):
                r = n * 8 + 7 * s
                v.append(flat[pl.ds(r, 8, stride=256), :])
                v.append(flat[pl.ds(r + 2048, 4, stride=256), :])
                v.append(jnp.zeros((4, 128), F32))
            turned_terms(dz.at[s], 0, jnp.concatenate(v, axis=0))

    def product(d, parts):
        s = jnp.dot(d, jnp.concatenate(parts, axis=1), preferred_element_type=F32)
        s = s[:128] + s[128:]
        out = []
        for q in range(len(parts)):
            v = s[:, q * 128:q * 128 + 128]
            out.append((v + swap(v))[:, :64])
        return out

    for j in range(3):
        for h in range(2):
            parts = [a_ref[0, :, q, h:h + 4, j:j + 8].reshape(3072, 128) for q in range(2)]
            for q, v in enumerate(product(dt[...], parts)):
                sums[j, 2 * h + q] = v
    for s in range(2):
        parts = [px_ref[s, 0, j:j + 8].reshape(768, 128) for j in range(3)]
        for j, v in enumerate(product(dx[s], parts)):
            sums[j, 3 * s] += v
        parts = [py_ref[s, 0, i % 2, i // 2:i // 2 + 4].reshape(384, 128) for i in range(4)]
        for i, v in enumerate(product(dy[s], parts)):
            sums[2 * s, i] += v

    @pl.when(l != 1)
    def _():
        s = l // 2
        for j in range(3):
            parts = [pz_ref[s, i % 2, i // 2:i // 2 + 4, j:j + 8].reshape(512, 128) for i in range(4)]
            for i, v in enumerate(product(dz[s], parts)):
                sums[j, i] += v

    for i in range(3):
        for j in range(3):
            out_ref[i, j, 0] = (sums[j, i, 0:64] + sums[j, i + 1, 64:128]).T


def collect_kernel(want_ref, back_ref, own_ref, m_ref, out_ref, faces, edges, corners, rows):
    g = pl.program_id(0)
    high = half_of((64, 128))
    high8 = half_of((8, 128))
    rowi = lax.broadcasted_iota(jnp.int32, (8, 128), 0)

    @pl.when(g == 0)
    def _():
        faces[...] = jnp.zeros_like(faces)
        edges[...] = jnp.zeros_like(edges)
        corners[...] = jnp.zeros_like(corners)

        def index(p, j, spare):
            q = want_ref[p, j]
            return jnp.where(q < 0, spare, q)

        def body(p, carry):
            v = back_ref[p, 0:64, :]
            faces[index(p, 0, 72)] += jnp.where(high, 0.0, v)
            faces[index(p, 1, 72)] += jnp.where(high, v, 0.0)
            v = back_ref[p, 64:72, :]
            edges[index(p, 2, 144)] += jnp.where(high8, 0.0, v)
            edges[index(p, 3, 144)] += jnp.where(high8, v, 0.0)
            v = back_ref[p, 72:80, :]
            edges[index(p, 4, 144)] += jnp.where(high8, 0.0, v)
            v = jnp.where(high8, v, 0.0)
            corners[index(p, 5, 96)] += jnp.where(rowi == 0, v, 0.0)
            corners[index(p, 6, 96)] += jnp.where(rowi == 1, v, 0.0)
            return carry

        lax.fori_loop(0, 64, body, 0)

    def fold(v):
        return (v + swap(v))[:, :64]

    bricks = own_ref.shape[0]
    for p in range(bricks):
        rows[...] = own_ref[p].reshape(512, 64)
        for k, (a, b, c) in enumerate(OFFSETS):
            n = (g * bricks + p) * PER_KIND[KIND[k]] + ORDINAL[k]
            x0, y0, z0 = source_coord(a), source_coord(b), source_coord(c)
            if KIND[k] == 0:
                for i in range(8):
                    v = fold(faces[n, i * 8:i * 8 + 8, :])
                    if a:
                        s = slice(x0 * 64 + i * 8, x0 * 64 + i * 8 + 8)
                    elif b:
                        s = slice(i * 64 + y0 * 8, i * 64 + y0 * 8 + 8)
                    else:
                        s = pl.ds(i * 64 + z0, 8, stride=8)
                    rows[s, :] = rows[s, :] + v
            elif KIND[k] == 1:
                v = fold(edges[n])
                if not c:
                    s = slice(x0 * 64 + y0 * 8, x0 * 64 + y0 * 8 + 8)
                elif not b:
                    s = pl.ds(x0 * 64 + z0, 8, stride=8)
                else:
                    s = pl.ds(y0 * 8 + z0, 8, stride=64)
                rows[s, :] = rows[s, :] + v
            else:
                r = x0 * 64 + y0 * 8 + z0
                v = fold(corners[n])
                rows[r:r + 1, :] = rows[r:r + 1, :] + (v[0:1] + v[1:2])
        out_ref[p] = rows[...].T * m_ref[p].astype(F32)


def swap_scenes(v):
    scene = lax.axis_index("scene")
    mine = lax.dynamic_slice_in_dim(v, scene * 864, 864, 0)
    theirs = lax.dynamic_slice_in_dim(v, (1 - scene) * 864, 864, 0)
    return mine + lax.ppermute(theirs, "scene", [(0, 1), (1, 0)])


def sum_stage(v, stride):
    at = (lax.axis_index("brick") // stride) % 4
    n = v.shape[0] // 4

    def quarter(k):
        return lax.dynamic_slice_in_dim(v, k * n, n, 0)

    sent = [lax.ppermute(quarter(at ^ d), "brick", [(m, m ^ (d * stride)) for m in range(64)]) for d in (1, 2, 3)]
    return quarter(at), sent


def whole(memory=pltpu.VMEM):
    return pl.BlockSpec(memory_space=memory)


def const_block(shape):
    return pl.BlockSpec(shape, lambda g: (0,) * len(shape))


def lead_block(shape):
    return pl.BlockSpec(shape, lambda g: (g,) + (0,) * (len(shape) - 1))


def in_hbm(x):
    return pltpu.with_memory_space_constraint(x, pltpu.HBM)


def hbm_out(shape, kind):
    return pltpu.HBM(shape, kind)


def params(mib):
    return pltpu.CompilerParams(vmem_limit_bytes=mib * 1024 * 1024)


def on_device(features, voxel_mask, weight, bias, cotangent, owner, slot, live):
    x = features[0].transpose(0, 2, 1)
    cot = cotangent[0].transpose(0, 2, 1)
    mask = voxel_mask.reshape(12, 1, 512)

    peer = owner.reshape(312)
    alive = live.reshape(312)
    kinds = jnp.asarray(np.tile(np.array(KIND, np.int32), 12))
    first = jnp.asarray(np.tile(np.array([FIRST[q] for q in KIND], np.int32), 12))
    per = jnp.asarray(np.tile(np.array([PER_KIND[q] for q in KIND], np.int32), 12))
    ordinal = jnp.asarray(np.tile(np.array(ORDINAL, np.int32), 12))
    entry = slot.reshape(312) * per + ordinal
    key = peer * 3 + kinds
    order = jnp.arange(312, dtype=jnp.int32)
    same = jnp.logical_and(key[:, None] == key[None, :], order[:, None] < order[None, :])
    place = first + jnp.sum(same.astype(jnp.int32), axis=0)
    spot = jnp.where(alive > 0, peer * 8 + place, -1)
    hit = spot[None, :] == jnp.arange(512, dtype=jnp.int32)[:, None]
    wanted = jnp.sum(jnp.where(hit, entry[None, :] + 1, 0), axis=1).reshape(64, 8) - 1
    code = (peer * 8 + place) * 2 + alive
    asked = lax.all_to_all(wanted, "brick", split_axis=0, concat_axis=0, tiled=True)

    wf, wb = pl.pallas_call(
        weights_kernel,
        in_specs=[whole()],
        out_specs=[whole(), whole()],
        out_shape=[hbm_out((4608, 256), BF16)] * 2,
        compiler_params=params(16),
        cost_estimate=pl.CostEstimate(flops=0, bytes_accessed=6000000, transcendentals=0),
        name="weights",
    )(weight)

    faces, edges, corners, rows = pl.pallas_call(
        tables_kernel,
        grid=(3,),
        in_specs=[lead_block((4, 64, 512)), lead_block((4, 1, 512))],
        out_specs=[
            lead_block((24, 64, 128)),
            lead_block((48, 8, 128)),
            lead_block((32, 8, 128)),
            lead_block((4, 512, 128)),
        ],
        out_shape=[
            jax.ShapeDtypeStruct((72, 64, 128), F32),
            jax.ShapeDtypeStruct((144, 8, 128), F32),
            jax.ShapeDtypeStruct((96, 8, 128), F32),
            hbm_out((12, 512, 128), F32),
        ],
        scratch_shapes=[pltpu.VMEM((512, 128), F32)],
        compiler_params=params(16),
        name="tables",
    )(x, mask)

    out = pl.pallas_call(
        pack_kernel,
        in_specs=[whole(pltpu.SMEM), whole(), whole(), whole()],
        out_specs=whole(),
        out_shape=jax.ShapeDtypeStruct((64, 80, 128), F32),
        compiler_params=params(16),
        name="pack",
    )(asked, faces, edges, corners)
    recv = lax.all_to_all(out, "brick", split_axis=0, concat_axis=0, tiled=True)

    bias2 = jnp.concatenate([bias, bias]).reshape(1, 128)
    turned_block = lead_block((2, 64, 512))
    turned_shape = jax.ShapeDtypeStruct((12, 64, 512), F32)
    mask_block = lead_block((2, 1, 512))
    brick_block = lead_block((2, 4, 2, 8, 8, 64))
    brick_shape = jax.ShapeDtypeStruct((12, 4, 2, 8, 8, 64), F32)
    packed_block = lead_block((2, 4, 8, 8, 128))
    packed_shape = jax.ShapeDtypeStruct((12, 4, 8, 8, 128), F32)
    own_pre, cot_p, windows = pl.pallas_call(
        own_forward_kernel,
        grid=(6,),
        in_specs=[lead_block((2, 512, 128)), mask_block, turned_block, const_block((4608, 256)), const_block((1, 128))],
        out_specs=[
            packed_block,
            packed_block,
            pl.BlockSpec((3, 1, 2, 5, 10, 16, 128), lambda g: (0, g, 0, 0, 0, 0, 0)),
        ],
        out_shape=[
            hbm_out(packed_shape.shape, F32),
            hbm_out(packed_shape.shape, F32),
            hbm_out((3, 6, 2, 5, 10, 16, 128), BF16),
        ],
        compiler_params=params(24),
        cost_estimate=pl.CostEstimate(flops=2 * 3072 * 4608 * 256, bytes_accessed=15000000, transcendentals=0),
        name="own_forward",
    )(in_hbm(rows), mask, in_hbm(cot), in_hbm(wf), bias2)

    flat = (3072, 128)
    side_x, side_y, side_z = (2, 3, 10, 6, 16, 128), (2, 3, 2, 5, 6, 16, 128), (2, 2, 5, 10, 16, 128)
    held = pl.BlockSpec(memory_space=pl.ANY)
    act, dpre, send, px, py, pz = pl.pallas_call(
        halo_kernel,
        in_specs=[whole(pltpu.SMEM), whole()] + [held] * 4,
        out_specs=[held, held, whole(), held, held, held],
        out_shape=[
            hbm_out(flat, F32),
            hbm_out(flat, F32),
            hbm_out((64, 80, 128), F32),
            hbm_out(side_x, BF16),
            hbm_out(side_y, BF16),
            hbm_out(side_z, BF16),
        ],
        scratch_shapes=[
            pltpu.VMEM(flat, F32),
            pltpu.VMEM(flat, F32),
            pltpu.VMEM((4608, 256), BF16),
            pltpu.VMEM((4608, 256), BF16),
            pltpu.VMEM(flat, F32),
            pltpu.VMEM(flat, F32),
            pltpu.VMEM(side_x, BF16),
            pltpu.VMEM(side_y, BF16),
            pltpu.VMEM(side_z, BF16),
            pltpu.VMEM((3200, 128), F32),
            pltpu.VMEM((2, 3, 12, 6, 16, 128), BF16),
            pltpu.VMEM((2, 3, 2, 5, 6, 16, 128), BF16),
            pltpu.VMEM((2, 2, 6, 12, 16, 128), BF16),
            pltpu.VMEM((2, 960, 128), F32),
            pltpu.VMEM((2, 384, 128), F32),
            pltpu.VMEM((1600, 128), F32),
            pltpu.VMEM((8, 128), F32),
            pltpu.SemaphoreType.DMA((9,)),
        ],
        compiler_params=params(44),
        name="halo",
    )(code, recv, in_hbm(own_pre.reshape(flat)), in_hbm(cot_p.reshape(flat)), in_hbm(wf), in_hbm(wb))
    back = lax.all_to_all(send, "brick", split_axis=0, concat_axis=0, tiled=True)
    act = act.reshape(packed_shape.shape)
    dpre = dpre.reshape(packed_shape.shape)

    z = pl.pallas_call(
        kernel_grad_kernel,
        grid=(3,),
        in_specs=[
            pl.BlockSpec((1, 6, 2, 5, 10, 16, 128), lambda l: (l, 0, 0, 0, 0, 0, 0)),
            pl.BlockSpec((2, 1, 10, 6, 16, 128), lambda l: (0, l, 0, 0, 0, 0)),
            pl.BlockSpec((2, 1, 2, 5, 6, 16, 128), lambda l: (0, l, 0, 0, 0, 0, 0)),
            const_block(side_z),
            const_block(packed_shape.shape),
        ],
        out_specs=pl.BlockSpec((3, 3, 1, 64, 64), lambda l: (0, 0, l, 0, 0)),
        out_shape=jax.ShapeDtypeStruct((3, 3, 3, 64, 64), F32),
        scratch_shapes=[
            pltpu.VMEM((256, 3072), BF16),
            pltpu.VMEM((2, 256, 768), BF16),
            pltpu.VMEM((2, 256, 384), BF16),
            pltpu.VMEM((2, 256, 512), BF16),
            pltpu.VMEM((3, 4, 128, 64), F32),
        ],
        compiler_params=params(40),
        cost_estimate=pl.CostEstimate(flops=0, bytes_accessed=1000, transcendentals=0),
        name="kernel_grad",
    )(in_hbm(windows), in_hbm(px), in_hbm(py), in_hbm(pz), in_hbm(dpre))
    kernel = z.reshape(1728, 64)
    scale = 1.0 / math.sqrt(float(2 * 768 * 512))
    total = swap_scenes(kernel)
    dpre, total = lax.optimization_barrier((dpre, total))
    kept, sent = sum_stage(total, 16)

    def own_backward(body, first, d, extra):
        def block(shape):
            return pl.BlockSpec(shape, lambda g: (g + first,) + (0,) * (len(shape) - 1))

        packed2, brick2, turned2 = block((2, 4, 8, 8, 128)), block((2, 4, 2, 8, 8, 64)), block((2, 64, 512))
        return pl.pallas_call(
            body,
            grid=(3,),
            in_specs=[packed2, packed2, block((2, 1, 512)), const_block((4608, 256))] + [held] * len(extra),
            out_specs=[brick2, turned2],
            out_shape=[hbm_out(brick_shape.shape, F32), hbm_out(turned_shape.shape, F32)],
            scratch_shapes=[pltpu.VMEM((3, 1, 2, 5, 10, 16, 128), BF16)],
            input_output_aliases={4 + n: n for n in range(len(extra))},
            compiler_params=params(24),
            cost_estimate=pl.CostEstimate(flops=0, bytes_accessed=1000, transcendentals=0),
            name="own_backward",
        )(in_hbm(d), in_hbm(act), mask, in_hbm(wb), *extra)

    own, activated = own_backward(own_backward_kernel, 0, dpre, [])
    total = kept + sent[0] + sent[1] + sent[2]
    own, total, activated = lax.optimization_barrier((own, total, activated))
    total = jnp.pad(total.reshape(16, 864), ((0, 0), (0, 32))).reshape(16, 7, 128)
    kept, sent = sum_stage(total, 4)
    own, activated = own_backward(rest_kernel, 3, dpre, [in_hbm(own), in_hbm(activated)])
    own, activated, kept = lax.optimization_barrier((own, activated, kept))
    total = kept + sent[0] + sent[1] + sent[2]
    back, total = lax.optimization_barrier((back, total))
    kept, sent = sum_stage(total, 1)

    grad = pl.pallas_call(
        collect_kernel,
        grid=(4,),
        in_specs=[
            pl.BlockSpec(memory_space=pltpu.SMEM),
            const_block((64, 80, 128)),
            lead_block((3, 4, 2, 8, 8, 64)),
            lead_block((3, 1, 512)),
        ],
        out_specs=lead_block((3, 64, 512)),
        out_shape=turned_shape,
        scratch_shapes=[
            pltpu.VMEM((73, 64, 128), F32),
            pltpu.VMEM((145, 8, 128), F32),
            pltpu.VMEM((97, 8, 128), F32),
            pltpu.VMEM((512, 64), F32),
        ],
        compiler_params=params(24),
        name="collect",
    )(asked, back, in_hbm(own), mask)
    grad, kept = lax.optimization_barrier((grad, kept))
    share = (kept + sent[0] + sent[1] + sent[2]).reshape(896)[:864] * scale
    return activated.transpose(0, 2, 1)[None], grad.transpose(0, 2, 1)[None], share


def solution(mesh):
    big = P("scene", "brick", None, None)
    flat = P("scene", "brick", None)
    return jax.shard_map(
        on_device,
        mesh=mesh,
        in_specs=(big, flat, P(), P(), big, big, flat, flat),
        out_specs=(big, big, P(("scene", "brick"))),
        check_vma=False,
    )
```

```python
import math

import jax
import jax.numpy as jnp
import numpy as np
from jax import lax
from jax.experimental import pallas as pl
from jax.experimental.pallas import tpu as pltpu
from jax.sharding import PartitionSpec as P

OFFSETS = [(a, b, c) for a in (-1, 0, 1) for b in (-1, 0, 1) for c in (-1, 0, 1) if (a, b, c) != (0, 0, 0)]
KIND = [sum(1 for v in o if v != 0) - 1 for o in OFFSETS]
ORDINAL = [KIND[:k].count(KIND[k]) for k in range(26)]
PER_KIND = (6, 12, 8)
FIRST = (0, 2, 5)
F32, BF16 = jnp.float32, jnp.bfloat16


def source_coord(step):
    return 0 if step == 1 else 7


def target_coord(step):
    return 9 if step == 1 else 0


def half_of(shape):
    return lax.broadcasted_iota(jnp.int32, shape, len(shape) - 1) >= 64


def swap(v):
    return pltpu.roll(v, 64, axis=v.ndim - 1)


def split_halves(v, low):
    top = v.astype(BF16).astype(F32)
    return jnp.where(low, top, v - top).astype(BF16)


def masked_rows(x_ref, m_ref, p):
    return (x_ref[p] * m_ref[p].astype(F32)).T


def tables_kernel(x_ref, m_ref, face_ref, edge_ref, corner_ref, row_ref, rows):
    for p in range(x_ref.shape[0]):
        x = masked_rows(x_ref, m_ref, p)
        x = jnp.concatenate([x, x], axis=1)
        rows[...] = x
        row_ref[p] = x
        for k, (a, b, c) in enumerate(OFFSETS):
            n = ORDINAL[k]
            x0, y0, z0 = source_coord(a), source_coord(b), source_coord(c)
            if KIND[k] == 0:
                for i in range(8):
                    if a:
                        v = rows[x0 * 64 + i * 8:x0 * 64 + i * 8 + 8, :]
                    elif b:
                        v = rows[i * 64 + y0 * 8:i * 64 + y0 * 8 + 8, :]
                    else:
                        v = rows[pl.ds(i * 64 + z0, 8, stride=8), :]
                    face_ref[p * 6 + n, i * 8:i * 8 + 8, :] = v
            elif KIND[k] == 1:
                if not c:
                    v = rows[x0 * 64 + y0 * 8:x0 * 64 + y0 * 8 + 8, :]
                elif not b:
                    v = rows[pl.ds(x0 * 64 + z0, 8, stride=8), :]
                else:
                    v = rows[pl.ds(y0 * 8 + z0, 8, stride=64), :]
                edge_ref[p * 12 + n] = v
            else:
                r = x0 * 64 + y0 * 8 + z0
                corner_ref[p * 8 + n] = jnp.broadcast_to(rows[r:r + 1, :], (8, 128))


def pack_kernel(want_ref, face_ref, edge_ref, corner_ref, out_ref):
    high = half_of((64, 128))
    high8 = half_of((8, 128))
    row0 = lax.broadcasted_iota(jnp.int32, (8, 128), 0) == 0

    def body(p, carry):
        q = [jnp.maximum(want_ref[p, j], 0) for j in range(7)]
        out_ref[p, 0:64, :] = jnp.where(high, face_ref[q[1]], face_ref[q[0]])
        out_ref[p, 64:72, :] = jnp.where(high8, edge_ref[q[3]], edge_ref[q[2]])
        corners = jnp.where(row0, corner_ref[q[5]], corner_ref[q[6]])
        out_ref[p, 72:80, :] = jnp.where(high8, corners, edge_ref[q[4]])
        return carry

    lax.fori_loop(0, 64, body, 0)


def placed(v, other):
    return jnp.where(other, v, swap(v))


def shifted(v, l, row):
    if l == 1:
        return v
    turned = pltpu.roll(v, 1 if l == 0 else 7, axis=0)
    return jnp.where(row == (0 if l == 0 else 7), 0.0, turned)


def weights_kernel(w_ref, f_ref, b_ref):
    zero = jnp.zeros((64, 64), F32)

    def fill(out_ref, s, sides):
        c = jnp.concatenate(sides, axis=1)
        top = c.astype(BF16)
        low = (c - top.astype(F32)).astype(BF16)
        v = jnp.concatenate([top, low], axis=1)
        out_ref[s * 128:s * 128 + 128, :] = jnp.concatenate([v, v], axis=0)

    for j in range(3):
        for l in range(3):
            w = [w_ref[i * 9 + j * 3 + l] for i in range(3)]
            t = [w_ref[(2 - i) * 9 + (2 - j) * 3 + 2 - l].T for i in range(3)]
            for i in range(4):
                s = i * 9 + j * 3 + l
                fill(f_ref, s, [w[i] if i < 3 else zero, w[i - 1] if i else zero])
                fill(b_ref, s, [t[i] if i < 3 else zero, t[i - 1] if i else zero])


def convolve(a_ref, w_ref):
    slices = [(i, j, l) for i in range(4) for j in range(3) for l in range(3)]
    acc = None
    for s in range(0, 36, 4):
        parts = [a_ref[l, 0, i % 2, i // 2:i // 2 + 4, j:j + 8].reshape(512, 128) for i, j, l in slices[s:s + 4]]
        lhs = jnp.concatenate(parts, axis=1)
        d = jnp.dot(lhs, w_ref[s * 128:s * 128 + 512, :], preferred_element_type=F32)
        acc = d if acc is None else acc + d
    return (acc[:, :128] + acc[:, 128:]).reshape(4, 8, 16, 128)


def clear_border(a_ref):
    spare = jnp.zeros((16, 128), BF16)
    for l in range(3):
        for x in range(10):
            for y in range(10):
                if x in (0, 9) or y in (0, 9):
                    a_ref[l, 0, x % 2, x // 2, y] = spare


def own_forward_kernel(x_ref, m_ref, cot_ref, w_ref, bias_ref, pre_ref, cotm_ref, a_ref):
    clear_border(a_ref)
    row = lax.broadcasted_iota(jnp.int32, (8, 128), 0)
    low = jnp.logical_not(half_of((16, 128)))
    for x in range(8):
        for y in range(8):
            r = x * 64 + y * 8
            for l in range(3):
                v = jnp.concatenate([shifted(x_ref[b, r:r + 8, :], l, row) for b in range(2)], axis=0)
                a_ref[l, 0, (x + 1) % 2, (x + 1) // 2, y + 1] = split_halves(v, low)
    pre = convolve(a_ref, w_ref) + bias_ref[...]
    for b in range(2):
        pre_ref[b] = pre[:, :, b * 8:b * 8 + 8]
        c = masked_rows(cot_ref, m_ref, b).reshape(4, 2, 8, 8, 64)
        cotm_ref[b] = jnp.concatenate([c[:, 0], c[:, 1]], axis=-1)


def own_backward_kernel(d_ref, w_ref, own_ref, a_ref):
    @pl.when(pl.program_id(0) == 0)
    def _():
        a_ref[...] = jnp.zeros_like(a_ref)

    row = lax.broadcasted_iota(jnp.int32, (8, 128), 0)
    half = half_of((8, 128))
    low = jnp.logical_not(half_of((16, 128)))
    for x in range(8):
        for y in range(8):
            cols = []
            for b in range(2):
                cols.append(placed(d_ref[b, x // 2, y], half if x % 2 else jnp.logical_not(half)))
            for l in range(3):
                v = jnp.concatenate([shifted(cols[b], l, row) for b in range(2)], axis=0)
                a_ref[l, 0, (x + 1) % 2, (x + 1) // 2, y + 1] = split_halves(v, low)
    out = convolve(a_ref, w_ref)
    for b in range(2):
        own_ref[b, :, 0] = out[:, :, b * 8:b * 8 + 8, :64]
        own_ref[b, :, 1] = out[:, :, b * 8:b * 8 + 8, 64:]


def activated_kernel(act_ref, m_ref, out_ref):
    for b in range(2):
        mask = m_ref[b].astype(F32)
        for h in range(2):
            t = act_ref[b, 2 * h:2 * h + 2].reshape(128, 128).T
            v = jnp.concatenate([t[:64, :64], t[64:, :64], t[:64, 64:], t[64:, 64:]], axis=1)
            a = slice(h * 256, h * 256 + 256)
            out_ref[b, :, a] = v * mask[:, a]


def unpack_code(code_ref, b, k):
    c = code_ref[b * 26 + k]
    return c >> 4, (c >> 1) & 7, c & 1


def edge_rows(pos):
    e = pos - 2
    return pl.ds(pl.multiple_of(64 + 8 * (e >> 1), 8), 8), e & 1


def halo_kernel(code_ref, recv_ref, own_hbm, cot_hbm, wf_hbm, wb_hbm,
                act_hbm, dpre_hbm, send_ref, px_hbm, py_hbm, pz_hbm,
                pre, cot_ref, wf_ref, wb_ref, act_ref, dpre_ref, px, py, pz,
                zf, qx, qy, qz, rx, ry, rz, tmp, sems):
    arriving = [pltpu.make_async_copy(a, b, sems.at[n]) for n, (a, b) in enumerate(
        [(own_hbm, pre), (wf_hbm, wf_ref), (cot_hbm, cot_ref), (wb_hbm, wb_ref)])]
    leaving = [pltpu.make_async_copy(a, b, sems.at[4 + n]) for n, (a, b) in enumerate(
        [(px, px_hbm), (py, py_hbm), (pz, pz_hbm), (act_ref, act_hbm), (dpre_ref, dpre_hbm)])]
    for c in arriving:
        c.start()
    high8 = half_of((8, 128))
    half8 = high8.astype(jnp.int32)
    row = lax.broadcasted_iota(jnp.int32, (8, 128), 0)
    low = jnp.logical_not(half_of((16, 128)))
    spare = jnp.zeros((16, 128), BF16)

    def zrow(s, x, y, b):
        return ((s * 10 + x) * 10 + y) * 16 + b

    for s in range(2):
        for l in range(3):
            for g in range(6):
                py[s, l, 0, 0, g] = spare
                py[s, l, 1, 4, g] = spare
        for x in range(10):
            for y in range(10):
                r = zrow(s, x, y, 8)
                zf[r:r + 8, :] = jnp.zeros((8, 128), F32)

    def face(k, b, i):
        o, pos, alive = unpack_code(code_ref, b, k)
        v = recv_ref[o, i * 8:i * 8 + 8, :]
        return placed(v, half8 == pos) * alive.astype(F32)

    def edge(k, b):
        o, pos, alive = unpack_code(code_ref, b, k)
        rows, h = edge_rows(pos)
        return placed(recv_ref[o, rows, :], half8 == h) * alive.astype(F32)

    for k, (dx, dy, dz) in enumerate(OFFSETS):
        xt, yt = target_coord(dx), target_coord(dy)
        sx, sy, sz = int(dx == 1), int(dy == 1), int(dz == 1)
        for g in range(6):
            pair = (2 * g, 2 * g + 1)
            if KIND[k] == 0 and not dz:
                for i in range(8):
                    v = [face(k, b, i) for b in pair]
                    for l in range(3):
                        w = split_halves(jnp.concatenate([shifted(u, l, row) for u in v], axis=0), low)
                        if dx:
                            px[sx, l, i + 1, g] = w
                        else:
                            py[sy, l, (i + 1) % 2, (i + 1) // 2, g] = w
            elif KIND[k] == 1 and not dz:
                v = [edge(k, b) for b in pair]
                for l in range(3):
                    px[sx, l, yt, g] = split_halves(jnp.concatenate([shifted(u, l, row) for u in v], axis=0), low)
            else:
                for b in pair:
                    if KIND[k] == 0:
                        for i in range(8):
                            zf[pl.ds(zrow(sz, i + 1, 1, b), 8, stride=16), :] = face(k, b, i)
                    elif KIND[k] == 1 and dx:
                        zf[pl.ds(zrow(sz, xt, 1, b), 8, stride=16), :] = edge(k, b)
                    elif KIND[k] == 1:
                        zf[pl.ds(zrow(sz, 1, yt, b), 8, stride=160), :] = edge(k, b)
                    else:
                        o, pos, alive = unpack_code(code_ref, b, k)
                        v = recv_ref[o, 72:80, :]
                        v = jnp.where(pos == 5, v[0:1, :], v[1:2, :])
                        r = zrow(sz, xt, yt, b)
                        zf[r:r + 1, :] = placed(v, high8[0:1]) * alive.astype(F32)
    for s in range(2):
        for x in range(10):
            for y in range(10):
                r = zrow(s, x, y, 0)
                pz[s, x % 2, x // 2, y] = split_halves(zf[r:r + 16, :], low)

    def side_x(src, s, ii, ys, w_ref):
        parts = [src[s, l, j:j + ys].reshape(ys * 96, 128) for j in range(3) for l in range(3)]
        v = jnp.dot(jnp.concatenate(parts, axis=1), w_ref[ii * 1152:ii * 1152 + 1152, :], preferred_element_type=F32)
        return v[:, :128] + v[:, 128:]

    def side_y(src, s, j, w_ref):
        acc = None
        for h in range(2):
            parts = [src[s, l, i, h:h + 4].reshape(384, 128) for i in range(2) for l in range(3)]
            at = [((2 * h + i) * 9 + j * 3) * 128 for i in range(2)]
            w = jnp.concatenate([w_ref[a:a + 384, :] for a in at], axis=0)
            v = jnp.dot(jnp.concatenate(parts, axis=1), w, preferred_element_type=F32)
            acc = v if acc is None else acc + v
        return acc[:, :128] + acc[:, 128:]

    def side_z(src, s, l, xs, ys, w_ref):
        slices = [(i, j) for i in range(4) for j in range(3)]
        acc = None
        for n in range(0, 12, 4):
            parts = [src[s, i % 2, i // 2:i // 2 + xs, j:j + ys].reshape(xs * ys * 16, 128) for i, j in slices[n:n + 4]]
            at = [(i * 9 + j * 3 + l) * 128 for i, j in slices[n:n + 4]]
            w = jnp.concatenate([w_ref[a:a + 128, :] for a in at], axis=0)
            v = jnp.dot(jnp.concatenate(parts, axis=1), w, preferred_element_type=F32)
            acc = v if acc is None else acc + v
        return acc[:, :128] + acc[:, 128:]

    def prow(b, xh, y, z):
        return ((b * 4 + xh) * 8 + y) * 8 + z

    for c in leaving[:3]:
        c.start()
    arriving[0].wait()
    arriving[1].wait()
    for s in range(2):
        v = side_x(px, s, 3 * s, 8, wf_ref)
        for y in range(8):
            for b in range(12):
                r, q = prow(b, 3 * s, y, 0), (y * 12 + b) * 8
                pre[r:r + 8, :] += v[q:q + 8]
        v = side_y(py, s, 2 * s, wf_ref)
        for xh in range(4):
            for b in range(12):
                r, q = prow(b, xh, 7 * s, 0), (xh * 12 + b) * 8
                pre[r:r + 8, :] += v[q:q + 8]
        v = side_z(pz, s, 2 * s, 4, 8, wf_ref)
        for xh in range(4):
            for y in range(8):
                q = (xh * 8 + y) * 16
                a = pl.ds(prow(0, xh, y, 7 * s), 8, stride=256)
                pre[a, :] = pre[a, :] + v[q:q + 8]
                a = pl.ds(prow(8, xh, y, 7 * s), 4, stride=256)
                pre[a, :] = pre[a, :] + v[q + 8:q + 12]

    def activate(n, carry):
        a = pl.ds(pl.multiple_of(n * 128, 128), 128)
        p = pre[a, :]
        sig = jax.nn.sigmoid(p)
        ps = p * sig
        act_ref[a, :] = ps
        dpre_ref[a, :] = cot_ref[a, :] * (sig + ps * (1.0 - sig))
        return carry

    arriving[2].wait()
    lax.fori_loop(0, 24, activate, 0)
    leaving[3].start()
    leaving[4].start()

    for s in range(2):
        for l in range(3):
            for g in range(6):
                for y in (0, 1, 10, 11):
                    qx[s, l, y, g] = spare
                qy[s, l, 0, 0, g] = spare
                qy[s, l, 1, 4, g] = spare
    qz[...] = jnp.zeros_like(qz)
    wanted = [jnp.logical_not(high8), high8]
    wanted16 = [low, jnp.logical_not(low)]
    for s in range(2):
        for g in range(6):
            for y in range(8):
                v = []
                for b in (2 * g, 2 * g + 1):
                    r = prow(b, 3 * s, y, 0)
                    v.append(placed(dpre_ref[r:r + 8, :], wanted[s]))
                for l in range(3):
                    qx[s, l, y + 2, g] = split_halves(jnp.concatenate([shifted(u, l, row) for u in v], axis=0), low)
            for x in range(8):
                v = []
                for b in (2 * g, 2 * g + 1):
                    r = prow(b, x // 2, 7 * s, 0)
                    v.append(placed(dpre_ref[r:r + 8, :], wanted[x % 2]))
                for l in range(3):
                    w = split_halves(jnp.concatenate([shifted(u, l, row) for u in v], axis=0), low)
                    qy[s, l, (x + 1) % 2, (x + 1) // 2, g] = w
        for xh in range(4):
            for y in range(8):
                first = dpre_ref[pl.ds(prow(0, xh, y, 7 * s), 8, stride=256), :]
                last = dpre_ref[pl.ds(prow(8, xh, y, 7 * s), 4, stride=256), :]
                v = jnp.concatenate([first, last, jnp.zeros((4, 128), F32)], axis=0)
                for p in range(2):
                    qz[s, p, xh + 1, y + 2] = split_halves(placed(v, wanted16[p]), low)
    arriving[3].wait()
    for s in range(2):
        rx[s] = side_x(qx, s, 3 - 3 * s, 10, wb_ref)
        ry[s] = side_y(qy, s, 2 - 2 * s, wb_ref)
        rz[s * 800:s * 800 + 800, :] = side_z(qz, s, 2 - 2 * s, 5, 10, wb_ref)

    def rzrow(s, xh, y, b):
        return s * 800 + (xh * 10 + y) * 16 + b

    send_ref[...] = jnp.zeros_like(send_ref)
    for b in range(12):
        for k, (dx, dy, dz) in enumerate(OFFSETS):
            o, pos, _ = unpack_code(code_ref, b, k)
            xt, yt = target_coord(dx), target_coord(dy)
            sx, sy, sz = int(dx == 1), int(dy == 1), int(dz == 1)
            if KIND[k] == 0:
                for i in range(8):
                    if dx:
                        r, par = ((i + 1) * 12 + b) * 8, 1 - sx
                        v = rx[sx, r:r + 8, :]
                    elif dy:
                        r, par = ((i // 2) * 12 + b) * 8, i % 2
                        v = ry[sy, r:r + 8, :]
                    else:
                        par = (i + 1) % 2
                        v = rz[pl.ds(rzrow(sz, (i + 1) // 2, 1, b), 8, stride=16), :]
                    v = placed(v, wanted[par])
                    a = slice(i * 8, i * 8 + 8)
                    send_ref[o, a, :] = jnp.where(half8 == pos, v, send_ref[o, a, :])
            elif KIND[k] == 1:
                if not dz:
                    r = (yt * 12 + b) * 8
                    v = placed(rx[sx, r:r + 8, :], wanted[1 - sx])
                elif dx:
                    v = placed(rz[pl.ds(rzrow(sz, xt // 2, 1, b), 8, stride=16), :], wanted[xt % 2])
                else:
                    for q in range(2):
                        tmp[pl.ds(q, 4, stride=2), :] = rz[pl.ds(rzrow(sz, q, yt, b), 4, stride=160), :]
                    v = placed(tmp[...], half8 == 1 - (row & 1))
                a, h = edge_rows(pos)
                send_ref[o, a, :] = jnp.where(half8 == h, v, send_ref[o, a, :])
            else:
                r = rzrow(sz, xt // 2, yt, b)
                v = placed(jnp.broadcast_to(rz[r:r + 1, :], (8, 128)), wanted[xt % 2])
                spot = jnp.logical_and(row == pos - 5, high8)
                send_ref[o, 72:80, :] = jnp.where(spot, v, send_ref[o, 72:80, :])
    for c in leaving:
        c.wait()


def turned_terms(out_ref, at, v):
    t = v.T
    n = t.shape[1]
    top = t.astype(BF16)
    out_ref[0:128, at:at + n] = top
    out_ref[128:256, at:at + n] = (t - top.astype(F32)).astype(BF16)


def kernel_grad_kernel(a_ref, px_ref, py_ref, pz_ref, d_ref, out_ref, dt, dx, dy, dz, sums):
    l = pl.program_id(0)

    @pl.when(l == 0)
    def _():
        for g in range(6):
            v = jnp.concatenate([d_ref[2 * g], d_ref[2 * g + 1]], axis=2)
            turned_terms(dt, g * 512, v.reshape(512, 128))
        flat = d_ref.reshape(3072, 128)
        for s in range(2):
            for y in range(8):
                v = jnp.concatenate([d_ref[b, 3 * s, y] for b in range(12)], axis=0)
                if y % 4 == 0:
                    held = []
                held.append(v)
                if y % 4 == 3:
                    turned_terms(dx.at[s], (y - 3) * 96, jnp.concatenate(held, axis=0))
            v = [d_ref[b, xh, 7 * s] for xh in range(4) for b in range(12)]
            turned_terms(dy.at[s], 0, jnp.concatenate(v, axis=0))
            v = []
            for n in range(32):
                r = n * 8 + 7 * s
                v.append(flat[pl.ds(r, 8, stride=256), :])
                v.append(flat[pl.ds(r + 2048, 4, stride=256), :])
                v.append(jnp.zeros((4, 128), F32))
            turned_terms(dz.at[s], 0, jnp.concatenate(v, axis=0))

    def product(d, parts):
        s = jnp.dot(d, jnp.concatenate(parts, axis=1), preferred_element_type=F32)
        s = s[:128] + s[128:]
        out = []
        for q in range(len(parts)):
            v = s[:, q * 128:q * 128 + 128]
            out.append((v + swap(v))[:, :64])
        return out

    for j in range(3):
        for h in range(2):
            parts = [a_ref[0, :, q, h:h + 4, j:j + 8].reshape(3072, 128) for q in range(2)]
            for q, v in enumerate(product(dt[...], parts)):
                sums[j, 2 * h + q] = v
    for s in range(2):
        parts = [px_ref[s, 0, j:j + 8].reshape(768, 128) for j in range(3)]
        for j, v in enumerate(product(dx[s], parts)):
            sums[j, 3 * s] += v
        parts = [py_ref[s, 0, i % 2, i // 2:i // 2 + 4].reshape(384, 128) for i in range(4)]
        for i, v in enumerate(product(dy[s], parts)):
            sums[2 * s, i] += v

    @pl.when(l != 1)
    def _():
        s = l // 2
        for j in range(3):
            parts = [pz_ref[s, i % 2, i // 2:i // 2 + 4, j:j + 8].reshape(512, 128) for i in range(4)]
            for i, v in enumerate(product(dz[s], parts)):
                sums[j, i] += v

    for i in range(3):
        for j in range(3):
            out_ref[i, j, 0] = (sums[j, i, 0:64] + sums[j, i + 1, 64:128]).T


def collect_kernel(want_ref, back_ref, own_ref, m_ref, out_ref, faces, edges, corners, rows):
    g = pl.program_id(0)
    high = half_of((64, 128))
    high8 = half_of((8, 128))
    rowi = lax.broadcasted_iota(jnp.int32, (8, 128), 0)

    @pl.when(g == 0)
    def _():
        faces[...] = jnp.zeros_like(faces)
        edges[...] = jnp.zeros_like(edges)
        corners[...] = jnp.zeros_like(corners)

        def index(p, j, spare):
            q = want_ref[p, j]
            return jnp.where(q < 0, spare, q)

        def body(p, carry):
            v = back_ref[p, 0:64, :]
            faces[index(p, 0, 72)] += jnp.where(high, 0.0, v)
            faces[index(p, 1, 72)] += jnp.where(high, v, 0.0)
            v = back_ref[p, 64:72, :]
            edges[index(p, 2, 144)] += jnp.where(high8, 0.0, v)
            edges[index(p, 3, 144)] += jnp.where(high8, v, 0.0)
            v = back_ref[p, 72:80, :]
            edges[index(p, 4, 144)] += jnp.where(high8, 0.0, v)
            v = jnp.where(high8, v, 0.0)
            corners[index(p, 5, 96)] += jnp.where(rowi == 0, v, 0.0)
            corners[index(p, 6, 96)] += jnp.where(rowi == 1, v, 0.0)
            return carry

        lax.fori_loop(0, 64, body, 0)

    def fold(v):
        return (v + swap(v))[:, :64]

    bricks = own_ref.shape[0]
    for p in range(bricks):
        rows[...] = own_ref[p].reshape(512, 64)
        for k, (a, b, c) in enumerate(OFFSETS):
            n = (g * bricks + p) * PER_KIND[KIND[k]] + ORDINAL[k]
            x0, y0, z0 = source_coord(a), source_coord(b), source_coord(c)
            if KIND[k] == 0:
                for i in range(8):
                    v = fold(faces[n, i * 8:i * 8 + 8, :])
                    if a:
                        s = slice(x0 * 64 + i * 8, x0 * 64 + i * 8 + 8)
                    elif b:
                        s = slice(i * 64 + y0 * 8, i * 64 + y0 * 8 + 8)
                    else:
                        s = pl.ds(i * 64 + z0, 8, stride=8)
                    rows[s, :] = rows[s, :] + v
            elif KIND[k] == 1:
                v = fold(edges[n])
                if not c:
                    s = slice(x0 * 64 + y0 * 8, x0 * 64 + y0 * 8 + 8)
                elif not b:
                    s = pl.ds(x0 * 64 + z0, 8, stride=8)
                else:
                    s = pl.ds(y0 * 8 + z0, 8, stride=64)
                rows[s, :] = rows[s, :] + v
            else:
                r = x0 * 64 + y0 * 8 + z0
                v = fold(corners[n])
                rows[r:r + 1, :] = rows[r:r + 1, :] + (v[0:1] + v[1:2])
        out_ref[p] = rows[...].T * m_ref[p].astype(F32)


def swap_scenes(v):
    scene = lax.axis_index("scene")
    mine = lax.dynamic_slice_in_dim(v, scene * 864, 864, 0)
    theirs = lax.dynamic_slice_in_dim(v, (1 - scene) * 864, 864, 0)
    return mine + lax.ppermute(theirs, "scene", [(0, 1), (1, 0)])


def sum_stage(v, stride):
    at = (lax.axis_index("brick") // stride) % 4
    n = v.shape[0] // 4

    def quarter(k):
        return lax.dynamic_slice_in_dim(v, k * n, n, 0)

    sent = [lax.ppermute(quarter(at ^ d), "brick", [(m, m ^ (d * stride)) for m in range(64)]) for d in (1, 2, 3)]
    return quarter(at), sent


def whole(memory=pltpu.VMEM):
    return pl.BlockSpec(memory_space=memory)


def const_block(shape):
    return pl.BlockSpec(shape, lambda g: (0,) * len(shape))


def lead_block(shape):
    return pl.BlockSpec(shape, lambda g: (g,) + (0,) * (len(shape) - 1))


def in_hbm(x):
    return pltpu.with_memory_space_constraint(x, pltpu.HBM)


def hbm_out(shape, kind):
    return pltpu.HBM(shape, kind)


def params(mib):
    return pltpu.CompilerParams(vmem_limit_bytes=mib * 1024 * 1024)


def on_device(features, voxel_mask, weight, bias, cotangent, owner, slot, live):
    x = features[0].transpose(0, 2, 1)
    cot = cotangent[0].transpose(0, 2, 1)
    mask = voxel_mask.reshape(12, 1, 512)

    peer = owner.reshape(312)
    alive = live.reshape(312)
    kinds = jnp.asarray(np.tile(np.array(KIND, np.int32), 12))
    first = jnp.asarray(np.tile(np.array([FIRST[q] for q in KIND], np.int32), 12))
    per = jnp.asarray(np.tile(np.array([PER_KIND[q] for q in KIND], np.int32), 12))
    ordinal = jnp.asarray(np.tile(np.array(ORDINAL, np.int32), 12))
    entry = slot.reshape(312) * per + ordinal
    key = peer * 3 + kinds
    order = jnp.arange(312, dtype=jnp.int32)
    same = jnp.logical_and(key[:, None] == key[None, :], order[:, None] < order[None, :])
    place = first + jnp.sum(same.astype(jnp.int32), axis=0)
    spot = jnp.where(alive > 0, peer * 8 + place, -1)
    hit = spot[None, :] == jnp.arange(512, dtype=jnp.int32)[:, None]
    wanted = jnp.sum(jnp.where(hit, entry[None, :] + 1, 0), axis=1).reshape(64, 8) - 1
    code = (peer * 8 + place) * 2 + alive
    asked = lax.all_to_all(wanted, "brick", split_axis=0, concat_axis=0, tiled=True)

    wf, wb = pl.pallas_call(
        weights_kernel,
        in_specs=[whole()],
        out_specs=[whole(), whole()],
        out_shape=[hbm_out((4608, 256), BF16)] * 2,
        compiler_params=params(16),
        cost_estimate=pl.CostEstimate(flops=0, bytes_accessed=6000000, transcendentals=0),
        name="weights",
    )(weight)

    faces, edges, corners, rows = pl.pallas_call(
        tables_kernel,
        grid=(3,),
        in_specs=[lead_block((4, 64, 512)), lead_block((4, 1, 512))],
        out_specs=[
            lead_block((24, 64, 128)),
            lead_block((48, 8, 128)),
            lead_block((32, 8, 128)),
            lead_block((4, 512, 128)),
        ],
        out_shape=[
            jax.ShapeDtypeStruct((72, 64, 128), F32),
            jax.ShapeDtypeStruct((144, 8, 128), F32),
            jax.ShapeDtypeStruct((96, 8, 128), F32),
            hbm_out((12, 512, 128), F32),
        ],
        scratch_shapes=[pltpu.VMEM((512, 128), F32)],
        compiler_params=params(16),
        name="tables",
    )(x, mask)

    out = pl.pallas_call(
        pack_kernel,
        in_specs=[whole(pltpu.SMEM), whole(), whole(), whole()],
        out_specs=whole(),
        out_shape=jax.ShapeDtypeStruct((64, 80, 128), F32),
        compiler_params=params(16),
        name="pack",
    )(asked, faces, edges, corners)
    recv = lax.all_to_all(out, "brick", split_axis=0, concat_axis=0, tiled=True)

    bias2 = jnp.concatenate([bias, bias]).reshape(1, 128)
    turned_block = lead_block((2, 64, 512))
    turned_shape = jax.ShapeDtypeStruct((12, 64, 512), F32)
    mask_block = lead_block((2, 1, 512))
    brick_block = lead_block((2, 4, 2, 8, 8, 64))
    brick_shape = jax.ShapeDtypeStruct((12, 4, 2, 8, 8, 64), F32)
    packed_block = lead_block((2, 4, 8, 8, 128))
    packed_shape = jax.ShapeDtypeStruct((12, 4, 8, 8, 128), F32)
    own_pre, cot_p, windows = pl.pallas_call(
        own_forward_kernel,
        grid=(6,),
        in_specs=[lead_block((2, 512, 128)), mask_block, turned_block, const_block((4608, 256)), const_block((1, 128))],
        out_specs=[
            packed_block,
            packed_block,
            pl.BlockSpec((3, 1, 2, 5, 10, 16, 128), lambda g: (0, g, 0, 0, 0, 0, 0)),
        ],
        out_shape=[
            hbm_out(packed_shape.shape, F32),
            hbm_out(packed_shape.shape, F32),
            hbm_out((3, 6, 2, 5, 10, 16, 128), BF16),
        ],
        compiler_params=params(24),
        cost_estimate=pl.CostEstimate(flops=2 * 3072 * 4608 * 256, bytes_accessed=15000000, transcendentals=0),
        name="own_forward",
    )(in_hbm(rows), mask, in_hbm(cot), in_hbm(wf), bias2)

    flat = (3072, 128)
    side_x, side_y, side_z = (2, 3, 10, 6, 16, 128), (2, 3, 2, 5, 6, 16, 128), (2, 2, 5, 10, 16, 128)
    held = pl.BlockSpec(memory_space=pl.ANY)
    act, dpre, send, px, py, pz = pl.pallas_call(
        halo_kernel,
        in_specs=[whole(pltpu.SMEM), whole()] + [held] * 4,
        out_specs=[held, held, whole(), held, held, held],
        out_shape=[
            hbm_out(flat, F32),
            hbm_out(flat, F32),
            jax.ShapeDtypeStruct((64, 80, 128), F32),
            hbm_out(side_x, BF16),
            hbm_out(side_y, BF16),
            hbm_out(side_z, BF16),
        ],
        scratch_shapes=[
            pltpu.VMEM(flat, F32),
            pltpu.VMEM(flat, F32),
            pltpu.VMEM((4608, 256), BF16),
            pltpu.VMEM((4608, 256), BF16),
            pltpu.VMEM(flat, F32),
            pltpu.VMEM(flat, F32),
            pltpu.VMEM(side_x, BF16),
            pltpu.VMEM(side_y, BF16),
            pltpu.VMEM(side_z, BF16),
            pltpu.VMEM((3200, 128), F32),
            pltpu.VMEM((2, 3, 12, 6, 16, 128), BF16),
            pltpu.VMEM((2, 3, 2, 5, 6, 16, 128), BF16),
            pltpu.VMEM((2, 2, 6, 12, 16, 128), BF16),
            pltpu.VMEM((2, 960, 128), F32),
            pltpu.VMEM((2, 384, 128), F32),
            pltpu.VMEM((1600, 128), F32),
            pltpu.VMEM((8, 128), F32),
            pltpu.SemaphoreType.DMA((9,)),
        ],
        compiler_params=params(44),
        name="halo",
    )(code, recv, in_hbm(own_pre.reshape(flat)), in_hbm(cot_p.reshape(flat)), in_hbm(wf), in_hbm(wb))
    back = lax.all_to_all(send, "brick", split_axis=0, concat_axis=0, tiled=True)
    act = act.reshape(packed_shape.shape)
    dpre = dpre.reshape(packed_shape.shape)

    z = pl.pallas_call(
        kernel_grad_kernel,
        grid=(3,),
        in_specs=[
            pl.BlockSpec((1, 6, 2, 5, 10, 16, 128), lambda l: (l, 0, 0, 0, 0, 0, 0)),
            pl.BlockSpec((2, 1, 10, 6, 16, 128), lambda l: (0, l, 0, 0, 0, 0)),
            pl.BlockSpec((2, 1, 2, 5, 6, 16, 128), lambda l: (0, l, 0, 0, 0, 0, 0)),
            const_block(side_z),
            const_block(packed_shape.shape),
        ],
        out_specs=pl.BlockSpec((3, 3, 1, 64, 64), lambda l: (0, 0, l, 0, 0)),
        out_shape=jax.ShapeDtypeStruct((3, 3, 3, 64, 64), F32),
        scratch_shapes=[
            pltpu.VMEM((256, 3072), BF16),
            pltpu.VMEM((2, 256, 768), BF16),
            pltpu.VMEM((2, 256, 384), BF16),
            pltpu.VMEM((2, 256, 512), BF16),
            pltpu.VMEM((3, 4, 128, 64), F32),
        ],
        compiler_params=params(40),
        cost_estimate=pl.CostEstimate(flops=0, bytes_accessed=1000, transcendentals=0),
        name="kernel_grad",
    )(in_hbm(windows), in_hbm(px), in_hbm(py), in_hbm(pz), in_hbm(dpre))
    kernel = z.reshape(1728, 64)
    scale = 1.0 / math.sqrt(float(2 * 768 * 512))
    act, kernel = lax.optimization_barrier((act, kernel))
    total = swap_scenes(kernel)
    dpre, total = lax.optimization_barrier((dpre, total))
    kept, sent = sum_stage(total, 16)

    own = pl.pallas_call(
        own_backward_kernel,
        grid=(6,),
        in_specs=[packed_block, const_block((4608, 256))],
        out_specs=brick_block,
        out_shape=brick_shape,
        scratch_shapes=[pltpu.VMEM((3, 1, 2, 5, 10, 16, 128), BF16)],
        compiler_params=params(24),
        cost_estimate=pl.CostEstimate(flops=0, bytes_accessed=1000, transcendentals=0),
        name="own_backward",
    )(in_hbm(dpre), in_hbm(wb))
    activated = pl.pallas_call(
        activated_kernel,
        grid=(6,),
        in_specs=[packed_block, mask_block],
        out_specs=turned_block,
        out_shape=turned_shape,
        compiler_params=params(8),
        cost_estimate=pl.CostEstimate(flops=0, bytes_accessed=1000, transcendentals=0),
        name="activated",
    )(in_hbm(act), mask)

    total = kept + sent[0] + sent[1] + sent[2]
    own, total, activated = lax.optimization_barrier((own, total, activated))
    total = jnp.pad(total.reshape(16, 864), ((0, 0), (0, 32))).reshape(16, 7, 128)
    back, total = lax.optimization_barrier((back, total))
    layers = [[16 * n + m for m in range(16)] for n in range(4)]
    shares = lax.all_to_all(total, "brick", split_axis=0, concat_axis=0, tiled=True, axis_index_groups=layers)

    grad = pl.pallas_call(
        collect_kernel,
        grid=(4,),
        in_specs=[
            pl.BlockSpec(memory_space=pltpu.SMEM),
            const_block((64, 80, 128)),
            lead_block((3, 4, 2, 8, 8, 64)),
            lead_block((3, 1, 512)),
        ],
        out_specs=lead_block((3, 64, 512)),
        out_shape=turned_shape,
        scratch_shapes=[
            pltpu.VMEM((73, 64, 128), F32),
            pltpu.VMEM((145, 8, 128), F32),
            pltpu.VMEM((97, 8, 128), F32),
            pltpu.VMEM((512, 64), F32),
        ],
        compiler_params=params(24),
        name="collect",
    )(asked, back, own, mask)
    share = jnp.sum(shares, axis=0).reshape(896)[:864] * scale
    return activated.transpose(0, 2, 1)[None], grad.transpose(0, 2, 1)[None], share


def solution(mesh):
    big = P("scene", "brick", None, None)
    flat = P("scene", "brick", None)
    return jax.shard_map(
        on_device,
        mesh=mesh,
        in_specs=(big, flat, P(), P(), big, big, flat, flat),
        out_specs=(big, big, P(("scene", "brick"))),
        check_vma=False,
    )
```

```python
import math

import jax
import jax.numpy as jnp
import numpy as np
from jax import lax
from jax.experimental import pallas as pl
from jax.experimental.pallas import tpu as pltpu
from jax.sharding import PartitionSpec as P

OFFSETS = [(a, b, c) for a in (-1, 0, 1) for b in (-1, 0, 1) for c in (-1, 0, 1) if (a, b, c) != (0, 0, 0)]
KIND = [sum(1 for v in o if v != 0) - 1 for o in OFFSETS]
ORDINAL = [KIND[:k].count(KIND[k]) for k in range(26)]
PER_KIND = (6, 12, 8)
FIRST = (0, 2, 5)
F32, BF16 = jnp.float32, jnp.bfloat16


def source_coord(step):
    return 0 if step == 1 else 7


def target_coord(step):
    return 9 if step == 1 else 0


def half_of(shape):
    return lax.broadcasted_iota(jnp.int32, shape, len(shape) - 1) >= 64


def swap(v):
    return pltpu.roll(v, 64, axis=v.ndim - 1)


def split_halves(v, low):
    top = v.astype(BF16).astype(F32)
    return jnp.where(low, top, v - top).astype(BF16)


def masked_rows(x_ref, m_ref, p):
    return (x_ref[p] * m_ref[p].astype(F32)).T


def tables_kernel(x_ref, m_ref, face_ref, edge_ref, corner_ref, row_ref, rows):
    for p in range(x_ref.shape[0]):
        x = masked_rows(x_ref, m_ref, p)
        x = jnp.concatenate([x, x], axis=1)
        rows[...] = x
        row_ref[p] = x
        for k, (a, b, c) in enumerate(OFFSETS):
            n = ORDINAL[k]
            x0, y0, z0 = source_coord(a), source_coord(b), source_coord(c)
            if KIND[k] == 0:
                for i in range(8):
                    if a:
                        v = rows[x0 * 64 + i * 8:x0 * 64 + i * 8 + 8, :]
                    elif b:
                        v = rows[i * 64 + y0 * 8:i * 64 + y0 * 8 + 8, :]
                    else:
                        v = rows[pl.ds(i * 64 + z0, 8, stride=8), :]
                    face_ref[p * 6 + n, i * 8:i * 8 + 8, :] = v
            elif KIND[k] == 1:
                if not c:
                    v = rows[x0 * 64 + y0 * 8:x0 * 64 + y0 * 8 + 8, :]
                elif not b:
                    v = rows[pl.ds(x0 * 64 + z0, 8, stride=8), :]
                else:
                    v = rows[pl.ds(y0 * 8 + z0, 8, stride=64), :]
                edge_ref[p * 12 + n] = v
            else:
                r = x0 * 64 + y0 * 8 + z0
                corner_ref[p * 8 + n] = jnp.broadcast_to(rows[r:r + 1, :], (8, 128))


def pack_kernel(want_ref, face_ref, edge_ref, corner_ref, out_ref):
    high = half_of((64, 128))
    high8 = half_of((8, 128))
    row0 = lax.broadcasted_iota(jnp.int32, (8, 128), 0) == 0

    def body(p, carry):
        q = [jnp.maximum(want_ref[p, j], 0) for j in range(7)]
        out_ref[p, 0:64, :] = jnp.where(high, face_ref[q[1]], face_ref[q[0]])
        out_ref[p, 64:72, :] = jnp.where(high8, edge_ref[q[3]], edge_ref[q[2]])
        corners = jnp.where(row0, corner_ref[q[5]], corner_ref[q[6]])
        out_ref[p, 72:80, :] = jnp.where(high8, corners, edge_ref[q[4]])
        return carry

    lax.fori_loop(0, 64, body, 0)


def placed(v, other):
    return jnp.where(other, v, swap(v))


def shifted(v, l, row):
    if l == 1:
        return v
    turned = pltpu.roll(v, 1 if l == 0 else 7, axis=0)
    return jnp.where(row == (0 if l == 0 else 7), 0.0, turned)


def weights_kernel(w_ref, f_ref, b_ref):
    zero = jnp.zeros((64, 64), F32)

    def fill(out_ref, s, sides):
        c = jnp.concatenate(sides, axis=1)
        top = c.astype(BF16)
        low = (c - top.astype(F32)).astype(BF16)
        v = jnp.concatenate([top, low], axis=1)
        out_ref[s * 128:s * 128 + 128, :] = jnp.concatenate([v, v], axis=0)

    for j in range(3):
        for l in range(3):
            w = [w_ref[i * 9 + j * 3 + l] for i in range(3)]
            t = [w_ref[(2 - i) * 9 + (2 - j) * 3 + 2 - l].T for i in range(3)]
            for i in range(4):
                s = i * 9 + j * 3 + l
                fill(f_ref, s, [w[i] if i < 3 else zero, w[i - 1] if i else zero])
                fill(b_ref, s, [t[i] if i < 3 else zero, t[i - 1] if i else zero])


def convolve(a_ref, w_ref):
    slices = [(i, j, l) for i in range(4) for j in range(3) for l in range(3)]
    acc = None
    for s in range(0, 36, 4):
        parts = [a_ref[l, 0, i % 2, i // 2:i // 2 + 4, j:j + 8].reshape(512, 128) for i, j, l in slices[s:s + 4]]
        lhs = jnp.concatenate(parts, axis=1)
        d = jnp.dot(lhs, w_ref[s * 128:s * 128 + 512, :], preferred_element_type=F32)
        acc = d if acc is None else acc + d
    return (acc[:, :128] + acc[:, 128:]).reshape(4, 8, 16, 128)


def clear_border(a_ref):
    spare = jnp.zeros((16, 128), BF16)
    for l in range(3):
        for x in range(10):
            for y in range(10):
                if x in (0, 9) or y in (0, 9):
                    a_ref[l, 0, x % 2, x // 2, y] = spare


def own_forward_kernel(x_ref, m_ref, cot_ref, w_ref, bias_ref, pre_ref, cotm_ref, a_ref):
    clear_border(a_ref)
    row = lax.broadcasted_iota(jnp.int32, (8, 128), 0)
    low = jnp.logical_not(half_of((16, 128)))
    for x in range(8):
        for y in range(8):
            r = x * 64 + y * 8
            for l in range(3):
                v = jnp.concatenate([shifted(x_ref[b, r:r + 8, :], l, row) for b in range(2)], axis=0)
                a_ref[l, 0, (x + 1) % 2, (x + 1) // 2, y + 1] = split_halves(v, low)
    pre = convolve(a_ref, w_ref) + bias_ref[...]
    for b in range(2):
        pre_ref[b] = pre[:, :, b * 8:b * 8 + 8]
        c = masked_rows(cot_ref, m_ref, b).reshape(4, 2, 8, 8, 64)
        cotm_ref[b] = jnp.concatenate([c[:, 0], c[:, 1]], axis=-1)


def own_backward_kernel(d_ref, act_ref, m_ref, w_ref, own_ref, out_ref, a_ref):
    @pl.when(pl.program_id(0) == 0)
    def _():
        a_ref[...] = jnp.zeros_like(a_ref)

    row = lax.broadcasted_iota(jnp.int32, (8, 128), 0)
    half = half_of((8, 128))
    low = jnp.logical_not(half_of((16, 128)))
    for x in range(8):
        for y in range(8):
            cols = []
            for b in range(2):
                cols.append(placed(d_ref[b, x // 2, y], half if x % 2 else jnp.logical_not(half)))
            for l in range(3):
                v = jnp.concatenate([shifted(cols[b], l, row) for b in range(2)], axis=0)
                a_ref[l, 0, (x + 1) % 2, (x + 1) // 2, y + 1] = split_halves(v, low)
    out = convolve(a_ref, w_ref)
    for b in range(2):
        own_ref[b, :, 0] = out[:, :, b * 8:b * 8 + 8, :64]
        own_ref[b, :, 1] = out[:, :, b * 8:b * 8 + 8, 64:]
        mask = m_ref[b].astype(F32)
        for h in range(2):
            t = act_ref[b, 2 * h:2 * h + 2].reshape(128, 128).T
            v = jnp.concatenate([t[:64, :64], t[64:, :64], t[:64, 64:], t[64:, 64:]], axis=1)
            a = slice(h * 256, h * 256 + 256)
            out_ref[b, :, a] = v * mask[:, a]


def unpack_code(code_ref, b, k):
    c = code_ref[b * 26 + k]
    return c >> 4, (c >> 1) & 7, c & 1


def edge_rows(pos):
    e = pos - 2
    return pl.ds(pl.multiple_of(64 + 8 * (e >> 1), 8), 8), e & 1


def halo_kernel(code_ref, recv_ref, own_hbm, cot_hbm, wf_hbm, wb_hbm,
                act_hbm, dpre_hbm, send_hbm, px_hbm, py_hbm, pz_hbm,
                pre, cot_ref, wf_ref, wb_ref, act_ref, dpre_ref, px, py, pz,
                send_ref, zf, qx, qy, qz, rx, ry, rz, tmp, sems):
    arriving = [pltpu.make_async_copy(a, b, sems.at[n]) for n, (a, b) in enumerate(
        [(own_hbm, pre), (wf_hbm, wf_ref), (cot_hbm, cot_ref), (wb_hbm, wb_ref)])]
    leaving = [pltpu.make_async_copy(a, b, sems.at[4 + n]) for n, (a, b) in enumerate(
        [(px, px_hbm), (py, py_hbm), (pz, pz_hbm), (act_ref, act_hbm), (dpre_ref, dpre_hbm)])]
    faces_out = pltpu.make_async_copy(send_ref.at[:, 0:64], send_hbm.at[:, 0:64], sems.at[9])
    rest_out = pltpu.make_async_copy(send_ref.at[:, 64:80], send_hbm.at[:, 64:80], sems.at[10])
    for c in arriving:
        c.start()
    high8 = half_of((8, 128))
    half8 = high8.astype(jnp.int32)
    row = lax.broadcasted_iota(jnp.int32, (8, 128), 0)
    low = jnp.logical_not(half_of((16, 128)))
    spare = jnp.zeros((16, 128), BF16)

    def zrow(s, x, y, b):
        return ((s * 10 + x) * 10 + y) * 16 + b

    for s in range(2):
        for l in range(3):
            for g in range(6):
                py[s, l, 0, 0, g] = spare
                py[s, l, 1, 4, g] = spare
        for x in range(10):
            for y in range(10):
                r = zrow(s, x, y, 8)
                zf[r:r + 8, :] = jnp.zeros((8, 128), F32)

    def face(k, b, i):
        o, pos, alive = unpack_code(code_ref, b, k)
        v = recv_ref[o, i * 8:i * 8 + 8, :]
        return placed(v, half8 == pos) * alive.astype(F32)

    def edge(k, b):
        o, pos, alive = unpack_code(code_ref, b, k)
        rows, h = edge_rows(pos)
        return placed(recv_ref[o, rows, :], half8 == h) * alive.astype(F32)

    for k, (dx, dy, dz) in enumerate(OFFSETS):
        xt, yt = target_coord(dx), target_coord(dy)
        sx, sy, sz = int(dx == 1), int(dy == 1), int(dz == 1)
        for g in range(6):
            pair = (2 * g, 2 * g + 1)
            if KIND[k] == 0 and not dz:
                for i in range(8):
                    v = [face(k, b, i) for b in pair]
                    for l in range(3):
                        w = split_halves(jnp.concatenate([shifted(u, l, row) for u in v], axis=0), low)
                        if dx:
                            px[sx, l, i + 1, g] = w
                        else:
                            py[sy, l, (i + 1) % 2, (i + 1) // 2, g] = w
            elif KIND[k] == 1 and not dz:
                v = [edge(k, b) for b in pair]
                for l in range(3):
                    px[sx, l, yt, g] = split_halves(jnp.concatenate([shifted(u, l, row) for u in v], axis=0), low)
            else:
                for b in pair:
                    if KIND[k] == 0:
                        for i in range(8):
                            zf[pl.ds(zrow(sz, i + 1, 1, b), 8, stride=16), :] = face(k, b, i)
                    elif KIND[k] == 1 and dx:
                        zf[pl.ds(zrow(sz, xt, 1, b), 8, stride=16), :] = edge(k, b)
                    elif KIND[k] == 1:
                        zf[pl.ds(zrow(sz, 1, yt, b), 8, stride=160), :] = edge(k, b)
                    else:
                        o, pos, alive = unpack_code(code_ref, b, k)
                        v = recv_ref[o, 72:80, :]
                        v = jnp.where(pos == 5, v[0:1, :], v[1:2, :])
                        r = zrow(sz, xt, yt, b)
                        zf[r:r + 1, :] = placed(v, high8[0:1]) * alive.astype(F32)
    for s in range(2):
        for x in range(10):
            for y in range(10):
                r = zrow(s, x, y, 0)
                pz[s, x % 2, x // 2, y] = split_halves(zf[r:r + 16, :], low)

    def side_x(src, s, ii, ys, w_ref):
        parts = [src[s, l, j:j + ys].reshape(ys * 96, 128) for j in range(3) for l in range(3)]
        v = jnp.dot(jnp.concatenate(parts, axis=1), w_ref[ii * 1152:ii * 1152 + 1152, :], preferred_element_type=F32)
        return v[:, :128] + v[:, 128:]

    def side_y(src, s, j, w_ref):
        acc = None
        for h in range(2):
            parts = [src[s, l, i, h:h + 4].reshape(384, 128) for i in range(2) for l in range(3)]
            at = [((2 * h + i) * 9 + j * 3) * 128 for i in range(2)]
            w = jnp.concatenate([w_ref[a:a + 384, :] for a in at], axis=0)
            v = jnp.dot(jnp.concatenate(parts, axis=1), w, preferred_element_type=F32)
            acc = v if acc is None else acc + v
        return acc[:, :128] + acc[:, 128:]

    def side_z(src, s, l, xs, ys, w_ref):
        slices = [(i, j) for i in range(4) for j in range(3)]
        acc = None
        for n in range(0, 12, 4):
            parts = [src[s, i % 2, i // 2:i // 2 + xs, j:j + ys].reshape(xs * ys * 16, 128) for i, j in slices[n:n + 4]]
            at = [(i * 9 + j * 3 + l) * 128 for i, j in slices[n:n + 4]]
            w = jnp.concatenate([w_ref[a:a + 128, :] for a in at], axis=0)
            v = jnp.dot(jnp.concatenate(parts, axis=1), w, preferred_element_type=F32)
            acc = v if acc is None else acc + v
        return acc[:, :128] + acc[:, 128:]

    def prow(b, xh, y, z):
        return ((b * 4 + xh) * 8 + y) * 8 + z

    for c in leaving[:3]:
        c.start()
    arriving[0].wait()
    arriving[1].wait()
    for s in range(2):
        v = side_x(px, s, 3 * s, 8, wf_ref)
        for y in range(8):
            for b in range(12):
                r, q = prow(b, 3 * s, y, 0), (y * 12 + b) * 8
                pre[r:r + 8, :] += v[q:q + 8]
        v = side_y(py, s, 2 * s, wf_ref)
        for xh in range(4):
            for b in range(12):
                r, q = prow(b, xh, 7 * s, 0), (xh * 12 + b) * 8
                pre[r:r + 8, :] += v[q:q + 8]
        v = side_z(pz, s, 2 * s, 4, 8, wf_ref)
        for xh in range(4):
            for y in range(8):
                q = (xh * 8 + y) * 16
                a = pl.ds(prow(0, xh, y, 7 * s), 8, stride=256)
                pre[a, :] = pre[a, :] + v[q:q + 8]
                a = pl.ds(prow(8, xh, y, 7 * s), 4, stride=256)
                pre[a, :] = pre[a, :] + v[q + 8:q + 12]

    def activate(n, carry):
        a = pl.ds(pl.multiple_of(n * 128, 128), 128)
        p = pre[a, :]
        sig = jax.nn.sigmoid(p)
        ps = p * sig
        act_ref[a, :] = ps
        dpre_ref[a, :] = cot_ref[a, :] * (sig + ps * (1.0 - sig))
        return carry

    arriving[2].wait()
    lax.fori_loop(0, 24, activate, 0)
    leaving[3].start()
    leaving[4].start()

    for s in range(2):
        for l in range(3):
            for g in range(6):
                for y in (0, 1, 10, 11):
                    qx[s, l, y, g] = spare
                qy[s, l, 0, 0, g] = spare
                qy[s, l, 1, 4, g] = spare
    qz[...] = jnp.zeros_like(qz)
    wanted = [jnp.logical_not(high8), high8]
    wanted16 = [low, jnp.logical_not(low)]
    for s in range(2):
        for g in range(6):
            for y in range(8):
                v = []
                for b in (2 * g, 2 * g + 1):
                    r = prow(b, 3 * s, y, 0)
                    v.append(placed(dpre_ref[r:r + 8, :], wanted[s]))
                for l in range(3):
                    qx[s, l, y + 2, g] = split_halves(jnp.concatenate([shifted(u, l, row) for u in v], axis=0), low)
            for x in range(8):
                v = []
                for b in (2 * g, 2 * g + 1):
                    r = prow(b, x // 2, 7 * s, 0)
                    v.append(placed(dpre_ref[r:r + 8, :], wanted[x % 2]))
                for l in range(3):
                    w = split_halves(jnp.concatenate([shifted(u, l, row) for u in v], axis=0), low)
                    qy[s, l, (x + 1) % 2, (x + 1) // 2, g] = w
        for xh in range(4):
            for y in range(8):
                first = dpre_ref[pl.ds(prow(0, xh, y, 7 * s), 8, stride=256), :]
                last = dpre_ref[pl.ds(prow(8, xh, y, 7 * s), 4, stride=256), :]
                v = jnp.concatenate([first, last, jnp.zeros((4, 128), F32)], axis=0)
                for p in range(2):
                    qz[s, p, xh + 1, y + 2] = split_halves(placed(v, wanted16[p]), low)
    arriving[3].wait()
    for s in range(2):
        rx[s] = side_x(qx, s, 3 - 3 * s, 10, wb_ref)
        ry[s] = side_y(qy, s, 2 - 2 * s, wb_ref)
        rz[s * 800:s * 800 + 800, :] = side_z(qz, s, 2 - 2 * s, 5, 10, wb_ref)

    def rzrow(s, xh, y, b):
        return s * 800 + (xh * 10 + y) * 16 + b

    send_ref[...] = jnp.zeros_like(send_ref)
    kinds = [k for k in range(26) if KIND[k] == 0] + [k for k in range(26) if KIND[k]]
    for n, k in enumerate(kinds):
        if n == 6:
            faces_out.start()
        dx, dy, dz = OFFSETS[k]
        for b in range(12):
            o, pos, _ = unpack_code(code_ref, b, k)
            xt, yt = target_coord(dx), target_coord(dy)
            sx, sy, sz = int(dx == 1), int(dy == 1), int(dz == 1)
            if KIND[k] == 0:
                for i in range(8):
                    if dx:
                        r, par = ((i + 1) * 12 + b) * 8, 1 - sx
                        v = rx[sx, r:r + 8, :]
                    elif dy:
                        r, par = ((i // 2) * 12 + b) * 8, i % 2
                        v = ry[sy, r:r + 8, :]
                    else:
                        par = (i + 1) % 2
                        v = rz[pl.ds(rzrow(sz, (i + 1) // 2, 1, b), 8, stride=16), :]
                    v = placed(v, wanted[par])
                    a = slice(i * 8, i * 8 + 8)
                    send_ref[o, a, :] = jnp.where(half8 == pos, v, send_ref[o, a, :])
            elif KIND[k] == 1:
                if not dz:
                    r = (yt * 12 + b) * 8
                    v = placed(rx[sx, r:r + 8, :], wanted[1 - sx])
                elif dx:
                    v = placed(rz[pl.ds(rzrow(sz, xt // 2, 1, b), 8, stride=16), :], wanted[xt % 2])
                else:
                    for q in range(2):
                        tmp[pl.ds(q, 4, stride=2), :] = rz[pl.ds(rzrow(sz, q, yt, b), 4, stride=160), :]
                    v = placed(tmp[...], half8 == 1 - (row & 1))
                a, h = edge_rows(pos)
                send_ref[o, a, :] = jnp.where(half8 == h, v, send_ref[o, a, :])
            else:
                r = rzrow(sz, xt // 2, yt, b)
                v = placed(jnp.broadcast_to(rz[r:r + 1, :], (8, 128)), wanted[xt % 2])
                spot = jnp.logical_and(row == pos - 5, high8)
                send_ref[o, 72:80, :] = jnp.where(spot, v, send_ref[o, 72:80, :])
    rest_out.start()
    for c in leaving + [faces_out, rest_out]:
        c.wait()


def turned_terms(out_ref, at, v):
    t = v.T
    n = t.shape[1]
    top = t.astype(BF16)
    out_ref[0:128, at:at + n] = top
    out_ref[128:256, at:at + n] = (t - top.astype(F32)).astype(BF16)


def kernel_grad_kernel(a_ref, px_ref, py_ref, pz_ref, d_ref, out_ref, dt, dx, dy, dz, sums):
    l = pl.program_id(0)

    @pl.when(l == 0)
    def _():
        for g in range(6):
            v = jnp.concatenate([d_ref[2 * g], d_ref[2 * g + 1]], axis=2)
            turned_terms(dt, g * 512, v.reshape(512, 128))
        flat = d_ref.reshape(3072, 128)
        for s in range(2):
            for y in range(8):
                v = jnp.concatenate([d_ref[b, 3 * s, y] for b in range(12)], axis=0)
                if y % 4 == 0:
                    held = []
                held.append(v)
                if y % 4 == 3:
                    turned_terms(dx.at[s], (y - 3) * 96, jnp.concatenate(held, axis=0))
            v = [d_ref[b, xh, 7 * s] for xh in range(4) for b in range(12)]
            turned_terms(dy.at[s], 0, jnp.concatenate(v, axis=0))
            v = []
            for n in range(32):
                r = n * 8 + 7 * s
                v.append(flat[pl.ds(r, 8, stride=256), :])
                v.append(flat[pl.ds(r + 2048, 4, stride=256), :])
                v.append(jnp.zeros((4, 128), F32))
            turned_terms(dz.at[s], 0, jnp.concatenate(v, axis=0))

    def product(d, parts):
        s = jnp.dot(d, jnp.concatenate(parts, axis=1), preferred_element_type=F32)
        s = s[:128] + s[128:]
        out = []
        for q in range(len(parts)):
            v = s[:, q * 128:q * 128 + 128]
            out.append((v + swap(v))[:, :64])
        return out

    for j in range(3):
        for h in range(2):
            parts = [a_ref[0, :, q, h:h + 4, j:j + 8].reshape(3072, 128) for q in range(2)]
            for q, v in enumerate(product(dt[...], parts)):
                sums[j, 2 * h + q] = v
    for s in range(2):
        parts = [px_ref[s, 0, j:j + 8].reshape(768, 128) for j in range(3)]
        for j, v in enumerate(product(dx[s], parts)):
            sums[j, 3 * s] += v
        parts = [py_ref[s, 0, i % 2, i // 2:i // 2 + 4].reshape(384, 128) for i in range(4)]
        for i, v in enumerate(product(dy[s], parts)):
            sums[2 * s, i] += v

    @pl.when(l != 1)
    def _():
        s = l // 2
        for j in range(3):
            parts = [pz_ref[s, i % 2, i // 2:i // 2 + 4, j:j + 8].reshape(512, 128) for i in range(4)]
            for i, v in enumerate(product(dz[s], parts)):
                sums[j, i] += v

    for i in range(3):
        for j in range(3):
            out_ref[i, j, 0] = (sums[j, i, 0:64] + sums[j, i + 1, 64:128]).T


def collect_kernel(want_ref, back_ref, own_ref, m_ref, out_ref, faces, edges, corners, rows):
    g = pl.program_id(0)
    high = half_of((64, 128))
    high8 = half_of((8, 128))
    rowi = lax.broadcasted_iota(jnp.int32, (8, 128), 0)

    @pl.when(g == 0)
    def _():
        faces[...] = jnp.zeros_like(faces)
        edges[...] = jnp.zeros_like(edges)
        corners[...] = jnp.zeros_like(corners)

        def index(p, j, spare):
            q = want_ref[p, j]
            return jnp.where(q < 0, spare, q)

        def body(p, carry):
            v = back_ref[p, 0:64, :]
            faces[index(p, 0, 72)] += jnp.where(high, 0.0, v)
            faces[index(p, 1, 72)] += jnp.where(high, v, 0.0)
            v = back_ref[p, 64:72, :]
            edges[index(p, 2, 144)] += jnp.where(high8, 0.0, v)
            edges[index(p, 3, 144)] += jnp.where(high8, v, 0.0)
            v = back_ref[p, 72:80, :]
            edges[index(p, 4, 144)] += jnp.where(high8, 0.0, v)
            v = jnp.where(high8, v, 0.0)
            corners[index(p, 5, 96)] += jnp.where(rowi == 0, v, 0.0)
            corners[index(p, 6, 96)] += jnp.where(rowi == 1, v, 0.0)
            return carry

        lax.fori_loop(0, 64, body, 0)

    def fold(v):
        return (v + swap(v))[:, :64]

    bricks = own_ref.shape[0]
    for p in range(bricks):
        rows[...] = own_ref[p].reshape(512, 64)
        for k, (a, b, c) in enumerate(OFFSETS):
            n = (g * bricks + p) * PER_KIND[KIND[k]] + ORDINAL[k]
            x0, y0, z0 = source_coord(a), source_coord(b), source_coord(c)
            if KIND[k] == 0:
                for i in range(8):
                    v = fold(faces[n, i * 8:i * 8 + 8, :])
                    if a:
                        s = slice(x0 * 64 + i * 8, x0 * 64 + i * 8 + 8)
                    elif b:
                        s = slice(i * 64 + y0 * 8, i * 64 + y0 * 8 + 8)
                    else:
                        s = pl.ds(i * 64 + z0, 8, stride=8)
                    rows[s, :] = rows[s, :] + v
            elif KIND[k] == 1:
                v = fold(edges[n])
                if not c:
                    s = slice(x0 * 64 + y0 * 8, x0 * 64 + y0 * 8 + 8)
                elif not b:
                    s = pl.ds(x0 * 64 + z0, 8, stride=8)
                else:
                    s = pl.ds(y0 * 8 + z0, 8, stride=64)
                rows[s, :] = rows[s, :] + v
            else:
                r = x0 * 64 + y0 * 8 + z0
                v = fold(corners[n])
                rows[r:r + 1, :] = rows[r:r + 1, :] + (v[0:1] + v[1:2])
        out_ref[p] = rows[...].T * m_ref[p].astype(F32)


def swap_scenes(v):
    scene = lax.axis_index("scene")
    mine = lax.dynamic_slice_in_dim(v, scene * 864, 864, 0)
    theirs = lax.dynamic_slice_in_dim(v, (1 - scene) * 864, 864, 0)
    return mine + lax.ppermute(theirs, "scene", [(0, 1), (1, 0)])


def sum_stage(v, stride):
    at = (lax.axis_index("brick") // stride) % 4
    n = v.shape[0] // 4

    def quarter(k):
        return lax.dynamic_slice_in_dim(v, k * n, n, 0)

    sent = [lax.ppermute(quarter(at ^ d), "brick", [(m, m ^ (d * stride)) for m in range(64)]) for d in (1, 2, 3)]
    return quarter(at), sent


def whole(memory=pltpu.VMEM):
    return pl.BlockSpec(memory_space=memory)


def const_block(shape):
    return pl.BlockSpec(shape, lambda g: (0,) * len(shape))


def lead_block(shape):
    return pl.BlockSpec(shape, lambda g: (g,) + (0,) * (len(shape) - 1))


def in_hbm(x):
    return pltpu.with_memory_space_constraint(x, pltpu.HBM)


def hbm_out(shape, kind):
    return pltpu.HBM(shape, kind)


def params(mib):
    return pltpu.CompilerParams(vmem_limit_bytes=mib * 1024 * 1024)


def on_device(features, voxel_mask, weight, bias, cotangent, owner, slot, live):
    x = features[0].transpose(0, 2, 1)
    cot = cotangent[0].transpose(0, 2, 1)
    mask = voxel_mask.reshape(12, 1, 512)

    peer = owner.reshape(312)
    alive = live.reshape(312)
    kinds = jnp.asarray(np.tile(np.array(KIND, np.int32), 12))
    first = jnp.asarray(np.tile(np.array([FIRST[q] for q in KIND], np.int32), 12))
    per = jnp.asarray(np.tile(np.array([PER_KIND[q] for q in KIND], np.int32), 12))
    ordinal = jnp.asarray(np.tile(np.array(ORDINAL, np.int32), 12))
    entry = slot.reshape(312) * per + ordinal
    key = peer * 3 + kinds
    order = jnp.arange(312, dtype=jnp.int32)
    same = jnp.logical_and(key[:, None] == key[None, :], order[:, None] < order[None, :])
    place = first + jnp.sum(same.astype(jnp.int32), axis=0)
    spot = jnp.where(alive > 0, peer * 8 + place, -1)
    hit = spot[None, :] == jnp.arange(512, dtype=jnp.int32)[:, None]
    wanted = jnp.sum(jnp.where(hit, entry[None, :] + 1, 0), axis=1).reshape(64, 8) - 1
    code = (peer * 8 + place) * 2 + alive
    asked = lax.all_to_all(wanted, "brick", split_axis=0, concat_axis=0, tiled=True)

    wf, wb = pl.pallas_call(
        weights_kernel,
        in_specs=[whole()],
        out_specs=[whole(), whole()],
        out_shape=[hbm_out((4608, 256), BF16)] * 2,
        compiler_params=params(16),
        cost_estimate=pl.CostEstimate(flops=0, bytes_accessed=6000000, transcendentals=0),
        name="weights",
    )(weight)

    faces, edges, corners, rows = pl.pallas_call(
        tables_kernel,
        grid=(3,),
        in_specs=[lead_block((4, 64, 512)), lead_block((4, 1, 512))],
        out_specs=[
            lead_block((24, 64, 128)),
            lead_block((48, 8, 128)),
            lead_block((32, 8, 128)),
            lead_block((4, 512, 128)),
        ],
        out_shape=[
            jax.ShapeDtypeStruct((72, 64, 128), F32),
            jax.ShapeDtypeStruct((144, 8, 128), F32),
            jax.ShapeDtypeStruct((96, 8, 128), F32),
            hbm_out((12, 512, 128), F32),
        ],
        scratch_shapes=[pltpu.VMEM((512, 128), F32)],
        compiler_params=params(16),
        name="tables",
    )(x, mask)

    out = pl.pallas_call(
        pack_kernel,
        in_specs=[whole(pltpu.SMEM), whole(), whole(), whole()],
        out_specs=whole(),
        out_shape=jax.ShapeDtypeStruct((64, 80, 128), F32),
        compiler_params=params(16),
        name="pack",
    )(asked, faces, edges, corners)
    recv = lax.all_to_all(out, "brick", split_axis=0, concat_axis=0, tiled=True)

    bias2 = jnp.concatenate([bias, bias]).reshape(1, 128)
    turned_block = lead_block((2, 64, 512))
    turned_shape = jax.ShapeDtypeStruct((12, 64, 512), F32)
    mask_block = lead_block((2, 1, 512))
    brick_block = lead_block((2, 4, 2, 8, 8, 64))
    brick_shape = jax.ShapeDtypeStruct((12, 4, 2, 8, 8, 64), F32)
    packed_block = lead_block((2, 4, 8, 8, 128))
    packed_shape = jax.ShapeDtypeStruct((12, 4, 8, 8, 128), F32)
    own_pre, cot_p, windows = pl.pallas_call(
        own_forward_kernel,
        grid=(6,),
        in_specs=[lead_block((2, 512, 128)), mask_block, turned_block, const_block((4608, 256)), const_block((1, 128))],
        out_specs=[
            packed_block,
            packed_block,
            pl.BlockSpec((3, 1, 2, 5, 10, 16, 128), lambda g: (0, g, 0, 0, 0, 0, 0)),
        ],
        out_shape=[
            hbm_out(packed_shape.shape, F32),
            hbm_out(packed_shape.shape, F32),
            hbm_out((3, 6, 2, 5, 10, 16, 128), BF16),
        ],
        compiler_params=params(24),
        cost_estimate=pl.CostEstimate(flops=2 * 3072 * 4608 * 256, bytes_accessed=15000000, transcendentals=0),
        name="own_forward",
    )(in_hbm(rows), mask, in_hbm(cot), in_hbm(wf), bias2)

    flat = (3072, 128)
    side_x, side_y, side_z = (2, 3, 10, 6, 16, 128), (2, 3, 2, 5, 6, 16, 128), (2, 2, 5, 10, 16, 128)
    held = pl.BlockSpec(memory_space=pl.ANY)
    act, dpre, send, px, py, pz = pl.pallas_call(
        halo_kernel,
        in_specs=[whole(pltpu.SMEM), whole()] + [held] * 4,
        out_specs=[held] * 6,
        out_shape=[
            hbm_out(flat, F32),
            hbm_out(flat, F32),
            hbm_out((64, 80, 128), F32),
            hbm_out(side_x, BF16),
            hbm_out(side_y, BF16),
            hbm_out(side_z, BF16),
        ],
        scratch_shapes=[
            pltpu.VMEM(flat, F32),
            pltpu.VMEM(flat, F32),
            pltpu.VMEM((4608, 256), BF16),
            pltpu.VMEM((4608, 256), BF16),
            pltpu.VMEM(flat, F32),
            pltpu.VMEM(flat, F32),
            pltpu.VMEM(side_x, BF16),
            pltpu.VMEM(side_y, BF16),
            pltpu.VMEM(side_z, BF16),
            pltpu.VMEM((64, 80, 128), F32),
            pltpu.VMEM((3200, 128), F32),
            pltpu.VMEM((2, 3, 12, 6, 16, 128), BF16),
            pltpu.VMEM((2, 3, 2, 5, 6, 16, 128), BF16),
            pltpu.VMEM((2, 2, 6, 12, 16, 128), BF16),
            pltpu.VMEM((2, 960, 128), F32),
            pltpu.VMEM((2, 384, 128), F32),
            pltpu.VMEM((1600, 128), F32),
            pltpu.VMEM((8, 128), F32),
            pltpu.SemaphoreType.DMA((11,)),
        ],
        compiler_params=params(44),
        name="halo",
    )(code, recv, in_hbm(own_pre.reshape(flat)), in_hbm(cot_p.reshape(flat)), in_hbm(wf), in_hbm(wb))
    back = lax.all_to_all(send, "brick", split_axis=0, concat_axis=0, tiled=True)
    act = act.reshape(packed_shape.shape)
    dpre = dpre.reshape(packed_shape.shape)

    z = pl.pallas_call(
        kernel_grad_kernel,
        grid=(3,),
        in_specs=[
            pl.BlockSpec((1, 6, 2, 5, 10, 16, 128), lambda l: (l, 0, 0, 0, 0, 0, 0)),
            pl.BlockSpec((2, 1, 10, 6, 16, 128), lambda l: (0, l, 0, 0, 0, 0)),
            pl.BlockSpec((2, 1, 2, 5, 6, 16, 128), lambda l: (0, l, 0, 0, 0, 0, 0)),
            const_block(side_z),
            const_block(packed_shape.shape),
        ],
        out_specs=pl.BlockSpec((3, 3, 1, 64, 64), lambda l: (0, 0, l, 0, 0)),
        out_shape=jax.ShapeDtypeStruct((3, 3, 3, 64, 64), F32),
        scratch_shapes=[
            pltpu.VMEM((256, 3072), BF16),
            pltpu.VMEM((2, 256, 768), BF16),
            pltpu.VMEM((2, 256, 384), BF16),
            pltpu.VMEM((2, 256, 512), BF16),
            pltpu.VMEM((3, 4, 128, 64), F32),
        ],
        compiler_params=params(40),
        cost_estimate=pl.CostEstimate(flops=0, bytes_accessed=1000, transcendentals=0),
        name="kernel_grad",
    )(in_hbm(windows), in_hbm(px), in_hbm(py), in_hbm(pz), in_hbm(dpre))
    kernel = z.reshape(1728, 64)
    scale = 1.0 / math.sqrt(float(2 * 768 * 512))
    total = swap_scenes(kernel)
    dpre, total = lax.optimization_barrier((dpre, total))
    kept, sent = sum_stage(total, 16)

    own, activated = pl.pallas_call(
        own_backward_kernel,
        grid=(6,),
        in_specs=[packed_block, packed_block, mask_block, const_block((4608, 256))],
        out_specs=[brick_block, turned_block],
        out_shape=[hbm_out(brick_shape.shape, F32), hbm_out(turned_shape.shape, F32)],
        scratch_shapes=[pltpu.VMEM((3, 1, 2, 5, 10, 16, 128), BF16)],
        compiler_params=params(24),
        cost_estimate=pl.CostEstimate(flops=0, bytes_accessed=1000, transcendentals=0),
        name="own_backward",
    )(in_hbm(dpre), in_hbm(act), mask, in_hbm(wb))

    total = kept + sent[0] + sent[1] + sent[2]
    own, total, activated = lax.optimization_barrier((own, total, activated))
    total = jnp.pad(total.reshape(16, 864), ((0, 0), (0, 32))).reshape(16, 7, 128)
    back, total = lax.optimization_barrier((back, total))
    layers = [[16 * n + m for m in range(16)] for n in range(4)]
    shares = lax.all_to_all(total, "brick", split_axis=0, concat_axis=0, tiled=True, axis_index_groups=layers)

    grad = pl.pallas_call(
        collect_kernel,
        grid=(4,),
        in_specs=[
            pl.BlockSpec(memory_space=pltpu.SMEM),
            const_block((64, 80, 128)),
            lead_block((3, 4, 2, 8, 8, 64)),
            lead_block((3, 1, 512)),
        ],
        out_specs=lead_block((3, 64, 512)),
        out_shape=turned_shape,
        scratch_shapes=[
            pltpu.VMEM((73, 64, 128), F32),
            pltpu.VMEM((145, 8, 128), F32),
            pltpu.VMEM((97, 8, 128), F32),
            pltpu.VMEM((512, 64), F32),
        ],
        compiler_params=params(24),
        name="collect",
    )(asked, back, in_hbm(own), mask)
    share = jnp.sum(shares, axis=0).reshape(896)[:864] * scale
    return activated.transpose(0, 2, 1)[None], grad.transpose(0, 2, 1)[None], share


def solution(mesh):
    big = P("scene", "brick", None, None)
    flat = P("scene", "brick", None)
    return jax.shard_map(
        on_device,
        mesh=mesh,
        in_specs=(big, flat, P(), P(), big, big, flat, flat),
        out_specs=(big, big, P(("scene", "brick"))),
        check_vma=False,
    )
```

```python
import math

import jax
import jax.numpy as jnp
import numpy as np
from jax import lax
from jax.experimental import pallas as pl
from jax.experimental.pallas import tpu as pltpu
from jax.sharding import PartitionSpec as P

OFFSETS = [(a, b, c) for a in (-1, 0, 1) for b in (-1, 0, 1) for c in (-1, 0, 1) if (a, b, c) != (0, 0, 0)]
KIND = [sum(1 for v in o if v != 0) - 1 for o in OFFSETS]
ORDINAL = [KIND[:k].count(KIND[k]) for k in range(26)]
PER_KIND = (6, 12, 8)
FIRST = (0, 2, 5)
F32, BF16 = jnp.float32, jnp.bfloat16


def source_coord(step):
    return 0 if step == 1 else 7


def target_coord(step):
    return 9 if step == 1 else 0


def half_of(shape):
    return lax.broadcasted_iota(jnp.int32, shape, len(shape) - 1) >= 64


def swap(v):
    return pltpu.roll(v, 64, axis=v.ndim - 1)


def split_halves(v, low):
    top = v.astype(BF16).astype(F32)
    return jnp.where(low, top, v - top).astype(BF16)


def masked_rows(x_ref, m_ref, p):
    return (x_ref[p] * m_ref[p].astype(F32)).T


def tables_kernel(x_ref, m_ref, face_ref, edge_ref, corner_ref, row_ref, rows):
    for p in range(x_ref.shape[0]):
        x = masked_rows(x_ref, m_ref, p)
        x = jnp.concatenate([x, x], axis=1)
        rows[...] = x
        row_ref[p] = x
        for k, (a, b, c) in enumerate(OFFSETS):
            n = ORDINAL[k]
            x0, y0, z0 = source_coord(a), source_coord(b), source_coord(c)
            if KIND[k] == 0:
                for i in range(8):
                    if a:
                        v = rows[x0 * 64 + i * 8:x0 * 64 + i * 8 + 8, :]
                    elif b:
                        v = rows[i * 64 + y0 * 8:i * 64 + y0 * 8 + 8, :]
                    else:
                        v = rows[pl.ds(i * 64 + z0, 8, stride=8), :]
                    face_ref[p * 6 + n, i * 8:i * 8 + 8, :] = v
            elif KIND[k] == 1:
                if not c:
                    v = rows[x0 * 64 + y0 * 8:x0 * 64 + y0 * 8 + 8, :]
                elif not b:
                    v = rows[pl.ds(x0 * 64 + z0, 8, stride=8), :]
                else:
                    v = rows[pl.ds(y0 * 8 + z0, 8, stride=64), :]
                edge_ref[p * 12 + n] = v
            else:
                r = x0 * 64 + y0 * 8 + z0
                corner_ref[p * 8 + n] = jnp.broadcast_to(rows[r:r + 1, :], (8, 128))


def pack_kernel(want_ref, face_ref, edge_ref, corner_ref, out_ref):
    high = half_of((64, 128))
    high8 = half_of((8, 128))
    row0 = lax.broadcasted_iota(jnp.int32, (8, 128), 0) == 0

    def body(p, carry):
        q = [jnp.maximum(want_ref[p, j], 0) for j in range(7)]
        out_ref[p, 0:64, :] = jnp.where(high, face_ref[q[1]], face_ref[q[0]])
        out_ref[p, 64:72, :] = jnp.where(high8, edge_ref[q[3]], edge_ref[q[2]])
        corners = jnp.where(row0, corner_ref[q[5]], corner_ref[q[6]])
        out_ref[p, 72:80, :] = jnp.where(high8, corners, edge_ref[q[4]])
        return carry

    lax.fori_loop(0, 64, body, 0)


def placed(v, other):
    return jnp.where(other, v, swap(v))


def shifted(v, l, row):
    if l == 1:
        return v
    turned = pltpu.roll(v, 1 if l == 0 else 7, axis=0)
    return jnp.where(row == (0 if l == 0 else 7), 0.0, turned)


def weights_kernel(w_ref, f_ref, b_ref):
    zero = jnp.zeros((64, 64), F32)

    def fill(out_ref, s, sides):
        c = jnp.concatenate(sides, axis=1)
        top = c.astype(BF16)
        low = (c - top.astype(F32)).astype(BF16)
        v = jnp.concatenate([top, low], axis=1)
        out_ref[s * 128:s * 128 + 128, :] = jnp.concatenate([v, v], axis=0)

    for j in range(3):
        for l in range(3):
            w = [w_ref[i * 9 + j * 3 + l] for i in range(3)]
            t = [w_ref[(2 - i) * 9 + (2 - j) * 3 + 2 - l].T for i in range(3)]
            for i in range(4):
                s = i * 9 + j * 3 + l
                fill(f_ref, s, [w[i] if i < 3 else zero, w[i - 1] if i else zero])
                fill(b_ref, s, [t[i] if i < 3 else zero, t[i - 1] if i else zero])


def convolve(a_ref, w_ref):
    slices = [(i, j, l) for i in range(4) for j in range(3) for l in range(3)]
    acc = None
    for s in range(0, 36, 4):
        parts = [a_ref[l, 0, i % 2, i // 2:i // 2 + 4, j:j + 8].reshape(512, 128) for i, j, l in slices[s:s + 4]]
        lhs = jnp.concatenate(parts, axis=1)
        d = jnp.dot(lhs, w_ref[s * 128:s * 128 + 512, :], preferred_element_type=F32)
        acc = d if acc is None else acc + d
    return (acc[:, :128] + acc[:, 128:]).reshape(4, 8, 16, 128)


def clear_border(a_ref):
    spare = jnp.zeros((16, 128), BF16)
    for l in range(3):
        for x in range(10):
            for y in range(10):
                if x in (0, 9) or y in (0, 9):
                    a_ref[l, 0, x % 2, x // 2, y] = spare


def own_forward_kernel(x_ref, m_ref, cot_ref, w_ref, bias_ref, pre_ref, cotm_ref, a_ref):
    clear_border(a_ref)
    row = lax.broadcasted_iota(jnp.int32, (8, 128), 0)
    low = jnp.logical_not(half_of((16, 128)))
    for x in range(8):
        for y in range(8):
            r = x * 64 + y * 8
            for l in range(3):
                v = jnp.concatenate([shifted(x_ref[b, r:r + 8, :], l, row) for b in range(2)], axis=0)
                a_ref[l, 0, (x + 1) % 2, (x + 1) // 2, y + 1] = split_halves(v, low)
    pre = convolve(a_ref, w_ref) + bias_ref[...]
    for b in range(2):
        pre_ref[b] = pre[:, :, b * 8:b * 8 + 8]
        c = masked_rows(cot_ref, m_ref, b).reshape(4, 2, 8, 8, 64)
        cotm_ref[b] = jnp.concatenate([c[:, 0], c[:, 1]], axis=-1)


def own_backward_kernel(d_ref, act_ref, m_ref, w_ref, own_ref, out_ref, a_ref):
    @pl.when(pl.program_id(0) == 0)
    def _():
        a_ref[...] = jnp.zeros_like(a_ref)

    row = lax.broadcasted_iota(jnp.int32, (8, 128), 0)
    half = half_of((8, 128))
    low = jnp.logical_not(half_of((16, 128)))
    for x in range(8):
        for y in range(8):
            cols = []
            for b in range(2):
                cols.append(placed(d_ref[b, x // 2, y], half if x % 2 else jnp.logical_not(half)))
            for l in range(3):
                v = jnp.concatenate([shifted(cols[b], l, row) for b in range(2)], axis=0)
                a_ref[l, 0, (x + 1) % 2, (x + 1) // 2, y + 1] = split_halves(v, low)
    out = convolve(a_ref, w_ref)
    for b in range(2):
        own_ref[b, :, 0] = out[:, :, b * 8:b * 8 + 8, :64]
        own_ref[b, :, 1] = out[:, :, b * 8:b * 8 + 8, 64:]
        mask = m_ref[b].astype(F32)
        for h in range(2):
            t = act_ref[b, 2 * h:2 * h + 2].reshape(128, 128).T
            v = jnp.concatenate([t[:64, :64], t[64:, :64], t[:64, 64:], t[64:, 64:]], axis=1)
            a = slice(h * 256, h * 256 + 256)
            out_ref[b, :, a] = v * mask[:, a]


def unpack_code(code_ref, b, k):
    c = code_ref[b * 26 + k]
    return c >> 4, (c >> 1) & 7, c & 1


def edge_rows(pos):
    e = pos - 2
    return pl.ds(pl.multiple_of(64 + 8 * (e >> 1), 8), 8), e & 1


def halo_kernel(code_ref, recv_ref, own_hbm, cot_hbm, wf_hbm, wb_hbm,
                act_hbm, dpre_hbm, send_hbm, px_hbm, py_hbm, pz_hbm,
                pre, cot_ref, wf_ref, wb_ref, act_ref, dpre_ref, px, py, pz,
                send_ref, zf, qx, qy, qz, rx, ry, rz, tmp, sems):
    arriving = [pltpu.make_async_copy(a, b, sems.at[n]) for n, (a, b) in enumerate(
        [(own_hbm, pre), (wf_hbm, wf_ref), (cot_hbm, cot_ref), (wb_hbm, wb_ref)])]
    leaving = [pltpu.make_async_copy(a, b, sems.at[4 + n]) for n, (a, b) in enumerate(
        [(px, px_hbm), (py, py_hbm), (pz, pz_hbm), (act_ref, act_hbm), (dpre_ref, dpre_hbm)])]
    faces_out = pltpu.make_async_copy(send_ref.at[:, 0:64], send_hbm.at[:, 0:64], sems.at[9])
    rest_out = pltpu.make_async_copy(send_ref.at[:, 64:80], send_hbm.at[:, 64:80], sems.at[10])
    for c in arriving:
        c.start()
    high8 = half_of((8, 128))
    half8 = high8.astype(jnp.int32)
    row = lax.broadcasted_iota(jnp.int32, (8, 128), 0)
    low = jnp.logical_not(half_of((16, 128)))
    spare = jnp.zeros((16, 128), BF16)

    def zrow(s, x, y, b):
        return ((s * 10 + x) * 10 + y) * 16 + b

    for s in range(2):
        for l in range(3):
            for g in range(6):
                py[s, l, 0, 0, g] = spare
                py[s, l, 1, 4, g] = spare
        for x in range(10):
            for y in range(10):
                r = zrow(s, x, y, 8)
                zf[r:r + 8, :] = jnp.zeros((8, 128), F32)

    def face(k, b, i):
        o, pos, alive = unpack_code(code_ref, b, k)
        v = recv_ref[o, i * 8:i * 8 + 8, :]
        return placed(v, half8 == pos) * alive.astype(F32)

    def edge(k, b):
        o, pos, alive = unpack_code(code_ref, b, k)
        rows, h = edge_rows(pos)
        return placed(recv_ref[o, rows, :], half8 == h) * alive.astype(F32)

    for k, (dx, dy, dz) in enumerate(OFFSETS):
        xt, yt = target_coord(dx), target_coord(dy)
        sx, sy, sz = int(dx == 1), int(dy == 1), int(dz == 1)
        for g in range(6):
            pair = (2 * g, 2 * g + 1)
            if KIND[k] == 0 and not dz:
                for i in range(8):
                    v = [face(k, b, i) for b in pair]
                    for l in range(3):
                        w = split_halves(jnp.concatenate([shifted(u, l, row) for u in v], axis=0), low)
                        if dx:
                            px[sx, l, i + 1, g] = w
                        else:
                            py[sy, l, (i + 1) % 2, (i + 1) // 2, g] = w
            elif KIND[k] == 1 and not dz:
                v = [edge(k, b) for b in pair]
                for l in range(3):
                    px[sx, l, yt, g] = split_halves(jnp.concatenate([shifted(u, l, row) for u in v], axis=0), low)
            else:
                for b in pair:
                    if KIND[k] == 0:
                        for i in range(8):
                            zf[pl.ds(zrow(sz, i + 1, 1, b), 8, stride=16), :] = face(k, b, i)
                    elif KIND[k] == 1 and dx:
                        zf[pl.ds(zrow(sz, xt, 1, b), 8, stride=16), :] = edge(k, b)
                    elif KIND[k] == 1:
                        zf[pl.ds(zrow(sz, 1, yt, b), 8, stride=160), :] = edge(k, b)
                    else:
                        o, pos, alive = unpack_code(code_ref, b, k)
                        v = recv_ref[o, 72:80, :]
                        v = jnp.where(pos == 5, v[0:1, :], v[1:2, :])
                        r = zrow(sz, xt, yt, b)
                        zf[r:r + 1, :] = placed(v, high8[0:1]) * alive.astype(F32)
    for s in range(2):
        for x in range(10):
            for y in range(10):
                r = zrow(s, x, y, 0)
                pz[s, x % 2, x // 2, y] = split_halves(zf[r:r + 16, :], low)

    def side_x(src, s, ii, ys, w_ref):
        parts = [src[s, l, j:j + ys].reshape(ys * 96, 128) for j in range(3) for l in range(3)]
        v = jnp.dot(jnp.concatenate(parts, axis=1), w_ref[ii * 1152:ii * 1152 + 1152, :], preferred_element_type=F32)
        return v[:, :128] + v[:, 128:]

    def side_y(src, s, j, w_ref):
        acc = None
        for h in range(2):
            parts = [src[s, l, i, h:h + 4].reshape(384, 128) for i in range(2) for l in range(3)]
            at = [((2 * h + i) * 9 + j * 3) * 128 for i in range(2)]
            w = jnp.concatenate([w_ref[a:a + 384, :] for a in at], axis=0)
            v = jnp.dot(jnp.concatenate(parts, axis=1), w, preferred_element_type=F32)
            acc = v if acc is None else acc + v
        return acc[:, :128] + acc[:, 128:]

    def side_z(src, s, l, xs, ys, w_ref):
        slices = [(i, j) for i in range(4) for j in range(3)]
        acc = None
        for n in range(0, 12, 4):
            parts = [src[s, i % 2, i // 2:i // 2 + xs, j:j + ys].reshape(xs * ys * 16, 128) for i, j in slices[n:n + 4]]
            at = [(i * 9 + j * 3 + l) * 128 for i, j in slices[n:n + 4]]
            w = jnp.concatenate([w_ref[a:a + 128, :] for a in at], axis=0)
            v = jnp.dot(jnp.concatenate(parts, axis=1), w, preferred_element_type=F32)
            acc = v if acc is None else acc + v
        return acc[:, :128] + acc[:, 128:]

    def prow(b, xh, y, z):
        return ((b * 4 + xh) * 8 + y) * 8 + z

    for c in leaving[:3]:
        c.start()
    arriving[0].wait()
    arriving[1].wait()
    for s in range(2):
        v = side_x(px, s, 3 * s, 8, wf_ref)
        for y in range(8):
            for b in range(12):
                r, q = prow(b, 3 * s, y, 0), (y * 12 + b) * 8
                pre[r:r + 8, :] += v[q:q + 8]
        v = side_y(py, s, 2 * s, wf_ref)
        for xh in range(4):
            for b in range(12):
                r, q = prow(b, xh, 7 * s, 0), (xh * 12 + b) * 8
                pre[r:r + 8, :] += v[q:q + 8]
        v = side_z(pz, s, 2 * s, 4, 8, wf_ref)
        for xh in range(4):
            for y in range(8):
                q = (xh * 8 + y) * 16
                a = pl.ds(prow(0, xh, y, 7 * s), 8, stride=256)
                pre[a, :] = pre[a, :] + v[q:q + 8]
                a = pl.ds(prow(8, xh, y, 7 * s), 4, stride=256)
                pre[a, :] = pre[a, :] + v[q + 8:q + 12]

    def activate(n, carry):
        a = pl.ds(pl.multiple_of(n * 128, 128), 128)
        p = pre[a, :]
        sig = jax.nn.sigmoid(p)
        ps = p * sig
        act_ref[a, :] = ps
        dpre_ref[a, :] = cot_ref[a, :] * (sig + ps * (1.0 - sig))
        return carry

    arriving[2].wait()
    lax.fori_loop(0, 24, activate, 0)
    leaving[3].start()
    leaving[4].start()

    for s in range(2):
        for l in range(3):
            for g in range(6):
                for y in (0, 1, 10, 11):
                    qx[s, l, y, g] = spare
                qy[s, l, 0, 0, g] = spare
                qy[s, l, 1, 4, g] = spare
    qz[...] = jnp.zeros_like(qz)
    wanted = [jnp.logical_not(high8), high8]
    wanted16 = [low, jnp.logical_not(low)]
    for s in range(2):
        for g in range(6):
            for y in range(8):
                v = []
                for b in (2 * g, 2 * g + 1):
                    r = prow(b, 3 * s, y, 0)
                    v.append(placed(dpre_ref[r:r + 8, :], wanted[s]))
                for l in range(3):
                    qx[s, l, y + 2, g] = split_halves(jnp.concatenate([shifted(u, l, row) for u in v], axis=0), low)
            for x in range(8):
                v = []
                for b in (2 * g, 2 * g + 1):
                    r = prow(b, x // 2, 7 * s, 0)
                    v.append(placed(dpre_ref[r:r + 8, :], wanted[x % 2]))
                for l in range(3):
                    w = split_halves(jnp.concatenate([shifted(u, l, row) for u in v], axis=0), low)
                    qy[s, l, (x + 1) % 2, (x + 1) // 2, g] = w
        for xh in range(4):
            for y in range(8):
                first = dpre_ref[pl.ds(prow(0, xh, y, 7 * s), 8, stride=256), :]
                last = dpre_ref[pl.ds(prow(8, xh, y, 7 * s), 4, stride=256), :]
                v = jnp.concatenate([first, last, jnp.zeros((4, 128), F32)], axis=0)
                for p in range(2):
                    qz[s, p, xh + 1, y + 2] = split_halves(placed(v, wanted16[p]), low)
    arriving[3].wait()
    for s in range(2):
        rx[s] = side_x(qx, s, 3 - 3 * s, 10, wb_ref)
        ry[s] = side_y(qy, s, 2 - 2 * s, wb_ref)
        rz[s * 800:s * 800 + 800, :] = side_z(qz, s, 2 - 2 * s, 5, 10, wb_ref)

    def rzrow(s, xh, y, b):
        return s * 800 + (xh * 10 + y) * 16 + b

    send_ref[...] = jnp.zeros_like(send_ref)
    kinds = [k for k in range(26) if KIND[k] == 0] + [k for k in range(26) if KIND[k]]
    for n, k in enumerate(kinds):
        if n == 6:
            faces_out.start()
        dx, dy, dz = OFFSETS[k]
        for b in range(12):
            o, pos, _ = unpack_code(code_ref, b, k)
            xt, yt = target_coord(dx), target_coord(dy)
            sx, sy, sz = int(dx == 1), int(dy == 1), int(dz == 1)
            if KIND[k] == 0:
                for i in range(8):
                    if dx:
                        r, par = ((i + 1) * 12 + b) * 8, 1 - sx
                        v = rx[sx, r:r + 8, :]
                    elif dy:
                        r, par = ((i // 2) * 12 + b) * 8, i % 2
                        v = ry[sy, r:r + 8, :]
                    else:
                        par = (i + 1) % 2
                        v = rz[pl.ds(rzrow(sz, (i + 1) // 2, 1, b), 8, stride=16), :]
                    v = placed(v, wanted[par])
                    a = slice(i * 8, i * 8 + 8)
                    send_ref[o, a, :] = jnp.where(half8 == pos, v, send_ref[o, a, :])
            elif KIND[k] == 1:
                if not dz:
                    r = (yt * 12 + b) * 8
                    v = placed(rx[sx, r:r + 8, :], wanted[1 - sx])
                elif dx:
                    v = placed(rz[pl.ds(rzrow(sz, xt // 2, 1, b), 8, stride=16), :], wanted[xt % 2])
                else:
                    for q in range(2):
                        tmp[pl.ds(q, 4, stride=2), :] = rz[pl.ds(rzrow(sz, q, yt, b), 4, stride=160), :]
                    v = placed(tmp[...], half8 == 1 - (row & 1))
                a, h = edge_rows(pos)
                send_ref[o, a, :] = jnp.where(half8 == h, v, send_ref[o, a, :])
            else:
                r = rzrow(sz, xt // 2, yt, b)
                v = placed(jnp.broadcast_to(rz[r:r + 1, :], (8, 128)), wanted[xt % 2])
                spot = jnp.logical_and(row == pos - 5, high8)
                send_ref[o, 72:80, :] = jnp.where(spot, v, send_ref[o, 72:80, :])
    rest_out.start()
    for c in leaving + [faces_out, rest_out]:
        c.wait()


def turned_terms(out_ref, at, v):
    t = v.T
    n = t.shape[1]
    top = t.astype(BF16)
    out_ref[0:128, at:at + n] = top
    out_ref[128:256, at:at + n] = (t - top.astype(F32)).astype(BF16)


def kernel_grad_kernel(a_ref, px_ref, py_ref, pz_ref, d_ref, out_ref, dt, dx, dy, dz, sums):
    l = pl.program_id(0)

    @pl.when(l == 0)
    def _():
        for g in range(6):
            v = jnp.concatenate([d_ref[2 * g], d_ref[2 * g + 1]], axis=2)
            turned_terms(dt, g * 512, v.reshape(512, 128))
        flat = d_ref.reshape(3072, 128)
        for s in range(2):
            for y in range(8):
                v = jnp.concatenate([d_ref[b, 3 * s, y] for b in range(12)], axis=0)
                if y % 4 == 0:
                    held = []
                held.append(v)
                if y % 4 == 3:
                    turned_terms(dx.at[s], (y - 3) * 96, jnp.concatenate(held, axis=0))
            v = [d_ref[b, xh, 7 * s] for xh in range(4) for b in range(12)]
            turned_terms(dy.at[s], 0, jnp.concatenate(v, axis=0))
            v = []
            for n in range(32):
                r = n * 8 + 7 * s
                v.append(flat[pl.ds(r, 8, stride=256), :])
                v.append(flat[pl.ds(r + 2048, 4, stride=256), :])
                v.append(jnp.zeros((4, 128), F32))
            turned_terms(dz.at[s], 0, jnp.concatenate(v, axis=0))

    def product(d, parts):
        s = jnp.dot(d, jnp.concatenate(parts, axis=1), preferred_element_type=F32)
        s = s[:128] + s[128:]
        out = []
        for q in range(len(parts)):
            v = s[:, q * 128:q * 128 + 128]
            out.append((v + swap(v))[:, :64])
        return out

    for j in range(3):
        for h in range(2):
            parts = [a_ref[0, :, q, h:h + 4, j:j + 8].reshape(3072, 128) for q in range(2)]
            for q, v in enumerate(product(dt[...], parts)):
                sums[j, 2 * h + q] = v
    for s in range(2):
        parts = [px_ref[s, 0, j:j + 8].reshape(768, 128) for j in range(3)]
        for j, v in enumerate(product(dx[s], parts)):
            sums[j, 3 * s] += v
        parts = [py_ref[s, 0, i % 2, i // 2:i // 2 + 4].reshape(384, 128) for i in range(4)]
        for i, v in enumerate(product(dy[s], parts)):
            sums[2 * s, i] += v

    @pl.when(l != 1)
    def _():
        s = l // 2
        for j in range(3):
            parts = [pz_ref[s, i % 2, i // 2:i // 2 + 4, j:j + 8].reshape(512, 128) for i in range(4)]
            for i, v in enumerate(product(dz[s], parts)):
                sums[j, i] += v

    for i in range(3):
        for j in range(3):
            out_ref[i, j, 0] = (sums[j, i, 0:64] + sums[j, i + 1, 64:128]).T


def collect_kernel(want_ref, back_ref, own_ref, m_ref, out_ref, faces, edges, corners, rows):
    g = pl.program_id(0)
    high = half_of((64, 128))
    high8 = half_of((8, 128))
    rowi = lax.broadcasted_iota(jnp.int32, (8, 128), 0)

    @pl.when(g == 0)
    def _():
        faces[...] = jnp.zeros_like(faces)
        edges[...] = jnp.zeros_like(edges)
        corners[...] = jnp.zeros_like(corners)

        def index(p, j, spare):
            q = want_ref[p, j]
            return jnp.where(q < 0, spare, q)

        def body(p, carry):
            v = back_ref[p, 0:64, :]
            faces[index(p, 0, 72)] += jnp.where(high, 0.0, v)
            faces[index(p, 1, 72)] += jnp.where(high, v, 0.0)
            v = back_ref[p, 64:72, :]
            edges[index(p, 2, 144)] += jnp.where(high8, 0.0, v)
            edges[index(p, 3, 144)] += jnp.where(high8, v, 0.0)
            v = back_ref[p, 72:80, :]
            edges[index(p, 4, 144)] += jnp.where(high8, 0.0, v)
            v = jnp.where(high8, v, 0.0)
            corners[index(p, 5, 96)] += jnp.where(rowi == 0, v, 0.0)
            corners[index(p, 6, 96)] += jnp.where(rowi == 1, v, 0.0)
            return carry

        lax.fori_loop(0, 64, body, 0)

    def fold(v):
        return (v + swap(v))[:, :64]

    bricks = own_ref.shape[0]
    for p in range(bricks):
        rows[...] = own_ref[p].reshape(512, 64)
        for k, (a, b, c) in enumerate(OFFSETS):
            n = (g * bricks + p) * PER_KIND[KIND[k]] + ORDINAL[k]
            x0, y0, z0 = source_coord(a), source_coord(b), source_coord(c)
            if KIND[k] == 0:
                for i in range(8):
                    v = fold(faces[n, i * 8:i * 8 + 8, :])
                    if a:
                        s = slice(x0 * 64 + i * 8, x0 * 64 + i * 8 + 8)
                    elif b:
                        s = slice(i * 64 + y0 * 8, i * 64 + y0 * 8 + 8)
                    else:
                        s = pl.ds(i * 64 + z0, 8, stride=8)
                    rows[s, :] = rows[s, :] + v
            elif KIND[k] == 1:
                v = fold(edges[n])
                if not c:
                    s = slice(x0 * 64 + y0 * 8, x0 * 64 + y0 * 8 + 8)
                elif not b:
                    s = pl.ds(x0 * 64 + z0, 8, stride=8)
                else:
                    s = pl.ds(y0 * 8 + z0, 8, stride=64)
                rows[s, :] = rows[s, :] + v
            else:
                r = x0 * 64 + y0 * 8 + z0
                v = fold(corners[n])
                rows[r:r + 1, :] = rows[r:r + 1, :] + (v[0:1] + v[1:2])
        out_ref[p] = rows[...].T * m_ref[p].astype(F32)


def swap_scenes(v):
    scene = lax.axis_index("scene")
    mine = lax.dynamic_slice_in_dim(v, scene * 864, 864, 0)
    theirs = lax.dynamic_slice_in_dim(v, (1 - scene) * 864, 864, 0)
    return mine + lax.ppermute(theirs, "scene", [(0, 1), (1, 0)])


def sum_stage(v, stride):
    at = (lax.axis_index("brick") // stride) % 4
    n = v.shape[0] // 4

    def quarter(k):
        return lax.dynamic_slice_in_dim(v, k * n, n, 0)

    sent = [lax.ppermute(quarter(at ^ d), "brick", [(m, m ^ (d * stride)) for m in range(64)]) for d in (1, 2, 3)]
    return quarter(at), sent


def whole(memory=pltpu.VMEM):
    return pl.BlockSpec(memory_space=memory)


def const_block(shape):
    return pl.BlockSpec(shape, lambda g: (0,) * len(shape))


def lead_block(shape):
    return pl.BlockSpec(shape, lambda g: (g,) + (0,) * (len(shape) - 1))


def in_hbm(x):
    return pltpu.with_memory_space_constraint(x, pltpu.HBM)


def hbm_out(shape, kind):
    return pltpu.HBM(shape, kind)


def params(mib):
    return pltpu.CompilerParams(vmem_limit_bytes=mib * 1024 * 1024)


def on_device(features, voxel_mask, weight, bias, cotangent, owner, slot, live):
    x = features[0].transpose(0, 2, 1)
    cot = cotangent[0].transpose(0, 2, 1)
    mask = voxel_mask.reshape(12, 1, 512)

    peer = owner.reshape(312)
    alive = live.reshape(312)
    kinds = jnp.asarray(np.tile(np.array(KIND, np.int32), 12))
    first = jnp.asarray(np.tile(np.array([FIRST[q] for q in KIND], np.int32), 12))
    per = jnp.asarray(np.tile(np.array([PER_KIND[q] for q in KIND], np.int32), 12))
    ordinal = jnp.asarray(np.tile(np.array(ORDINAL, np.int32), 12))
    entry = slot.reshape(312) * per + ordinal
    key = peer * 3 + kinds
    order = jnp.arange(312, dtype=jnp.int32)
    same = jnp.logical_and(key[:, None] == key[None, :], order[:, None] < order[None, :])
    place = first + jnp.sum(same.astype(jnp.int32), axis=0)
    spot = jnp.where(alive > 0, peer * 8 + place, -1)
    hit = spot[None, :] == jnp.arange(512, dtype=jnp.int32)[:, None]
    wanted = jnp.sum(jnp.where(hit, entry[None, :] + 1, 0), axis=1).reshape(64, 8) - 1
    code = (peer * 8 + place) * 2 + alive
    asked = lax.all_to_all(wanted, "brick", split_axis=0, concat_axis=0, tiled=True)

    wf, wb = pl.pallas_call(
        weights_kernel,
        in_specs=[whole()],
        out_specs=[whole(), whole()],
        out_shape=[hbm_out((4608, 256), BF16)] * 2,
        compiler_params=params(16),
        cost_estimate=pl.CostEstimate(flops=0, bytes_accessed=6000000, transcendentals=0),
        name="weights",
    )(weight)

    faces, edges, corners, rows = pl.pallas_call(
        tables_kernel,
        grid=(3,),
        in_specs=[lead_block((4, 64, 512)), lead_block((4, 1, 512))],
        out_specs=[
            lead_block((24, 64, 128)),
            lead_block((48, 8, 128)),
            lead_block((32, 8, 128)),
            lead_block((4, 512, 128)),
        ],
        out_shape=[
            jax.ShapeDtypeStruct((72, 64, 128), F32),
            jax.ShapeDtypeStruct((144, 8, 128), F32),
            jax.ShapeDtypeStruct((96, 8, 128), F32),
            hbm_out((12, 512, 128), F32),
        ],
        scratch_shapes=[pltpu.VMEM((512, 128), F32)],
        compiler_params=params(16),
        name="tables",
    )(x, mask)

    out = pl.pallas_call(
        pack_kernel,
        in_specs=[whole(pltpu.SMEM), whole(), whole(), whole()],
        out_specs=whole(),
        out_shape=jax.ShapeDtypeStruct((64, 80, 128), F32),
        compiler_params=params(16),
        name="pack",
    )(asked, faces, edges, corners)
    recv = lax.all_to_all(out, "brick", split_axis=0, concat_axis=0, tiled=True)

    bias2 = jnp.concatenate([bias, bias]).reshape(1, 128)
    turned_block = lead_block((2, 64, 512))
    turned_shape = jax.ShapeDtypeStruct((12, 64, 512), F32)
    mask_block = lead_block((2, 1, 512))
    brick_block = lead_block((2, 4, 2, 8, 8, 64))
    brick_shape = jax.ShapeDtypeStruct((12, 4, 2, 8, 8, 64), F32)
    packed_block = lead_block((2, 4, 8, 8, 128))
    packed_shape = jax.ShapeDtypeStruct((12, 4, 8, 8, 128), F32)
    own_pre, cot_p, windows = pl.pallas_call(
        own_forward_kernel,
        grid=(6,),
        in_specs=[lead_block((2, 512, 128)), mask_block, turned_block, const_block((4608, 256)), const_block((1, 128))],
        out_specs=[
            packed_block,
            packed_block,
            pl.BlockSpec((3, 1, 2, 5, 10, 16, 128), lambda g: (0, g, 0, 0, 0, 0, 0)),
        ],
        out_shape=[
            hbm_out(packed_shape.shape, F32),
            hbm_out(packed_shape.shape, F32),
            hbm_out((3, 6, 2, 5, 10, 16, 128), BF16),
        ],
        compiler_params=params(24),
        cost_estimate=pl.CostEstimate(flops=2 * 3072 * 4608 * 256, bytes_accessed=15000000, transcendentals=0),
        name="own_forward",
    )(in_hbm(rows), in_hbm(mask), in_hbm(cot), in_hbm(wf), bias2)

    flat = (3072, 128)
    side_x, side_y, side_z = (2, 3, 10, 6, 16, 128), (2, 3, 2, 5, 6, 16, 128), (2, 2, 5, 10, 16, 128)
    held = pl.BlockSpec(memory_space=pl.ANY)
    act, dpre, send, px, py, pz = pl.pallas_call(
        halo_kernel,
        in_specs=[whole(pltpu.SMEM), whole()] + [held] * 4,
        out_specs=[held] * 6,
        out_shape=[
            hbm_out(flat, F32),
            hbm_out(flat, F32),
            hbm_out((64, 80, 128), F32),
            hbm_out(side_x, BF16),
            hbm_out(side_y, BF16),
            hbm_out(side_z, BF16),
        ],
        scratch_shapes=[
            pltpu.VMEM(flat, F32),
            pltpu.VMEM(flat, F32),
            pltpu.VMEM((4608, 256), BF16),
            pltpu.VMEM((4608, 256), BF16),
            pltpu.VMEM(flat, F32),
            pltpu.VMEM(flat, F32),
            pltpu.VMEM(side_x, BF16),
            pltpu.VMEM(side_y, BF16),
            pltpu.VMEM(side_z, BF16),
            pltpu.VMEM((64, 80, 128), F32),
            pltpu.VMEM((3200, 128), F32),
            pltpu.VMEM((2, 3, 12, 6, 16, 128), BF16),
            pltpu.VMEM((2, 3, 2, 5, 6, 16, 128), BF16),
            pltpu.VMEM((2, 2, 6, 12, 16, 128), BF16),
            pltpu.VMEM((2, 960, 128), F32),
            pltpu.VMEM((2, 384, 128), F32),
            pltpu.VMEM((1600, 128), F32),
            pltpu.VMEM((8, 128), F32),
            pltpu.SemaphoreType.DMA((11,)),
        ],
        compiler_params=params(44),
        name="halo",
    )(code, recv, in_hbm(own_pre.reshape(flat)), in_hbm(cot_p.reshape(flat)), in_hbm(wf), in_hbm(wb))
    back = lax.all_to_all(send, "brick", split_axis=0, concat_axis=0, tiled=True)
    act = act.reshape(packed_shape.shape)
    dpre = dpre.reshape(packed_shape.shape)

    z = pl.pallas_call(
        kernel_grad_kernel,
        grid=(3,),
        in_specs=[
            pl.BlockSpec((1, 6, 2, 5, 10, 16, 128), lambda l: (l, 0, 0, 0, 0, 0, 0)),
            pl.BlockSpec((2, 1, 10, 6, 16, 128), lambda l: (0, l, 0, 0, 0, 0)),
            pl.BlockSpec((2, 1, 2, 5, 6, 16, 128), lambda l: (0, l, 0, 0, 0, 0, 0)),
            const_block(side_z),
            const_block(packed_shape.shape),
        ],
        out_specs=pl.BlockSpec((3, 3, 1, 64, 64), lambda l: (0, 0, l, 0, 0)),
        out_shape=jax.ShapeDtypeStruct((3, 3, 3, 64, 64), F32),
        scratch_shapes=[
            pltpu.VMEM((256, 3072), BF16),
            pltpu.VMEM((2, 256, 768), BF16),
            pltpu.VMEM((2, 256, 384), BF16),
            pltpu.VMEM((2, 256, 512), BF16),
            pltpu.VMEM((3, 4, 128, 64), F32),
        ],
        compiler_params=params(40),
        cost_estimate=pl.CostEstimate(flops=0, bytes_accessed=1000, transcendentals=0),
        name="kernel_grad",
    )(in_hbm(windows), in_hbm(px), in_hbm(py), in_hbm(pz), in_hbm(dpre))
    kernel = z.reshape(1728, 64)
    scale = 1.0 / math.sqrt(float(2 * 768 * 512))
    total = swap_scenes(kernel)
    dpre, total = lax.optimization_barrier((dpre, total))
    kept, sent = sum_stage(total, 16)

    own, activated = pl.pallas_call(
        own_backward_kernel,
        grid=(6,),
        in_specs=[packed_block, packed_block, mask_block, const_block((4608, 256))],
        out_specs=[brick_block, turned_block],
        out_shape=[hbm_out(brick_shape.shape, F32), hbm_out(turned_shape.shape, F32)],
        scratch_shapes=[pltpu.VMEM((3, 1, 2, 5, 10, 16, 128), BF16)],
        compiler_params=params(24),
        cost_estimate=pl.CostEstimate(flops=0, bytes_accessed=1000, transcendentals=0),
        name="own_backward",
    )(in_hbm(dpre), in_hbm(act), in_hbm(mask), in_hbm(wb))

    total = kept + sent[0] + sent[1] + sent[2]
    own, total, activated = lax.optimization_barrier((own, total, activated))
    total = jnp.pad(total.reshape(16, 864), ((0, 0), (0, 32))).reshape(16, 7, 128)
    back, total = lax.optimization_barrier((back, total))
    layers = [[16 * n + m for m in range(16)] for n in range(4)]
    shares = lax.all_to_all(total, "brick", split_axis=0, concat_axis=0, tiled=True, axis_index_groups=layers)

    grad = pl.pallas_call(
        collect_kernel,
        grid=(4,),
        in_specs=[
            pl.BlockSpec(memory_space=pltpu.SMEM),
            const_block((64, 80, 128)),
            lead_block((3, 4, 2, 8, 8, 64)),
            lead_block((3, 1, 512)),
        ],
        out_specs=lead_block((3, 64, 512)),
        out_shape=turned_shape,
        scratch_shapes=[
            pltpu.VMEM((73, 64, 128), F32),
            pltpu.VMEM((145, 8, 128), F32),
            pltpu.VMEM((97, 8, 128), F32),
            pltpu.VMEM((512, 64), F32),
        ],
        compiler_params=params(24),
        name="collect",
    )(asked, back, in_hbm(own), in_hbm(mask))
    share = jnp.sum(shares, axis=0).reshape(896)[:864] * scale
    return activated.transpose(0, 2, 1)[None], grad.transpose(0, 2, 1)[None], share


def solution(mesh):
    big = P("scene", "brick", None, None)
    flat = P("scene", "brick", None)
    return jax.shard_map(
        on_device,
        mesh=mesh,
        in_specs=(big, flat, P(), P(), big, big, flat, flat),
        out_specs=(big, big, P(("scene", "brick"))),
        check_vma=False,
    )
```
